32 devices in a mesh: items: 16 (over z, x, core), blk: 2 (over y).
Axes of the slice: x: 2, y: 2, z: 4, core: 2. Of those that a mesh axis runs over, the one named last changes fastest.
Arguments:
- byte_ids: int32 [32, 2048], P('items', 'blk'), may hold values from 0 to 261
- span_start: int32 [32, 8], P('items'), may hold values from 0 to 1920, as said below
- span_len: int32 [32, 8], P('items'), may hold values from 13 to 128, as said below
- embedding: bfloat16 [262, 768], replicated, may hold values from -6 to 6
- position: bfloat16 [2048, 768], replicated, may hold values from -5 to 5
- mask_vector: bfloat16 [768], replicated, may hold values from -6 to 6
- gain_bytes: bfloat16 [768], replicated, may hold values from 0.5 to 1.5
- key_enc: bfloat16 [768, 256], replicated, may hold values from -0.21875 to 0.21875
- value_enc: bfloat16 [768, 1280], replicated, may hold values from -0.21875 to 0.21875
- latent_init: bfloat16 [256, 1280], replicated, may hold values from -6 to 6
- gain_latent: bfloat16 [1280], replicated, may hold values from 0.5 to 1.5
- query_enc: bfloat16 [1280, 256], replicated, may hold values from -0.15625 to 0.15625
- out_enc: bfloat16 [1280, 1280], replicated, may hold values from -0.625 to 0.625
- gain_enc_mlp: bfloat16 [1280], replicated, may hold values from 0.5 to 1.5
- up_enc: bfloat16 [1280, 1280], replicated, may hold values from -0.15625 to 0.15625
- down_enc: bfloat16 [1280, 1280], replicated, may hold values from -0.25 to 0.25
- gain_self: bfloat16 [1280], replicated, may hold values from 0.5 to 1.5
- query_self: bfloat16 [1280, 256], replicated, may hold values from -0.15625 to 0.15625
- key_self: bfloat16 [1280, 256], replicated, may hold values from -0.15625 to 0.15625
- value_self: bfloat16 [1280, 1280], replicated, may hold values from -0.15625 to 0.15625
- out_self: bfloat16 [1280, 1280], replicated, may hold values from -0.5 to 0.5
- gain_self_mlp: bfloat16 [1280], replicated, may hold values from 0.5 to 1.5
- up_self: bfloat16 [1280, 1280], replicated, may hold values from -0.15625 to 0.15625
- down_self: bfloat16 [1280, 1280], replicated, may hold values from -0.25 to 0.25
- gain_dec_kv: bfloat16 [1280], replicated, may hold values from 0.5 to 1.5
- key_dec: bfloat16 [1280, 256], replicated, may hold values from -0.15625 to 0.15625
- value_dec: bfloat16 [1280, 768], replicated, may hold values from -0.15625 to 0.15625
- dec_query: bfloat16 [2048, 768], replicated, may hold values from -6 to 6
- gain_dec_q: bfloat16 [768], replicated, may hold values from 0.5 to 1.5
- query_dec: bfloat16 [768, 256], replicated, may hold values from -0.21875 to 0.21875
- out_dec: bfloat16 [768, 768], replicated, may hold values from -0.625 to 0.625
- gain_final: bfloat16 [768], replicated, may hold values from 0.5 to 1.5
- logit_cot: bfloat16 [32, 2048, 262], P('items', 'blk'), may hold values from -6 to 6
Outputs:
- logits: bfloat16 [32, 2048, 262], P('items', 'blk')
- grad_embedding: float32 [262, 768], P(None, ('items', 'blk'))
- grad_position: float32 [2048, 768], P(('items', 'blk'))
- grad_mask_vector: float32 [768], P(('items', 'blk'))
- grad_gain_bytes: float32 [768], P(('items', 'blk'))
- grad_key_enc: float32 [768, 256], P(('items', 'blk'))
- grad_value_enc: float32 [768, 1280], P(('items', 'blk'))
- grad_latent_init: float32 [256, 1280], P(('items', 'blk'))
- grad_gain_latent: float32 [1280], P(('items', 'blk'))
- grad_query_enc: float32 [1280, 256], P(('items', 'blk'))
- grad_out_enc: float32 [1280, 1280], P(('items', 'blk'))
- grad_gain_enc_mlp: float32 [1280], P(('items', 'blk'))
- grad_up_enc: float32 [1280, 1280], P(('items', 'blk'))
- grad_down_enc: float32 [1280, 1280], P(('items', 'blk'))
- grad_gain_self: float32 [1280], P(('items', 'blk'))
- grad_query_self: float32 [1280, 256], P(('items', 'blk'))
- grad_key_self: float32 [1280, 256], P(('items', 'blk'))
- grad_value_self: float32 [1280, 1280], P(('items', 'blk'))
- grad_out_self: float32 [1280, 1280], P(('items', 'blk'))
- grad_gain_self_mlp: float32 [1280], P(('items', 'blk'))
- grad_up_self: float32 [1280, 1280], P(('items', 'blk'))
- grad_down_self: float32 [1280, 1280], P(('items', 'blk'))
- grad_gain_dec_kv: float32 [1280], P(('items', 'blk'))
- grad_key_dec: float32 [1280, 256], P(('items', 'blk'))
- grad_value_dec: float32 [1280, 768], P(('items', 'blk'))
- grad_dec_query: float32 [2048, 768], P(('items', 'blk'))
- grad_gain_dec_q: float32 [768], P(('items', 'blk'))
- grad_query_dec: float32 [768, 256], P(('items', 'blk'))
- grad_out_dec: float32 [768, 768], P(('items', 'blk'))
- grad_gain_final: float32 [768], P(('items', 'blk'))
The draws below stay inside these ranges and needn't reach their ends.
Inputs may be any that keep to these rules, and one draw needn't show every extreme that they name: `span_start`: span s of an item lies inside bytes s * 256 to (s + 1) * 256 - 1; all spans of one item have the same length. `span_len`: between 5 and 50 percent of each item's bytes are masked.
All inputs are finite; a program needn't handle non-finite values.
Results may differ from the reference program's by a relative error of at most 0.02.
Values may be sent and summed in bfloat16 or wider, within the bound.
A program may use at most 384 MiB of HBM per device.

```python
import math
import jax
import jax.numpy as jnp
import numpy as np
from jax import lax

D = 768
C = 1280
QK = 256
HEADS = 8
LATENTS = 256
VOCAB = 262
BYTES = 2048
SPANS = 8
ITEMS = 32


def span_parts(key):
    region = BYTES // SPANS
    shortest = max((region + 19) // 20, 1)
    longest = region // 2
    lengths = jax.random.randint(jax.random.fold_in(key, 11), (ITEMS, 1), shortest, longest + 1)
    lengths = lengths.at[0, 0].set(longest).at[ITEMS - 1, 0].set(shortest)
    offsets = jax.random.randint(jax.random.fold_in(key, 12), (ITEMS, SPANS), 0, region - longest + 1)
    offsets = offsets.at[0, 0].set(0).at[0, SPANS - 1].set(region - longest)
    starts = offsets + region * jnp.arange(SPANS, dtype=jnp.int32)[None, :]
    return (starts.astype(jnp.int32), jnp.broadcast_to(lengths, (ITEMS, SPANS)).astype(jnp.int32))


def draw_span_start(key, part):
    starts, lengths = span_parts(key)
    return starts


def draw_span_len(key, part):
    starts, lengths = span_parts(key)
    return lengths


def with_ends(drawn, key, low, top_value):
    place = [jax.random.randint(jax.random.fold_in(key, axis), (), 0, length) for axis, length in enumerate(drawn.shape)]
    widest = drawn.shape.index(max(drawn.shape))
    beside = place[:widest] + [(place[widest] + 1) % drawn.shape[widest]] + place[widest + 1:]
    return drawn.at[tuple(place)].set(low).at[tuple(beside)].set(top_value)


def level_of(own_key, shape, shards, low, high):
    def one(dim, parts):
        steps = jax.random.uniform(jax.random.fold_in(jax.random.fold_in(own_key, 6), dim), (parts,), jnp.float32, low / len(shards), high / len(shards))
        return jnp.repeat(jnp.exp(steps), shape[dim] // parts).reshape((-1,) + (1,) * (len(shape) - dim - 1))

    level = one(*shards[0])
    for cut in shards[1:]:
        level = level * one(*cut)
    return level


def rank_bounds(amount, slope):
    weights = [(1 << 20) // math.isqrt(grade ** slope) + 1 for grade in range(1, amount + 1)]
    scale = 1 + sum(weights) // (1 << 30)
    return np.cumsum(np.array([max(1, weight // scale) for weight in weights]))


def skewed_ids(stream_key, shape, number_of, skew):
    table = rank_bounds(number_of, skew)
    lot = jax.random.randint(jax.random.fold_in(stream_key, 1), shape, 0, int(table[number_of - 1]))
    grade = jnp.searchsorted(jnp.asarray(table, jnp.int32), lot, side="right")
    return jax.random.permutation(jax.random.fold_in(stream_key, 2), number_of)[grade].astype(jnp.int32)


def bell_draw(key, dims, spread, reach, shards=(), kind=jnp.bfloat16):
    level = level_of(key, dims, shards, -0.22, 0.18) if shards else 1.0
    result = jax.random.normal(key, dims, jnp.float32) * spread * level
    return jnp.minimum(jnp.maximum(result, -reach), reach).astype(kind)


def setup_inputs(seed: int = 0) -> dict:
    arg_keys = jax.random.split(jax.random.key(seed), 34)
    return {
        "byte_ids": with_ends(skewed_ids(arg_keys[0], (ITEMS, BYTES), VOCAB, 2), jax.random.fold_in(arg_keys[0], 3), 0, VOCAB - 1).astype(jnp.int32),
        "span_start": draw_span_start(jax.random.fold_in(arg_keys[33], 71), 0),
        "span_len": draw_span_len(jax.random.fold_in(arg_keys[33], 71), 0),
        "embedding": bell_draw(arg_keys[3], (VOCAB, D), 1.0, 6.0),
        "position": bell_draw(arg_keys[4], (BYTES, D), 0.7, 5.0),
        "mask_vector": bell_draw(arg_keys[5], (D,), 1.0, 6.0),
        "gain_bytes": jnp.clip(1.0 + 0.1 * jax.random.normal(arg_keys[6], (D,), jnp.float32), 0.5, 1.5).astype(jnp.bfloat16),
        "key_enc": bell_draw(arg_keys[7], (D, QK), D ** -0.5, 0.21875),
        "value_enc": bell_draw(arg_keys[8], (D, C), D ** -0.5, 0.21875),
        "latent_init": bell_draw(arg_keys[9], (LATENTS, C), 1.0, 6.0),
        "gain_latent": jnp.clip(1.0 + 0.1 * jax.random.normal(arg_keys[10], (C,), jnp.float32), 0.5, 1.5).astype(jnp.bfloat16),
        "query_enc": bell_draw(arg_keys[11], (C, QK), C ** -0.5, 0.15625),
        "out_enc": bell_draw(arg_keys[12], (C, C), (C // 16) ** -0.5, 0.625),
        "gain_enc_mlp": jnp.clip(1.0 + 0.1 * jax.random.normal(arg_keys[13], (C,), jnp.float32), 0.5, 1.5).astype(jnp.bfloat16),
        "up_enc": bell_draw(arg_keys[14], (C, C), C ** -0.5, 0.15625),
        "down_enc": bell_draw(arg_keys[15], (C, C), (C // 2) ** -0.5, 0.25),
        "gain_self": jnp.clip(1.0 + 0.1 * jax.random.normal(arg_keys[16], (C,), jnp.float32), 0.5, 1.5).astype(jnp.bfloat16),
        "query_self": bell_draw(arg_keys[17], (C, QK), C ** -0.5, 0.15625),
        "key_self": bell_draw(arg_keys[18], (C, QK), C ** -0.5, 0.15625),
        "value_self": bell_draw(arg_keys[19], (C, C), C ** -0.5, 0.15625),
        "out_self": bell_draw(arg_keys[20], (C, C), (C // 8) ** -0.5, 0.5),
        "gain_self_mlp": jnp.clip(1.0 + 0.1 * jax.random.normal(arg_keys[21], (C,), jnp.float32), 0.5, 1.5).astype(jnp.bfloat16),
        "up_self": bell_draw(arg_keys[22], (C, C), C ** -0.5, 0.15625),
        "down_self": bell_draw(arg_keys[23], (C, C), (C // 2) ** -0.5, 0.25),
        "gain_dec_kv": jnp.clip(1.0 + 0.1 * jax.random.normal(arg_keys[24], (C,), jnp.float32), 0.5, 1.5).astype(jnp.bfloat16),
        "key_dec": bell_draw(arg_keys[25], (C, QK), C ** -0.5, 0.15625),
        "value_dec": bell_draw(arg_keys[26], (C, D), C ** -0.5, 0.15625),
        "dec_query": bell_draw(arg_keys[27], (BYTES, D), 1.0, 6.0),
        "gain_dec_q": jnp.clip(1.0 + 0.1 * jax.random.normal(arg_keys[28], (D,), jnp.float32), 0.5, 1.5).astype(jnp.bfloat16),
        "query_dec": bell_draw(arg_keys[29], (D, QK), D ** -0.5, 0.21875),
        "out_dec": bell_draw(arg_keys[30], (D, D), (D // 8) ** -0.5, 0.625),
        "gain_final": jnp.clip(1.0 + 0.1 * jax.random.normal(arg_keys[31], (D,), jnp.float32), 0.5, 1.5).astype(jnp.bfloat16),
        "logit_cot": bell_draw(arg_keys[32], (ITEMS, BYTES, VOCAB), 1.0, 6.0, ((0, 16), (1, 2))),
    }


@jax.custom_vjp
def low(v):
    return lax.optimization_barrier(v.astype(jnp.bfloat16)).astype(jnp.float32)

@jax.custom_vjp
def low_back(v):
    return v

def low_keep(v):
    return (low(v), None)

def low_pass(kept, grad):
    return (grad,)

def back_keep(v):
    return (v, None)

def back_low(kept, grad):
    return (low(grad),)
low.defvjp(low_keep, low_pass)
low_back.defvjp(back_keep, back_low)
EPS = 1e-05
HIGH = lax.Precision.HIGHEST
NAMES = ('embedding', 'position', 'mask_vector', 'gain_bytes', 'key_enc', 'value_enc', 'latent_init', 'gain_latent', 'query_enc', 'out_enc', 'gain_enc_mlp', 'up_enc', 'down_enc', 'gain_self', 'query_self', 'key_self', 'value_self', 'out_self', 'gain_self_mlp', 'up_self', 'down_self', 'gain_dec_kv', 'key_dec', 'value_dec', 'dec_query', 'gain_dec_q', 'query_dec', 'out_dec', 'gain_final')

def matmul(left, right):
    return jnp.dot(left, right, precision=HIGH)

def layer_norm(values_in, gain):
    centered = values_in - lax.optimization_barrier(jnp.mean(values_in, axis=-1, keepdims=True))
    variance = lax.optimization_barrier(jnp.mean(centered * centered, axis=-1, keepdims=True))
    return centered * lax.rsqrt(variance + EPS) * gain

def attend(queries, key_rows, value_rows, head_count):
    query_count = queries.shape[0]
    key_count = key_rows.shape[0]
    query_heads = queries.reshape(query_count, head_count, -1)
    key_heads = key_rows.reshape(key_count, head_count, -1)
    value_heads = value_rows.reshape(key_count, head_count, -1)
    scaling = query_heads.shape[2] ** (-0.5)
    scores = jnp.einsum('qhd,khd->hqk', query_heads, key_heads, precision=HIGH) * scaling
    attention_weights = low(jax.nn.softmax(scores, axis=-1))
    combined = jnp.einsum('hqk,khd->qhd', attention_weights, value_heads, precision=HIGH)
    return low(combined.reshape(query_count, -1))

def piece_bytes(params, item_ids, item_starts, item_lengths, first_byte):
    byte_count = item_ids.shape[0]
    places = first_byte + lax.iota(jnp.int32, byte_count)
    inside = (places[None, :] >= item_starts[:, None]) & (places[None, :] < item_starts[:, None] + item_lengths[:, None])
    masked = jnp.any(inside, axis=0)
    onehot = (item_ids[:, None] == lax.iota(jnp.int32, params['embedding'].shape[0])[None, :]).astype(jnp.float32)
    looked_up = matmul(onehot, params['embedding'])
    placed = lax.dynamic_slice_in_dim(params['position'], first_byte, byte_count, 0)
    bytes_in = jnp.where(masked[:, None], params['mask_vector'][None, :], looked_up) + placed
    normed = low(layer_norm(bytes_in, params['gain_bytes']))
    return (low(matmul(normed, params['key_enc'])), low(matmul(normed, params['value_enc'])))

def piece_latent(params, key_rows, value_rows, first_latent, latent_count):
    latents = lax.dynamic_slice_in_dim(params['latent_init'], first_latent, latent_count, 0)
    normed = low(layer_norm(latents, params['gain_latent']))
    queries = low(matmul(normed, params['query_enc']))
    attended = attend(queries, key_rows, value_rows, 1)
    after_attn = latents + matmul(attended, params['out_enc'])
    hidden = low(jax.nn.gelu(matmul(low(layer_norm(after_attn, params['gain_enc_mlp'])), params['up_enc'])))
    encoded = after_attn + matmul(hidden, params['down_enc'])
    normed_self = low(layer_norm(encoded, params['gain_self']))
    return (encoded, low(matmul(normed_self, params['query_self'])), low(matmul(normed_self, params['key_self'])), low(matmul(normed_self, params['value_self'])))

def piece_middle(params, encoded, query_rows, key_rows, value_rows):
    attended = attend(query_rows, key_rows, value_rows, HEADS)
    after_attn = encoded + matmul(attended, params['out_self'])
    hidden = low(jax.nn.gelu(matmul(low(layer_norm(after_attn, params['gain_self_mlp'])), params['up_self'])))
    latent_out = after_attn + matmul(hidden, params['down_self'])
    normed = low(layer_norm(latent_out, params['gain_dec_kv']))
    return (low(matmul(normed, params['key_dec'])), low(matmul(normed, params['value_dec'])))

def piece_decoder(params, key_rows, value_rows, first_byte, byte_count):
    queries_in = lax.dynamic_slice_in_dim(params['dec_query'], first_byte, byte_count, 0)
    normed = low(layer_norm(queries_in, params['gain_dec_q']))
    queries = low(matmul(normed, params['query_dec']))
    attended = attend(queries, key_rows, value_rows, 1)
    decoded = queries_in + matmul(attended, params['out_dec'])
    final = low(layer_norm(decoded, params['gain_final']))
    return low(matmul(final, params['embedding'].T))

def forward(weights, item_ids, item_starts, item_lengths):
    params = dict(zip(NAMES, weights))
    key_e, value_e = piece_bytes(params, item_ids, item_starts, item_lengths, 0)
    key_e, value_e = (low_back(key_e), low_back(value_e))
    encoded, query_s, key_s, value_s = piece_latent(params, key_e, value_e, 0, LATENTS)
    key_s, value_s = (low_back(key_s), low_back(value_s))
    key_d, value_d = piece_middle(params, encoded, query_s, key_s, value_s)
    key_d, value_d = (low_back(key_d), low_back(value_d))
    return piece_decoder(params, key_d, value_d, 0, BYTES)

def reference(byte_ids, span_start, span_len, embedding, position, mask_vector, gain_bytes, key_enc, value_enc, latent_init, gain_latent, query_enc, out_enc, gain_enc_mlp, up_enc, down_enc, gain_self, query_self, key_self, value_self, out_self, gain_self_mlp, up_self, down_self, gain_dec_kv, key_dec, value_dec, dec_query, gain_dec_q, query_dec, out_dec, gain_final, logit_cot):
    weights = tuple((weight.astype(jnp.float32) for weight in (embedding, position, mask_vector, gain_bytes, key_enc, value_enc, latent_init, gain_latent, query_enc, out_enc, gain_enc_mlp, up_enc, down_enc, gain_self, query_self, key_self, value_self, out_self, gain_self_mlp, up_self, down_self, gain_dec_kv, key_dec, value_dec, dec_query, gain_dec_q, query_dec, out_dec, gain_final)))

    def one_item(running, item):
        item_ids, item_starts, item_lengths, item_cot = item
        out_logits, pull = jax.vjp(lambda *current: forward(current, item_ids, item_starts, item_lengths), *weights)
        grads = pull(item_cot.astype(jnp.float32))
        return (tuple((left + right for left, right in zip(running, grads))), out_logits.astype(jnp.bfloat16))
    zeros = tuple((jnp.zeros(weight.shape, jnp.float32) for weight in weights))
    total, logits = lax.scan(one_item, zeros, (byte_ids, span_start, span_len, logit_cot))
    return (logits, total[0], total[1], total[2], total[3], total[4], total[5], total[6], total[7], total[8], total[9], total[10], total[11], total[12], total[13], total[14], total[15], total[16], total[17], total[18], total[19], total[20], total[21], total[22], total[23], total[24], total[25], total[26], total[27], total[28])
```

```python
import jax
import jax.numpy as jnp
from jax import lax
from jax.sharding import PartitionSpec as P

HEADS = 8
EPS = 1e-05
F32 = jnp.float32
BF16 = jnp.bfloat16
GELU_C = 0.7978845608028654
GELU_A = 0.044715


def nn(a, b):
    return lax.dot_general(a, b, (((1,), (0,)), ((), ())), preferred_element_type=F32)


def nt(a, b):
    return lax.dot_general(a, b, (((1,), (1,)), ((), ())), preferred_element_type=F32)


def tn(a, b):
    return lax.dot_general(a, b, (((0,), (0,)), ((), ())), preferred_element_type=F32)


def norm_forward(x, gain):
    centered = x - jnp.mean(x, axis=-1, keepdims=True)
    variance = jnp.mean(centered * centered, axis=-1, keepdims=True)
    rstd = lax.rsqrt(variance + EPS)
    hat = centered * rstd
    return (hat * gain.astype(F32)).astype(BF16), hat, rstd


def norm_backward(dy, hat, rstd, gain):
    dgain = jnp.sum(dy * hat, axis=0)
    dhat = dy * gain.astype(F32)
    first = jnp.mean(dhat, axis=-1, keepdims=True)
    second = jnp.mean(dhat * hat, axis=-1, keepdims=True)
    return rstd * (dhat - first - hat * second), dgain


def gelu_forward(u):
    t = jnp.tanh(GELU_C * (u + GELU_A * u * u * u))
    return (0.5 * u * (1.0 + t)).astype(BF16)


def gelu_backward(dh, u):
    t = jnp.tanh(GELU_C * (u + GELU_A * u * u * u))
    slope = 0.5 * (1.0 + t) + 0.5 * u * (1.0 - t * t) * GELU_C * (1.0 + 3.0 * GELU_A * u * u)
    return dh * slope


def softmax(s):
    e = jnp.exp(s - jnp.max(s, axis=-1, keepdims=True))
    return e / jnp.sum(e, axis=-1, keepdims=True)


def softmax_backward(dp, soft, scale):
    inner = jnp.sum(dp * soft, axis=-1, keepdims=True)
    return (soft * (dp - inner) * scale).astype(BF16)


class Reducer:
    def __init__(self):
        n_items = lax.axis_size("items")
        self.count = n_items * lax.axis_size("blk")
        self.k = n_items.bit_length() - 1
        self.n_items = n_items

    def bit(self, name):
        if name == "y":
            return lax.axis_index("blk")
        return (lax.axis_index("items") >> name) & 1

    def exchange(self, x, name):
        if name == "y":
            return lax.ppermute(x, "blk", [(0, 1), (1, 0)])
        return lax.ppermute(x, "items", [(i, i ^ (1 << name)) for i in range(self.n_items)])

    def split(self, g):
        rows, width = g.shape
        return g.astype(BF16).reshape((2,) * (self.k + 1) + (rows // self.count, width))

    def reduce(self, grads, order):
        dims = list(range(self.k - 1, -1, -1)) + ["y"]
        parts = [self.split(g) for g in grads]
        heights = [p.shape[-2] for p in parts]
        for number, name in enumerate(order):
            axis = dims.index(name)
            mine = self.bit(name)
            send = [lax.dynamic_index_in_dim(p, 1 - mine, axis, keepdims=False) for p in parts]
            keep = [lax.dynamic_index_in_dim(p, mine, axis, keepdims=False) for p in parts]
            if number == 0:
                send = [jnp.concatenate(send, axis=-2)] if len(send) > 1 else send
                keep = [jnp.concatenate(keep, axis=-2)] if len(keep) > 1 else keep
            got = self.exchange(send[0], name)
            total = keep[0].astype(F32) + got.astype(F32)
            last = number == len(order) - 1
            parts = [total if last else total.astype(BF16)]
            dims.pop(axis)
        out, at = [], 0
        for height in heights:
            out.append(parts[0][at : at + height])
            at += height
        return out


def local(
    byte_ids, span_start, span_len, embedding, position, mask_vector, gain_bytes, key_enc,
    value_enc, latent_init, gain_latent, query_enc, out_enc, gain_enc_mlp, up_enc, down_enc,
    gain_self, query_self, key_self, value_self, out_self, gain_self_mlp, up_self, down_self,
    gain_dec_kv, key_dec, value_dec, dec_query, gain_dec_q, query_dec, out_dec, gain_final,
    logit_cot,
):
    me = lax.axis_index("blk")
    half = byte_ids.shape[1]
    total = position.shape[0]
    vocab = embedding.shape[0]
    latents = latent_init.shape[0]
    reducer = Reducer()
    k = reducer.k
    order_yx = [0, "y", 1] + list(range(2, k))
    order_xy = [0, 1, "y"] + list(range(2, k))

    def swap(x):
        return lax.ppermute(x, "blk", [(0, 1), (1, 0)])

    def own_item(x):
        mine = lax.dynamic_index_in_dim(x, me, 0, keepdims=False)
        got = swap(lax.dynamic_index_in_dim(x, 1 - me, 0, keepdims=False))
        low_half = jnp.where(me == 0, mine, got)
        high_half = jnp.where(me == 0, got, mine)
        return jnp.concatenate([low_half, high_half], axis=0)

    ids = own_item(byte_ids)
    cot = own_item(logit_cot)
    starts = lax.dynamic_index_in_dim(span_start, me, 0, keepdims=False)
    lengths = lax.dynamic_index_in_dim(span_len, me, 0, keepdims=False)

    places = lax.iota(jnp.int32, total)
    inside = (places[None, :] >= starts[:, None]) & (places[None, :] < (starts + lengths)[:, None])
    codes = jnp.where(jnp.any(inside, axis=0), vocab, ids)
    padded = 512
    table = jnp.concatenate(
        [embedding, mask_vector[None, :], jnp.zeros((padded - vocab - 1, embedding.shape[1]), BF16)], axis=0
    )
    onehot = (codes[:, None] == lax.iota(jnp.int32, padded)[None, :]).astype(BF16)
    bytes_in = nn(onehot, table) + position.astype(F32)
    nb, hat_b, rstd_b = norm_forward(bytes_in, gain_bytes)
    k_e = nn(nb, key_enc).astype(BF16)
    v_e = nn(nb, value_enc).astype(BF16)

    latent32 = latent_init.astype(F32)
    nl, hat_l, rstd_l = norm_forward(latent32, gain_latent)
    q_e = nn(nl, query_enc).astype(BF16)
    scale_e = q_e.shape[1] ** (-0.5)
    soft_e = softmax(nt(q_e, k_e) * scale_e)
    p_e = soft_e.astype(BF16)
    a_e = nn(p_e, v_e).astype(BF16)
    after_enc = latent32 + nn(a_e, out_enc)
    n1, hat1, rstd1 = norm_forward(after_enc, gain_enc_mlp)
    u1 = nn(n1, up_enc)
    h1 = gelu_forward(u1)
    encoded = after_enc + nn(h1, down_enc)
    n2, hat2, rstd2 = norm_forward(encoded, gain_self)
    q_s = nn(n2, query_self).astype(BF16)
    k_s = nn(n2, key_self).astype(BF16)
    v_s = nn(n2, value_self).astype(BF16)

    def heads(x):
        return x.reshape(latents, HEADS, -1).transpose(1, 0, 2)

    def bdot(a, b, ca, cb):
        return lax.dot_general(a, b, (((ca,), (cb,)), ((0,), (0,))), preferred_element_type=F32)

    qh, kh, vh = heads(q_s), heads(k_s), heads(v_s)
    scale_s = qh.shape[2] ** (-0.5)
    soft_s = softmax(bdot(qh, kh, 2, 2) * scale_s)
    p_s = soft_s.astype(BF16)
    ah = bdot(p_s, vh, 2, 1).astype(BF16)
    a_s = ah.transpose(1, 0, 2).reshape(latents, -1)
    after_self = encoded + nn(a_s, out_self)
    n3, hat3, rstd3 = norm_forward(after_self, gain_self_mlp)
    u2 = nn(n3, up_self)
    h2 = gelu_forward(u2)
    latent_out = after_self + nn(h2, down_self)
    n4, hat4, rstd4 = norm_forward(latent_out, gain_dec_kv)
    k_d = nn(n4, key_dec).astype(BF16)
    v_d = nn(n4, value_dec).astype(BF16)

    query32 = dec_query.astype(F32)
    nq, hat_q, rstd_q = norm_forward(query32, gain_dec_q)
    q_d = nn(nq, query_dec).astype(BF16)
    scale_d = q_d.shape[1] ** (-0.5)
    soft_d = softmax(nt(q_d, k_d) * scale_d)
    p_d = soft_d.astype(BF16)
    a_d = nn(p_d, v_d).astype(BF16)
    decoded = query32 + nn(a_d, out_dec)
    nf, hat_f, rstd_f = norm_forward(decoded, gain_final)
    logits = nt(nf, embedding).astype(BF16)

    low_rows, high_rows = logits[:half], logits[half:]
    mine = jnp.where(me == 0, low_rows, high_rows)
    got = swap(jnp.where(me == 0, high_rows, low_rows))
    logits_out = jnp.stack([jnp.where(me == 0, mine, got), jnp.where(me == 0, got, mine)])

    dnf = nn(cot, embedding)
    g_emb_out = tn(nf, cot)
    ddec, g_gain_final = norm_backward(dnf, hat_f, rstd_f, gain_final)
    ddec16 = ddec.astype(BF16)
    da_d = nt(ddec16, out_dec)
    g_out_dec = tn(a_d, ddec16)
    da16 = da_d.astype(BF16)
    dv_d = tn(p_d, da16).astype(BF16)
    dp = nt(da16, v_d)
    ds = softmax_backward(dp, soft_d, scale_d)
    dq_d = nn(ds, k_d).astype(BF16)
    dk_d = tn(ds, q_d).astype(BF16)
    g_query_dec = tn(nq, dq_d)
    dnq, g_gain_dec_q = norm_backward(nt(dq_d, query_dec), hat_q, rstd_q, gain_dec_q)
    g_dec_query = ddec + dnq

    g_key_dec = tn(n4, dk_d)
    g_value_dec = tn(n4, dv_d)
    dlat, g_gain_dec_kv = norm_backward(nt(dk_d, key_dec) + nt(dv_d, value_dec), hat4, rstd4, gain_dec_kv)
    dlat16 = dlat.astype(BF16)
    g_down_self = tn(h2, dlat16)
    du2 = gelu_backward(nt(dlat16, down_self), u2).astype(BF16)
    g_up_self = tn(n3, du2)
    dx3, g_gain_self_mlp = norm_backward(nt(du2, up_self), hat3, rstd3, gain_self_mlp)
    dafter_self = dlat + dx3
    das16 = dafter_self.astype(BF16)
    g_out_self = tn(a_s, das16)
    da_s = heads(nt(das16, out_self))
    dah16 = da_s.astype(BF16)
    dvh = bdot(p_s, dah16, 1, 1)
    dps = bdot(dah16, vh, 2, 2)
    dss = softmax_backward(dps, soft_s, scale_s)
    dqh = bdot(dss, kh, 2, 1)
    dkh = bdot(dss, qh, 1, 1)

    def unheads(x):
        return x.transpose(1, 0, 2).reshape(latents, -1).astype(BF16)

    dq_s, dk_s, dv_s = unheads(dqh), unheads(dkh), unheads(dvh)
    g_query_self = tn(n2, dq_s)
    g_key_self = tn(n2, dk_s)
    g_value_self = tn(n2, dv_s)
    dn2 = nt(dq_s, query_self) + nt(dk_s, key_self) + nt(dv_s, value_self)
    dx2, g_gain_self = norm_backward(dn2, hat2, rstd2, gain_self)
    denc = dafter_self + dx2
    denc16 = denc.astype(BF16)
    g_down_enc = tn(h1, denc16)
    du1 = gelu_backward(nt(denc16, down_enc), u1).astype(BF16)
    g_up_enc = tn(n1, du1)
    dx1, g_gain_enc_mlp = norm_backward(nt(du1, up_enc), hat1, rstd1, gain_enc_mlp)
    dafter = denc + dx1
    daft16 = dafter.astype(BF16)
    g_out_enc = tn(a_e, daft16)
    da_e = nt(daft16, out_enc)
    dae16 = da_e.astype(BF16)
    dv_e = tn(p_e, dae16).astype(BF16)
    dpe = nt(dae16, v_e)
    dse = softmax_backward(dpe, soft_e, scale_e)
    dq_e = nn(dse, k_e).astype(BF16)
    dk_e = tn(dse, q_e).astype(BF16)
    g_query_enc = tn(nl, dq_e)
    dxl, g_gain_latent = norm_backward(nt(dq_e, query_enc), hat_l, rstd_l, gain_latent)
    g_latent = dafter + dxl

    g_key_enc = tn(nb, dk_e)
    g_value_enc = tn(nb, dv_e)
    dnb = nt(dk_e, key_enc) + nt(dv_e, value_enc)
    dbytes, g_gain_bytes = norm_backward(dnb, hat_b, rstd_b, gain_bytes)
    g_table = tn(dbytes.astype(BF16), onehot)
    g_emb = jnp.concatenate(
        [
            g_table[:, :vocab] + g_emb_out,
            g_table[:, vocab : vocab + 1],
            g_gain_bytes[:, None],
            g_gain_dec_q[:, None],
            g_gain_final[:, None],
            jnp.zeros((g_table.shape[0], padded - vocab - 4), F32),
        ],
        axis=1,
    )
    g_gains = jnp.stack(
        [g_gain_latent, g_gain_enc_mlp, g_gain_self, g_gain_self_mlp, g_gain_dec_kv], axis=1
    )
    g_gains = jnp.pad(g_gains, ((0, 0), (0, 256 - 5)))

    r_dec_query, r_out_dec, r_value_dec = reducer.reduce([g_dec_query, g_out_dec, g_value_dec], order_yx)
    r_down_self, r_up_self, r_out_self = reducer.reduce([g_down_self, g_up_self, g_out_self], order_xy)
    r_value_self, r_down_enc = reducer.reduce([g_value_self, g_down_enc], order_yx)
    r_up_enc, r_out_enc = reducer.reduce([g_up_enc, g_out_enc], order_xy)
    r_query_dec, r_key_dec, r_query_self, r_key_self = reducer.reduce(
        [g_query_dec, g_key_dec, g_query_self, g_key_self], order_xy
    )
    r_value_enc, r_latent = reducer.reduce([g_value_enc, g_latent], order_xy)
    (r_position,) = reducer.reduce([dbytes], order_yx)
    r_key_enc, r_query_enc, r_gains, r_emb_a, r_emb_b = reducer.reduce(
        [g_key_enc, g_query_enc, g_gains, g_emb[:, :256], g_emb[:, 256:]], order_yx
    )
    r_emb = jnp.concatenate([r_emb_a, r_emb_b], axis=1)
    return (
        logits_out,
        r_emb[:, :vocab].T,
        r_position,
        r_emb[:, vocab],
        r_emb[:, vocab + 1],
        r_key_enc,
        r_value_enc,
        r_latent,
        r_gains[:, 0],
        r_query_enc,
        r_out_enc,
        r_gains[:, 1],
        r_up_enc,
        r_down_enc,
        r_gains[:, 2],
        r_query_self,
        r_key_self,
        r_value_self,
        r_out_self,
        r_gains[:, 3],
        r_up_self,
        r_down_self,
        r_gains[:, 4],
        r_key_dec,
        r_value_dec,
        r_dec_query,
        r_emb[:, vocab + 2],
        r_query_dec,
        r_out_dec,
        r_emb[:, vocab + 3],
    )


def solution(mesh):
    split = P("items", "blk")
    rows = P(("items", "blk"))
    outs = [P("items", "blk", None), P(None, ("items", "blk"))] + [rows] * 28
    return jax.shard_map(
        local,
        mesh=mesh,
        in_specs=(split, P("items", None), P("items", None)) + (P(),) * 29 + (P("items", "blk", None),),
        out_specs=tuple(outs),
        check_vma=False,
    )
```

```python
import jax
import jax.numpy as jnp
from jax import lax
from jax.experimental import pallas as pl
from jax.experimental.pallas import tpu as pltpu
from jax.sharding import PartitionSpec as P

HEADS = 8
EPS = 1e-05
F32 = jnp.float32
BF16 = jnp.bfloat16
GELU_C = 0.7978845608028654
GELU_A = 0.044715


def nn(a, b):
    return lax.dot_general(a, b, (((1,), (0,)), ((), ())), preferred_element_type=F32)


def nt(a, b):
    return lax.dot_general(a, b, (((1,), (1,)), ((), ())), preferred_element_type=F32)


def tn(a, b):
    return lax.dot_general(a, b, (((0,), (0,)), ((), ())), preferred_element_type=F32)


def norm_forward(x, gain):
    centered = x - jnp.mean(x, axis=-1, keepdims=True)
    variance = jnp.mean(centered * centered, axis=-1, keepdims=True)
    rstd = lax.rsqrt(variance + EPS)
    hat = centered * rstd
    return (hat * gain.astype(F32)).astype(BF16), hat, rstd


def norm_backward(dy, hat, rstd, gain):
    dgain = jnp.sum(dy * hat, axis=0)
    dhat = dy * gain.astype(F32)
    first = jnp.mean(dhat, axis=-1, keepdims=True)
    second = jnp.mean(dhat * hat, axis=-1, keepdims=True)
    return rstd * (dhat - first - hat * second), dgain


def gelu_forward(u):
    t = jnp.tanh(GELU_C * (u + GELU_A * u * u * u))
    return (0.5 * u * (1.0 + t)).astype(BF16)


def gelu_backward(dh, u):
    t = jnp.tanh(GELU_C * (u + GELU_A * u * u * u))
    slope = 0.5 * (1.0 + t) + 0.5 * u * (1.0 - t * t) * GELU_C * (1.0 + 3.0 * GELU_A * u * u)
    return dh * slope


def softmax(s):
    e = jnp.exp(s - jnp.max(s, axis=-1, keepdims=True))
    return e / jnp.sum(e, axis=-1, keepdims=True)


def softmax_backward(dp, soft, scale):
    inner = jnp.sum(dp * soft, axis=-1, keepdims=True)
    return (soft * (dp - inner) * scale).astype(BF16)


class Reducer:
    def __init__(self):
        n_items = lax.axis_size("items")
        self.count = n_items * lax.axis_size("blk")
        self.k = n_items.bit_length() - 1
        self.n_items = n_items

    def bit(self, name):
        if name == "y":
            return lax.axis_index("blk")
        return (lax.axis_index("items") >> name) & 1

    def exchange(self, x, name):
        if name == "y":
            return lax.ppermute(x, "blk", [(0, 1), (1, 0)])
        return lax.ppermute(x, "items", [(i, i ^ (1 << name)) for i in range(self.n_items)])

    def split(self, g):
        rows, width = g.shape
        return g.astype(BF16).reshape((2,) * (self.k + 1) + (rows // self.count, width))

    def reduce(self, grads, order):
        dims = list(range(self.k - 1, -1, -1)) + ["y"]
        parts = [self.split(g) for g in grads]
        heights = [p.shape[-2] for p in parts]
        for number, name in enumerate(order):
            axis = dims.index(name)
            mine = self.bit(name)
            send = [lax.dynamic_index_in_dim(p, 1 - mine, axis, keepdims=False) for p in parts]
            keep = [lax.dynamic_index_in_dim(p, mine, axis, keepdims=False) for p in parts]
            if number == 0:
                send = [jnp.concatenate(send, axis=-2)] if len(send) > 1 else send
                keep = [jnp.concatenate(keep, axis=-2)] if len(keep) > 1 else keep
            got = self.exchange(send[0], name)
            total = keep[0].astype(F32) + got.astype(F32)
            last = number == len(order) - 1
            parts = [total if last else total.astype(BF16)]
            dims.pop(axis)
        out, at = [], 0
        for height in heights:
            out.append(parts[0][at : at + height])
            at += height
        return out


CHUNK = 256
LAG = 2
MESH = pl.DeviceIdType.MESH
STAGES = {"xy": ("c", "x", "y", "z0", "z1"), "yx": ("c", "y", "x", "z0", "z1")}
ITEM_BIT = {"c": 0, "x": 1, "z0": 2, "z1": 3}


def padded_rows(r):
    return -(-r // 16) * 16


def my_bit(name):
    if name == "y":
        return lax.axis_index("blk")
    return (lax.axis_index("items") // 2 ** ITEM_BIT[name]) % 2


def partner(name):
    if name == "y":
        return {"blk": 1 - lax.axis_index("blk")}
    return {"items": lax.axis_index("items") + (1 - 2 * my_bit(name)) * 2 ** ITEM_BIT[name]}


def divide(first, second, mine, r, by_rows):
    if by_rows:
        first, second = (
            jnp.concatenate([first[:r], second[:r]], axis=0),
            jnp.concatenate([first[r:], second[r:]], axis=0),
        )
    return jnp.where(mine == 0, first, second), jnp.where(mine == 0, second, first)


class Chunk:
    def __init__(self, bufs, at, sems, r, width, order):
        self.rc, self.r1, self.r2, self.r3, self.s4, self.r4, self.out = [b.at[at] for b in bufs]
        self.send, self.recv, self.at = sems[0], sems[1], at
        self.r, self.width, self.order = r, width, order
        self.step = 256 if r <= 40 and width % 256 == 0 else 128

    def copy(self, stage, source=None):
        src, dst = (
            (source, self.rc),
            (self.rc.at[:, :, 1], self.r1),
            (self.rc.at[:, 1, 0], self.r2),
            (self.rc.at[1, 0, 0], self.r3),
            (self.s4, self.r4),
        )[stage]
        return pltpu.make_async_remote_copy(
            src_ref=dst if src is None else src,
            dst_ref=dst,
            send_sem=self.send.at[self.at, stage],
            recv_sem=self.recv.at[self.at, stage],
            device_id=partner(STAGES[self.order][stage]),
            device_id_type=MESH,
        )

    def loop(self, pairs, body):
        columns = self.width // self.step

        def run(i, carry):
            body(i // columns, pl.ds(pl.multiple_of((i % columns) * self.step, self.step), self.step))
            return carry

        lax.fori_loop(0, pairs * columns, run, 0)

    def advance(self, stage, loaded=None):
        self.copy(stage).wait_recv()
        names = STAGES[self.order]
        r, kind, rc = self.r, self.rc.dtype, self.rc
        mine = my_bit(names[stage + 1]) if stage < 4 else None

        def total(a, b):
            return a.astype(F32) + b.astype(F32)

        def stage0(p, cols):
            q, z = p // 2, p % 2
            first = total(rc[q, z, 0, :, cols], loaded[q, z, 0, :, cols])
            second = total(rc[q, z, 1, :, cols], loaded[q, z, 1, :, cols])
            keep, send = divide(first, second, mine, r, self.order == "yx")
            rc[q, z, 0, :, cols] = keep.astype(kind)
            rc[q, z, 1, :, cols] = send.astype(kind)

        def stage1(q, cols):
            first = total(rc[q, 0, 0, :, cols], self.r1[q, 0, :, cols])
            second = total(rc[q, 1, 0, :, cols], self.r1[q, 1, :, cols])
            keep, send = divide(first, second, mine, r, True)
            rc[q, 0, 0, :, cols] = keep.astype(kind)
            rc[q, 1, 0, :, cols] = send.astype(kind)

        def stage2(q, cols):
            first = total(rc[0, 0, 0, :, cols], self.r2[0, :, cols])
            second = total(rc[1, 0, 0, :, cols], self.r2[1, :, cols])
            keep, send = divide(first, second, mine, r, True)
            rc[0, 0, 0, :, cols] = keep.astype(kind)
            rc[1, 0, 0, :, cols] = send.astype(kind)

        def stage3(q, cols):
            both = total(rc[0, 0, 0, :, cols], self.r3[:, cols])
            keep = jnp.where(mine == 0, both[:r], both[r:])
            send = jnp.where(mine == 0, both[r:], both[:r])
            extra = padded_rows(r) - r
            if extra:
                send = jnp.concatenate([send, jnp.zeros((extra, send.shape[1]), F32)], axis=0)
            self.s4[:, cols] = send.astype(kind)
            self.out[:, cols] = keep

        def stage4(q, cols):
            self.out[:, cols] = self.out[:, cols] + self.r4[:, cols].astype(F32)[:r]

        self.loop((4, 2, 1, 1, 1)[stage], (stage0, stage1, stage2, stage3, stage4)[stage])
        if stage < 4:
            self.copy(stage + 1).start()


def when(condition, action):
    if isinstance(condition, bool):
        if condition:
            action()
    else:
        pl.when(condition)(action)


def reduce_kernel(plan, *refs):
    widths, segments, others, steps = plan
    n_a, n_o = len(widths), len(others)
    a_src, o_src = refs[:n_a], refs[n_a : n_a + n_o]
    refs = refs[n_a + n_o :]
    a_out, o_out = refs[:n_a], refs[n_a : n_a + n_o]
    refs = refs[n_a + n_o :]
    a_bufs, refs = refs[:7], refs[7:]
    loads, refs = refs[0], refs[1:]
    o_bufs, refs = [refs[8 * i : 8 * i + 8] for i in range(n_o)], refs[8 * n_o :]
    a_sems, o_sems, load_sem, o_load_sem, a_out_sem, o_out_sem = refs[0:2], refs[2:4], refs[4], refs[5], refs[6], refs[7]
    core = my_bit("c")

    barrier = pltpu.get_barrier_semaphore()
    for name in ("c", "x", "y", "z0", "z1"):
        pl.semaphore_signal(barrier, inc=1, device_id=partner(name), device_id_type=MESH)
    pl.semaphore_wait(barrier, 5)

    def chunk(step, side):
        return Chunk(a_bufs, 2 * step + side, a_sems, 40, CHUNK, ("xy", "yx")[side])

    def columns(number):
        start = number * CHUNK
        return pl.ds(start if isinstance(number, int) else pl.multiple_of(start, CHUNK), CHUNK)

    def first_copy(segment, j, side):
        array, start = segments[segment][side]
        base = sum(seg[2] for seg in segments[:segment])
        return chunk(base + j, side).copy(0, a_src[array].at[:, :, :, 1 - core, :, columns(start + j)])

    def load(segment, step, j, side):
        array, start = segments[segment][side]
        slot = 2 * (step % 2) + side
        return pltpu.make_async_copy(
            a_src[array].at[:, :, :, core, :, columns(start + j)], loads.at[slot], load_sem.at[slot]
        )

    small = []
    for i, (r, width, order) in enumerate(others):
        rc, load_buf = o_bufs[i][0], o_bufs[i][7]
        item = Chunk([b.at[0:1] for b in o_bufs[i][:7]], 0, o_sems, r, width, order)
        item.at = i
        small.append(item)
        item.copy(0, o_src[i].at[:, :, :, 1 - core]).start()
        pltpu.make_async_copy(o_src[i].at[:, :, :, core], load_buf, o_load_sem.at[i]).start()
    for j in range(segments[0][2]):
        for side in range(2):
            first_copy(0, j, side).start()
    for i, item in enumerate(small):
        pltpu.make_async_copy(o_src[i].at[:, :, :, core], o_bufs[i][7], o_load_sem.at[i]).wait()
        item.advance(0, o_bufs[i][7])

    def lagged(step):
        for stage in range(4, 0, -1):
            old = step - stage * LAG
            if isinstance(step, int):
                go = 0 <= old < steps
            else:
                go = jnp.logical_and(old >= 0, old < steps)

            def act(old=old, stage=stage):
                for side in range(2):
                    chunk(old, side).advance(stage)

            when(go, act)

    base = 0
    for number, segment in enumerate(segments):
        count = segment[2]
        if number + 1 < len(segments):
            for j in range(segments[number + 1][2]):
                for side in range(2):
                    first_copy(number + 1, j, side).start()
        for side in range(2):
            load(number, base, 0, side).start()

        def step_body(j, number=number, base=base, count=count):
            step = base + j

            def ahead():
                for side in range(2):
                    load(number, step + 1, j + 1, side).start()

            when(j + 1 < count, ahead)
            for side in range(2):
                load(number, step, j, side).wait()
                chunk(step, side).advance(0, loads.at[2 * (step % 2) + side])
            lagged(step)

        if count > 1:

            def run(j, carry):
                step_body(j)
                return carry

            lax.fori_loop(0, count, run, 0)
        else:
            step_body(0)
        base += count
        if number < 4:
            for item in small:
                item.advance(number + 1)

    def drain(step, carry):
        lagged(step)
        return carry

    lax.fori_loop(steps, steps + 4 * LAG, drain, 0)

    outs = []
    for number, segment in enumerate(segments):
        base = sum(seg[2] for seg in segments[:number])
        for side in range(2):
            array, start = segment[side]
            for j in range(segment[2]):
                at = 2 * (base + j) + side
                outs.append(
                    pltpu.make_async_copy(
                        a_bufs[6].at[at], a_out[array].at[:, columns(start + j)], a_out_sem.at[at]
                    )
                )
    for i in range(n_o):
        outs.append(pltpu.make_async_copy(o_bufs[i][6].at[0], o_out[i], o_out_sem.at[i]))
    for copy in outs:
        copy.start()
    for number, segment in enumerate(segments):
        for j in range(segment[2]):
            for side in range(2):
                first_copy(number, j, side).wait_send()
    for i, item in enumerate(small):
        item.copy(0, o_src[i].at[:, :, :, 1 - core]).wait_send()
        for stage in range(1, 5):
            item.copy(stage).wait_send()

    def wait_sent(step, carry):
        for side in range(2):
            for stage in range(1, 5):
                chunk(step, side).copy(stage).wait_send()
        return carry

    lax.fori_loop(0, steps, wait_sent, 0)
    for copy in outs:
        copy.wait()


def buffers(count, r, width, kind):
    rp = padded_rows(r)
    return [
        pltpu.VMEM((count, 2, 2, 2, 2 * r, width), kind),
        pltpu.VMEM((count, 2, 2, 2 * r, width), kind),
        pltpu.VMEM((count, 2, 2 * r, width), kind),
        pltpu.VMEM((count, 2 * r, width), kind),
        pltpu.VMEM((count, rp, width), kind),
        pltpu.VMEM((count, rp, width), kind),
        pltpu.VMEM((count, r, width), F32),
    ]


def reduce_all(tall, segments, others):
    steps = sum(segment[2] for segment in segments)

    def view(g):
        return g.reshape(2, 2, 2, 2, g.shape[0] // 16, g.shape[1])

    plan = (
        tuple(g.shape[1] for g in tall),
        segments,
        tuple((g.shape[0] // 32, g.shape[1], order) for g, order in others),
        steps,
    )
    scratch = buffers(2 * steps, 40, CHUNK, BF16)
    scratch.append(pltpu.VMEM((4, 2, 2, 2, 80, CHUNK), BF16))
    for g, order in others:
        r = g.shape[0] // 32
        scratch += buffers(1, r, g.shape[1], g.dtype)
        scratch.append(pltpu.VMEM((2, 2, 2, 2 * r, g.shape[1]), g.dtype))
    dma = pltpu.SemaphoreType.DMA
    scratch += [dma((2 * steps, 5)), dma((2 * steps, 5)), dma((len(others), 5)), dma((len(others), 5))]
    scratch += [dma((4,)), dma((len(others),)), dma((2 * steps,)), dma((len(others),))]
    arrays = list(tall) + [g for g, order in others]
    anywhere = pl.BlockSpec(memory_space=pl.ANY)
    results = pl.pallas_call(
        lambda *refs: reduce_kernel(plan, *refs),
        out_shape=[jax.ShapeDtypeStruct((g.shape[0] // 32, g.shape[1]), F32) for g in arrays],
        in_specs=[anywhere] * len(arrays),
        out_specs=[anywhere] * len(arrays),
        scratch_shapes=scratch,
        compiler_params=pltpu.CompilerParams(
            collective_id=0, has_side_effects=True, vmem_limit_bytes=60 * 1024 * 1024
        ),
    )(*[view(g) for g in arrays])
    return results[: len(tall)], results[len(tall) :]


def local(
    byte_ids, span_start, span_len, embedding, position, mask_vector, gain_bytes, key_enc,
    value_enc, latent_init, gain_latent, query_enc, out_enc, gain_enc_mlp, up_enc, down_enc,
    gain_self, query_self, key_self, value_self, out_self, gain_self_mlp, up_self, down_self,
    gain_dec_kv, key_dec, value_dec, dec_query, gain_dec_q, query_dec, out_dec, gain_final,
    logit_cot,
):
    me = lax.axis_index("blk")
    half = byte_ids.shape[1]
    total = position.shape[0]
    vocab = embedding.shape[0]
    latents = latent_init.shape[0]
    reducer = Reducer()
    k = reducer.k
    order_yx = [0, "y", 1] + list(range(2, k))
    order_xy = [0, 1, "y"] + list(range(2, k))

    def swap(x):
        return lax.ppermute(x, "blk", [(0, 1), (1, 0)])

    def own_item(x):
        mine = lax.dynamic_index_in_dim(x, me, 0, keepdims=False)
        got = swap(lax.dynamic_index_in_dim(x, 1 - me, 0, keepdims=False))
        low_half = jnp.where(me == 0, mine, got)
        high_half = jnp.where(me == 0, got, mine)
        return jnp.concatenate([low_half, high_half], axis=0)

    ids = own_item(byte_ids)
    cot = own_item(logit_cot)
    starts = lax.dynamic_index_in_dim(span_start, me, 0, keepdims=False)
    lengths = lax.dynamic_index_in_dim(span_len, me, 0, keepdims=False)

    places = lax.iota(jnp.int32, total)
    inside = (places[None, :] >= starts[:, None]) & (places[None, :] < (starts + lengths)[:, None])
    codes = jnp.where(jnp.any(inside, axis=0), vocab, ids)
    padded = -(-(vocab + 1) // 128) * 128
    table = jnp.concatenate(
        [embedding, mask_vector[None, :], jnp.zeros((padded - vocab - 1, embedding.shape[1]), BF16)], axis=0
    )
    onehot = (codes[:, None] == lax.iota(jnp.int32, padded)[None, :]).astype(BF16)
    bytes_in = nn(onehot, table) + position.astype(F32)
    nb, hat_b, rstd_b = norm_forward(bytes_in, gain_bytes)
    k_e = nn(nb, key_enc).astype(BF16)
    v_e = nn(nb, value_enc).astype(BF16)

    latent32 = latent_init.astype(F32)
    nl, hat_l, rstd_l = norm_forward(latent32, gain_latent)
    q_e = nn(nl, query_enc).astype(BF16)
    scale_e = q_e.shape[1] ** (-0.5)
    soft_e = softmax(nt(q_e, k_e) * scale_e)
    p_e = soft_e.astype(BF16)
    a_e = nn(p_e, v_e).astype(BF16)
    after_enc = latent32 + nn(a_e, out_enc)
    n1, hat1, rstd1 = norm_forward(after_enc, gain_enc_mlp)
    u1 = nn(n1, up_enc)
    h1 = gelu_forward(u1)
    encoded = after_enc + nn(h1, down_enc)
    n2, hat2, rstd2 = norm_forward(encoded, gain_self)
    q_s = nn(n2, query_self).astype(BF16)
    k_s = nn(n2, key_self).astype(BF16)
    v_s = nn(n2, value_self).astype(BF16)

    def heads(x):
        return x.reshape(latents, HEADS, -1).transpose(1, 0, 2)

    def bdot(a, b, ca, cb):
        return lax.dot_general(a, b, (((ca,), (cb,)), ((0,), (0,))), preferred_element_type=F32)

    qh, kh, vh = heads(q_s), heads(k_s), heads(v_s)
    scale_s = qh.shape[2] ** (-0.5)
    soft_s = softmax(bdot(qh, kh, 2, 2) * scale_s)
    p_s = soft_s.astype(BF16)
    ah = bdot(p_s, vh, 2, 1).astype(BF16)
    a_s = ah.transpose(1, 0, 2).reshape(latents, -1)
    after_self = encoded + nn(a_s, out_self)
    n3, hat3, rstd3 = norm_forward(after_self, gain_self_mlp)
    u2 = nn(n3, up_self)
    h2 = gelu_forward(u2)
    latent_out = after_self + nn(h2, down_self)
    n4, hat4, rstd4 = norm_forward(latent_out, gain_dec_kv)
    k_d = nn(n4, key_dec).astype(BF16)
    v_d = nn(n4, value_dec).astype(BF16)

    query32 = dec_query.astype(F32)
    nq, hat_q, rstd_q = norm_forward(query32, gain_dec_q)
    q_d = nn(nq, query_dec).astype(BF16)
    scale_d = q_d.shape[1] ** (-0.5)
    soft_d = softmax(nt(q_d, k_d) * scale_d)
    p_d = soft_d.astype(BF16)
    a_d = nn(p_d, v_d).astype(BF16)
    decoded = query32 + nn(a_d, out_dec)
    nf, hat_f, rstd_f = norm_forward(decoded, gain_final)
    logits = nt(nf, embedding).astype(BF16)

    low_rows, high_rows = logits[:half], logits[half:]
    mine = jnp.where(me == 0, low_rows, high_rows)
    got = swap(jnp.where(me == 0, high_rows, low_rows))
    logits_out = jnp.stack([jnp.where(me == 0, mine, got), jnp.where(me == 0, got, mine)])

    dnf = nn(cot, embedding)
    g_emb_out = tn(nf, jnp.pad(cot, ((0, 0), (0, padded - vocab))))
    ddec, g_gain_final = norm_backward(dnf, hat_f, rstd_f, gain_final)
    ddec16 = ddec.astype(BF16)
    da_d = nt(ddec16, out_dec)
    g_out_dec = tn(a_d, ddec16)
    da16 = da_d.astype(BF16)
    dv_d = tn(p_d, da16).astype(BF16)
    dp = nt(da16, v_d)
    ds = softmax_backward(dp, soft_d, scale_d)
    dq_d = nn(ds, k_d).astype(BF16)
    dk_d = tn(ds, q_d).astype(BF16)
    g_query_dec = tn(nq, dq_d)
    dnq, g_gain_dec_q = norm_backward(nt(dq_d, query_dec), hat_q, rstd_q, gain_dec_q)
    g_dec_query = ddec + dnq

    g_key_dec = tn(n4, dk_d)
    g_value_dec = tn(n4, dv_d)
    dlat, g_gain_dec_kv = norm_backward(nt(dk_d, key_dec) + nt(dv_d, value_dec), hat4, rstd4, gain_dec_kv)
    dlat16 = dlat.astype(BF16)
    g_down_self = tn(h2, dlat16)
    du2 = gelu_backward(nt(dlat16, down_self), u2).astype(BF16)
    g_up_self = tn(n3, du2)
    dx3, g_gain_self_mlp = norm_backward(nt(du2, up_self), hat3, rstd3, gain_self_mlp)
    dafter_self = dlat + dx3
    das16 = dafter_self.astype(BF16)
    g_out_self = tn(a_s, das16)
    da_s = heads(nt(das16, out_self))
    dah16 = da_s.astype(BF16)
    dvh = bdot(p_s, dah16, 1, 1)
    dps = bdot(dah16, vh, 2, 2)
    dss = softmax_backward(dps, soft_s, scale_s)
    dqh = bdot(dss, kh, 2, 1)
    dkh = bdot(dss, qh, 1, 1)

    def unheads(x):
        return x.transpose(1, 0, 2).reshape(latents, -1).astype(BF16)

    dq_s, dk_s, dv_s = unheads(dqh), unheads(dkh), unheads(dvh)
    g_query_self = tn(n2, dq_s)
    g_key_self = tn(n2, dk_s)
    g_value_self = tn(n2, dv_s)
    dn2 = nt(dq_s, query_self) + nt(dk_s, key_self) + nt(dv_s, value_self)
    dx2, g_gain_self = norm_backward(dn2, hat2, rstd2, gain_self)
    denc = dafter_self + dx2
    denc16 = denc.astype(BF16)
    g_down_enc = tn(h1, denc16)
    du1 = gelu_backward(nt(denc16, down_enc), u1).astype(BF16)
    g_up_enc = tn(n1, du1)
    dx1, g_gain_enc_mlp = norm_backward(nt(du1, up_enc), hat1, rstd1, gain_enc_mlp)
    dafter = denc + dx1
    daft16 = dafter.astype(BF16)
    g_out_enc = tn(a_e, daft16)
    da_e = nt(daft16, out_enc)
    dae16 = da_e.astype(BF16)
    dv_e = tn(p_e, dae16).astype(BF16)
    dpe = nt(dae16, v_e)
    dse = softmax_backward(dpe, soft_e, scale_e)
    dq_e = nn(dse, k_e).astype(BF16)
    dk_e = tn(dse, q_e).astype(BF16)
    g_query_enc = tn(nl, dq_e)
    dxl, g_gain_latent = norm_backward(nt(dq_e, query_enc), hat_l, rstd_l, gain_latent)
    g_latent = dafter + dxl

    g_key_enc = tn(nb, dk_e)
    g_value_enc = tn(nb, dv_e)
    dnb = nt(dk_e, key_enc) + nt(dv_e, value_enc)
    dbytes, g_gain_bytes = norm_backward(dnb, hat_b, rstd_b, gain_bytes)
    g_table = tn(dbytes.astype(BF16), onehot) + g_emb_out
    wide_gains = [g_gain_latent, g_gain_enc_mlp, g_gain_self, g_gain_self_mlp, g_gain_dec_kv]
    byte_gains = [g_gain_bytes, g_gain_dec_q, g_gain_final]
    count = reducer.count
    vectors = jnp.concatenate([g.reshape(count, -1) for g in wide_gains + byte_gains], axis=1)
    length = vectors.shape[1]
    vectors = jnp.pad(vectors, ((0, 0), (0, 1024 - length))).reshape(count * 8, 128)

    if reducer.n_items == 16:
        low = lambda g: g.astype(BF16)
        tall = [
            g_up_enc, g_down_enc, g_out_enc, g_down_self, g_up_self, g_out_self,
            g_value_self, g_value_dec, g_key_self, g_query_self, g_key_dec, g_query_enc,
        ]
        segments = (
            ((0, 0), (1, 0), 5),
            ((2, 0), (3, 0), 5),
            ((4, 0), (5, 0), 5),
            ((6, 0), (7, 0), 3),
            ((6, 3), (8, 0), 1),
            ((6, 4), (9, 0), 1),
            ((10, 0), (11, 0), 1),
        )
        others = [
            (low(g_dec_query), "xy"), (low(dbytes), "yx"), (low(g_value_enc), "xy"), (low(g_out_dec), "yx"),
            (low(g_table), "yx"), (low(g_key_enc), "xy"), (low(g_query_dec), "yx"), (low(g_latent), "xy"),
            (vectors, "yx"),
        ]
        (
            r_up_enc, r_down_enc, r_out_enc, r_down_self, r_up_self, r_out_self,
            r_value_self, r_value_dec, r_key_self, r_query_self, r_key_dec, r_query_enc,
        ), (
            r_dec_query, r_position, r_value_enc, r_out_dec, r_emb, r_key_enc, r_query_dec, r_latent, r_vectors,
        ) = reduce_all([low(g) for g in tall], segments, others)
    else:
        r_dec_query, r_out_dec, r_value_dec = reducer.reduce([g_dec_query, g_out_dec, g_value_dec], order_yx)
        r_down_self, r_up_self, r_out_self = reducer.reduce([g_down_self, g_up_self, g_out_self], order_xy)
        r_value_self, r_down_enc = reducer.reduce([g_value_self, g_down_enc], order_yx)
        r_up_enc, r_out_enc = reducer.reduce([g_up_enc, g_out_enc], order_xy)
        r_query_dec, r_key_dec, r_query_self, r_key_self = reducer.reduce(
            [g_query_dec, g_key_dec, g_query_self, g_key_self], order_xy
        )
        r_value_enc, r_latent = reducer.reduce([g_value_enc, g_latent], order_xy)
        (r_position,) = reducer.reduce([dbytes], order_yx)
        r_key_enc, r_query_enc = reducer.reduce([g_key_enc, g_query_enc], order_yx)
        (r_emb,) = reducer.reduce([g_table], order_yx)
        (r_vectors,) = reducer.reduce([vectors], order_xy)

    flat = r_vectors.reshape(-1)
    pieces, at = [], 0
    for g in wide_gains + byte_gains:
        size = g.shape[0] // count
        pieces.append(flat[at : at + size])
        at += size
    (
        r_gain_latent, r_gain_enc_mlp, r_gain_self, r_gain_self_mlp, r_gain_dec_kv,
        r_gain_bytes, r_gain_dec_q, r_gain_final,
    ) = pieces
    return (
        logits_out, r_emb[:, :vocab].T, r_position, r_emb[:, vocab], r_gain_bytes, r_key_enc, r_value_enc,
        r_latent, r_gain_latent, r_query_enc, r_out_enc, r_gain_enc_mlp, r_up_enc, r_down_enc, r_gain_self,
        r_query_self, r_key_self, r_value_self, r_out_self, r_gain_self_mlp, r_up_self, r_down_self,
        r_gain_dec_kv, r_key_dec, r_value_dec, r_dec_query, r_gain_dec_q, r_query_dec, r_out_dec, r_gain_final,
    )


def solution(mesh):
    split = P("items", "blk")
    rows = P(("items", "blk"))
    outs = [P("items", "blk", None), P(None, ("items", "blk"))] + [rows] * 28
    return jax.shard_map(
        local,
        mesh=mesh,
        in_specs=(split, P("items", None), P("items", None)) + (P(),) * 29 + (P("items", "blk", None),),
        out_specs=tuple(outs),
        check_vma=False,
    )
```

```python
import jax
import jax.numpy as jnp
from jax import lax
from jax.experimental import pallas as pl
from jax.experimental.pallas import tpu as pltpu
from jax.sharding import PartitionSpec as P

HEADS = 8
EPS = 1e-05
F32 = jnp.float32
BF16 = jnp.bfloat16
GELU_C = 0.7978845608028654
GELU_A = 0.044715


def nn(a, b):
    return lax.dot_general(a, b, (((1,), (0,)), ((), ())), preferred_element_type=F32)


def nt(a, b):
    return lax.dot_general(a, b, (((1,), (1,)), ((), ())), preferred_element_type=F32)


def tn(a, b):
    return lax.dot_general(a, b, (((0,), (0,)), ((), ())), preferred_element_type=F32)


def norm_forward(x, gain):
    centered = x - jnp.mean(x, axis=-1, keepdims=True)
    variance = jnp.mean(centered * centered, axis=-1, keepdims=True)
    rstd = lax.rsqrt(variance + EPS)
    hat = centered * rstd
    return (hat * gain.astype(F32)).astype(BF16), hat, rstd


def norm_backward(dy, hat, rstd, gain):
    dgain = jnp.sum(dy * hat, axis=0)
    dhat = dy * gain.astype(F32)
    first = jnp.mean(dhat, axis=-1, keepdims=True)
    second = jnp.mean(dhat * hat, axis=-1, keepdims=True)
    return rstd * (dhat - first - hat * second), dgain


def gelu_forward(u):
    t = jnp.tanh(GELU_C * (u + GELU_A * u * u * u))
    return (0.5 * u * (1.0 + t)).astype(BF16)


def gelu_backward(dh, u):
    t = jnp.tanh(GELU_C * (u + GELU_A * u * u * u))
    slope = 0.5 * (1.0 + t) + 0.5 * u * (1.0 - t * t) * GELU_C * (1.0 + 3.0 * GELU_A * u * u)
    return dh * slope


def softmax(s):
    e = jnp.exp(s - jnp.max(s, axis=-1, keepdims=True))
    return e / jnp.sum(e, axis=-1, keepdims=True)


def softmax_backward(dp, soft, scale):
    inner = jnp.sum(dp * soft, axis=-1, keepdims=True)
    return (soft * (dp - inner) * scale).astype(BF16)


class Reducer:
    def __init__(self):
        n_items = lax.axis_size("items")
        self.count = n_items * lax.axis_size("blk")
        self.k = n_items.bit_length() - 1
        self.n_items = n_items

    def bit(self, name):
        if name == "y":
            return lax.axis_index("blk")
        return (lax.axis_index("items") >> name) & 1

    def exchange(self, x, name):
        if name == "y":
            return lax.ppermute(x, "blk", [(0, 1), (1, 0)])
        return lax.ppermute(x, "items", [(i, i ^ (1 << name)) for i in range(self.n_items)])

    def split(self, g):
        rows, width = g.shape
        return g.astype(BF16).reshape((2,) * (self.k + 1) + (rows // self.count, width))

    def reduce(self, grads, order):
        dims = list(range(self.k - 1, -1, -1)) + ["y"]
        parts = [self.split(g) for g in grads]
        heights = [p.shape[-2] for p in parts]
        for number, name in enumerate(order):
            axis = dims.index(name)
            mine = self.bit(name)
            send = [lax.dynamic_index_in_dim(p, 1 - mine, axis, keepdims=False) for p in parts]
            keep = [lax.dynamic_index_in_dim(p, mine, axis, keepdims=False) for p in parts]
            if number == 0:
                send = [jnp.concatenate(send, axis=-2)] if len(send) > 1 else send
                keep = [jnp.concatenate(keep, axis=-2)] if len(keep) > 1 else keep
            got = self.exchange(send[0], name)
            total = keep[0].astype(F32) + got.astype(F32)
            last = number == len(order) - 1
            parts = [total if last else total.astype(BF16)]
            dims.pop(axis)
        out, at = [], 0
        for height in heights:
            out.append(parts[0][at : at + height])
            at += height
        return out


CHUNK = 256
LAG = 2
MESH = pl.DeviceIdType.MESH
STAGES = {"xy": ("c", "x", "y", "z0", "z1"), "yx": ("c", "y", "x", "z0", "z1")}
ITEM_BIT = {"c": 0, "x": 1, "z0": 2, "z1": 3}


def padded_rows(r):
    return -(-r // 16) * 16


def my_bit(name):
    if name == "y":
        return lax.axis_index("blk")
    return (lax.axis_index("items") // 2 ** ITEM_BIT[name]) % 2


def partner(name):
    if name == "y":
        return {"blk": 1 - lax.axis_index("blk")}
    return {"items": lax.axis_index("items") + (1 - 2 * my_bit(name)) * 2 ** ITEM_BIT[name]}


def divide(first, second, mine, r, by_rows):
    if by_rows:
        first, second = (
            jnp.concatenate([first[:r], second[:r]], axis=0),
            jnp.concatenate([first[r:], second[r:]], axis=0),
        )
    return jnp.where(mine == 0, first, second), jnp.where(mine == 0, second, first)


class Chunk:
    def __init__(self, bufs, at, sems, r, width, order):
        self.rc, self.r1, self.r2, self.r3, self.s4, self.r4, self.out = [b.at[at] for b in bufs]
        self.send, self.recv, self.at = sems[0], sems[1], at
        self.r, self.width, self.order = r, width, order
        self.step = 256 if r <= 40 and width % 256 == 0 else 128

    def copy(self, stage, source=None):
        src, dst = (
            (source, self.rc),
            (self.rc.at[:, :, 1], self.r1),
            (self.rc.at[:, 1, 0], self.r2),
            (self.rc.at[1, 0, 0], self.r3),
            (self.s4, self.r4),
        )[stage]
        return pltpu.make_async_remote_copy(
            src_ref=dst if src is None else src,
            dst_ref=dst,
            send_sem=self.send.at[self.at, stage],
            recv_sem=self.recv.at[self.at, stage],
            device_id=partner(STAGES[self.order][stage]),
            device_id_type=MESH,
        )

    def loop(self, pairs, body):
        columns = self.width // self.step

        def run(i, carry):
            body(i // columns, pl.ds(pl.multiple_of((i % columns) * self.step, self.step), self.step))
            return carry

        lax.fori_loop(0, pairs * columns, run, 0)

    def advance(self, stage, loaded=None):
        self.copy(stage).wait_recv()
        names = STAGES[self.order]
        r, kind, rc = self.r, self.rc.dtype, self.rc
        mine = my_bit(names[stage + 1]) if stage < 4 else None

        def total(a, b):
            return a.astype(F32) + b.astype(F32)

        def stage0(p, cols):
            q, z = p // 2, p % 2
            first = total(rc[q, z, 0, :, cols], loaded[q, z, 0, :, cols])
            second = total(rc[q, z, 1, :, cols], loaded[q, z, 1, :, cols])
            keep, send = divide(first, second, mine, r, self.order == "yx")
            rc[q, z, 0, :, cols] = keep.astype(kind)
            rc[q, z, 1, :, cols] = send.astype(kind)

        def stage1(q, cols):
            first = total(rc[q, 0, 0, :, cols], self.r1[q, 0, :, cols])
            second = total(rc[q, 1, 0, :, cols], self.r1[q, 1, :, cols])
            keep, send = divide(first, second, mine, r, True)
            rc[q, 0, 0, :, cols] = keep.astype(kind)
            rc[q, 1, 0, :, cols] = send.astype(kind)

        def stage2(q, cols):
            first = total(rc[0, 0, 0, :, cols], self.r2[0, :, cols])
            second = total(rc[1, 0, 0, :, cols], self.r2[1, :, cols])
            keep, send = divide(first, second, mine, r, True)
            rc[0, 0, 0, :, cols] = keep.astype(kind)
            rc[1, 0, 0, :, cols] = send.astype(kind)

        def stage3(q, cols):
            both = total(rc[0, 0, 0, :, cols], self.r3[:, cols])
            keep = jnp.where(mine == 0, both[:r], both[r:])
            send = jnp.where(mine == 0, both[r:], both[:r])
            extra = padded_rows(r) - r
            if extra:
                send = jnp.concatenate([send, jnp.zeros((extra, send.shape[1]), F32)], axis=0)
            self.s4[:, cols] = send.astype(kind)
            self.out[:, cols] = keep

        def stage4(q, cols):
            self.out[:, cols] = self.out[:, cols] + self.r4[:, cols].astype(F32)[:r]

        self.loop((4, 2, 1, 1, 1)[stage], (stage0, stage1, stage2, stage3, stage4)[stage])
        if stage < 4:
            self.copy(stage + 1).start()


def when(condition, action):
    if isinstance(condition, bool):
        if condition:
            action()
    else:
        pl.when(condition)(action)


SLOTS = 4
AHEAD = 3
B_SLOTS = 3


def reduce_kernel(plan, *refs):
    sides, steps, n_act, n_cot, widths, others = plan
    n_a, n_o = len(widths), len(others)
    acts, refs = refs[:n_act], refs[n_act:]
    cots, refs = refs[:n_cot], refs[n_cot:]
    o_src, refs = refs[:n_o], refs[n_o:]
    a_out, o_out = refs[:n_a], refs[n_a : n_a + n_o]
    refs = refs[n_a + n_o :]
    a_bufs, refs = refs[:7], refs[7:]
    act_in, act_t, cot_in, made = refs[:4]
    refs = refs[4:]
    o_bufs, refs = [refs[8 * i : 8 * i + 8] for i in range(n_o)], refs[8 * n_o :]
    a_sems, o_sems = refs[0:2], refs[2:4]
    act_sem, cot_sem, o_load_sem, a_out_sem, o_out_sem = refs[4:]
    core = my_bit("c")
    rows = act_t.shape[1] // 4

    barrier = pltpu.get_barrier_semaphore()
    for name in ("c", "x", "y", "z0", "z1"):
        pl.semaphore_signal(barrier, inc=1, device_id=partner(name), device_id_type=MESH)
    pl.semaphore_wait(barrier, 5)

    def chunk(step, side):
        return Chunk(a_bufs, 2 * step + side, a_sems, 40, CHUNK, ("xy", "yx")[side])

    def act_copy(side, group):
        return pltpu.make_async_copy(acts[sides[side][0][group][1]], act_in.at[side], act_sem.at[side])

    def cot_copy(side, step):
        source, number, _ = sides[side][1][step]
        slot = step % B_SLOTS
        return pltpu.make_async_copy(
            cots[source].at[:, pl.ds(number * CHUNK, CHUNK)], cot_in.at[side, slot], cot_sem.at[side, slot]
        )

    def first_copy(step, side):
        return chunk(step, side).copy(0, made.at[side, step % SLOTS, 1 - core])

    def produce(step):
        for side in range(2):
            groups = sides[side][0]
            for g, (start, _) in enumerate(groups):

                def fresh(g=g, side=side, groups=groups):
                    act_copy(side, g).wait()

                    def turn(i, carry):
                        at = pl.ds(pl.multiple_of(i * 256, 256), 256)
                        act_t[side, at, :] = act_in[side, :, at].T
                        return carry

                    lax.fori_loop(0, act_in.shape[2] // 256, turn, 0)
                    if g + 1 < len(groups):
                        act_copy(side, g + 1).start()

                when(step == start, fresh)
            for later in range(B_SLOTS - 1, steps):
                when(step == later - (B_SLOTS - 1), lambda later=later, side=side: cot_copy(side, later).start())
            slot = step % B_SLOTS
            pltpu.make_async_copy(
                cots[0].at[:, pl.ds(0, CHUNK)], cot_in.at[side, slot], cot_sem.at[side, slot]
            ).wait()
            when(step >= SLOTS, lambda side=side: first_copy(step - SLOTS, side).wait_send())

            def product(i, carry, side=side, slot=slot):
                part = act_t[side, pl.ds(pl.multiple_of(i * rows, rows), rows), :]
                result = jnp.dot(part, cot_in[side, slot], preferred_element_type=F32)
                height = rows // 4
                for x in range(2):
                    for c in range(2):
                        at = (2 * x + c) * height
                        made[side, step % SLOTS, c, i // 2, i % 2, x] = result[at : at + height].astype(BF16)
                return carry

            lax.fori_loop(0, 4, product, 0)
            first_copy(step, side).start()

    small = []
    for i, (r, width, order) in enumerate(others):
        item = Chunk([b.at[0:1] for b in o_bufs[i][:7]], 0, o_sems, r, width, order)
        item.at = i
        small.append(item)
        item.copy(0, o_src[i].at[:, :, :, 1 - core]).start()
        pltpu.make_async_copy(o_src[i].at[:, :, :, core], o_bufs[i][7], o_load_sem.at[i]).start()
    for side in range(2):
        act_copy(side, 0).start()
        for step in range(B_SLOTS - 1):
            cot_copy(side, step).start()

    def begin(step, carry):
        produce(step)
        return carry

    lax.fori_loop(0, AHEAD, begin, 0)
    for i, item in enumerate(small):
        pltpu.make_async_copy(o_src[i].at[:, :, :, core], o_bufs[i][7], o_load_sem.at[i]).wait()
        item.advance(0, o_bufs[i][7])

    def run(step, carry):
        pl.when(step + AHEAD < steps)(lambda: produce(step + AHEAD))

        def enter():
            for side in range(2):
                chunk(step, side).advance(0, made.at[side, step % SLOTS, core])

        pl.when(step < steps)(enter)
        for stage in range(4, 0, -1):
            old = step - stage * LAG

            def act(old=old, stage=stage):
                for side in range(2):
                    chunk(old, side).advance(stage)

            pl.when(jnp.logical_and(old >= 0, old < steps))(act)
        for number in range(4):

            def others_on(number=number):
                for item in small:
                    item.advance(number + 1)

            pl.when(step == 4 + 5 * number)(others_on)
        return carry

    lax.fori_loop(0, steps + 4 * LAG, run, 0)

    outs = []
    for side in range(2):
        for step in range(steps):
            _, number, target = sides[side][1][step]
            at = 2 * step + side
            outs.append(
                pltpu.make_async_copy(
                    a_bufs[6].at[at], a_out[target].at[:, pl.ds(number * CHUNK, CHUNK)], a_out_sem.at[at]
                )
            )
    for i in range(n_o):
        outs.append(pltpu.make_async_copy(o_bufs[i][6].at[0], o_out[i], o_out_sem.at[i]))
    for copy in outs:
        copy.start()
    for step in range(steps - SLOTS, steps):
        for side in range(2):
            first_copy(step, side).wait_send()
    for i, item in enumerate(small):
        item.copy(0, o_src[i].at[:, :, :, 1 - core]).wait_send()
        for stage in range(1, 5):
            item.copy(stage).wait_send()

    def wait_sent(step, carry):
        for side in range(2):
            for stage in range(1, 5):
                chunk(step, side).copy(stage).wait_send()
        return carry

    lax.fori_loop(0, steps, wait_sent, 0)
    for copy in outs:
        copy.wait()


def buffers(count, r, width, kind):
    rp = padded_rows(r)
    return [
        pltpu.VMEM((count, 2, 2, 2, 2 * r, width), kind),
        pltpu.VMEM((count, 2, 2, 2 * r, width), kind),
        pltpu.VMEM((count, 2, 2 * r, width), kind),
        pltpu.VMEM((count, 2 * r, width), kind),
        pltpu.VMEM((count, rp, width), kind),
        pltpu.VMEM((count, rp, width), kind),
        pltpu.VMEM((count, r, width), F32),
    ]


def reduce_all(products, others):
    acts, cots, sides, widths = [], [], [], []
    for side in products:
        groups, sequence = [], []
        for act, own in side:
            groups.append((len(sequence), len(acts)))
            acts.append(act)
            for cot in own:
                for number in range(cot.shape[1] // CHUNK):
                    sequence.append((len(cots), number, len(widths)))
                cots.append(cot)
                widths.append(cot.shape[1])
        sides.append((tuple(groups), tuple(sequence)))
    steps = len(sides[0][1])
    assert steps == len(sides[1][1])

    def view(g):
        return g.reshape(2, 2, 2, 2, g.shape[0] // 16, g.shape[1])

    plan = (
        tuple(sides), steps, len(acts), len(cots), tuple(widths),
        tuple((g.shape[0] // 32, g.shape[1], order) for g, order in others),
    )
    depth, features = acts[0].shape
    scratch = buffers(2 * steps, 40, CHUNK, BF16)
    scratch += [
        pltpu.VMEM((2, depth, features), BF16),
        pltpu.VMEM((2, features, depth), BF16),
        pltpu.VMEM((2, B_SLOTS, depth, CHUNK), BF16),
        pltpu.VMEM((2, SLOTS, 2, 2, 2, 2, 80, CHUNK), BF16),
    ]
    for g, order in others:
        r = g.shape[0] // 32
        scratch += buffers(1, r, g.shape[1], g.dtype)
        scratch.append(pltpu.VMEM((2, 2, 2, 2 * r, g.shape[1]), g.dtype))
    dma = pltpu.SemaphoreType.DMA
    scratch += [dma((2 * steps, 5)), dma((2 * steps, 5)), dma((len(others), 5)), dma((len(others), 5))]
    scratch += [dma((2,)), dma((2, B_SLOTS)), dma((len(others),)), dma((2 * steps,)), dma((len(others),))]
    anywhere = pl.BlockSpec(memory_space=pl.ANY)
    arrays = acts + cots + [view(g) for g, order in others]
    results = pl.pallas_call(
        lambda *refs: reduce_kernel(plan, *refs),
        out_shape=[jax.ShapeDtypeStruct((features // 32, w), F32) for w in widths]
        + [jax.ShapeDtypeStruct((g.shape[0] // 32, g.shape[1]), F32) for g, order in others],
        in_specs=[anywhere] * len(arrays),
        out_specs=[anywhere] * (len(widths) + len(others)),
        scratch_shapes=scratch,
        compiler_params=pltpu.CompilerParams(
            collective_id=0, has_side_effects=True, vmem_limit_bytes=62 * 1024 * 1024
        ),
    )(*arrays)
    return results[: len(widths)], results[len(widths) :]


def finish(plain, table, vectors, sizes, vocab):
    count = len(plain)
    width = table.shape[0]

    def kernel(*refs):
        sources, refs = refs[:count], refs[count:]
        table_ref, vectors_ref = refs[:2]
        refs = refs[2:]
        targets, refs = refs[:count], refs[count:]
        emb_ref, mask_ref = refs[:2]
        gain_refs, refs = refs[2 : 2 + len(sizes)], refs[2 + len(sizes) :]
        staged, (in_sem, out_sem) = refs[:count], refs[count:]
        inward = [pltpu.make_async_copy(sources[i], staged[i], in_sem.at[i]) for i in range(count)]
        outward = [pltpu.make_async_copy(staged[i], targets[i], out_sem.at[i]) for i in range(count)]
        for copy in inward:
            copy.start()
        turned = table_ref[...].T
        emb_ref[...] = turned[:vocab]
        mask_ref[...] = turned[vocab]
        for i, gain_ref in enumerate(gain_refs):
            gain_ref[...] = vectors_ref[i, : sizes[i]]
        for i in range(count):
            inward[i].wait()
            outward[i].start()
        for copy in outward:
            copy.wait()

    anywhere = pl.BlockSpec(memory_space=pl.ANY)
    local_memory = pl.BlockSpec(memory_space=pltpu.VMEM)
    shapes = [jax.ShapeDtypeStruct(p.shape, F32) for p in plain]
    shapes += [jax.ShapeDtypeStruct((vocab, width), F32), jax.ShapeDtypeStruct((width,), F32)]
    shapes += [jax.ShapeDtypeStruct((n,), F32) for n in sizes]
    results = pl.pallas_call(
        kernel,
        out_shape=shapes,
        in_specs=[anywhere] * count + [local_memory] * 2,
        out_specs=[anywhere] * count + [local_memory] * (2 + len(sizes)),
        scratch_shapes=[pltpu.VMEM(p.shape, F32) for p in plain] + [pltpu.SemaphoreType.DMA((count,))] * 2,
    )(*plain, table, vectors)
    return results[:count], results[count], results[count + 1], results[count + 2 :]


def local(
    byte_ids, span_start, span_len, embedding, position, mask_vector, gain_bytes, key_enc,
    value_enc, latent_init, gain_latent, query_enc, out_enc, gain_enc_mlp, up_enc, down_enc,
    gain_self, query_self, key_self, value_self, out_self, gain_self_mlp, up_self, down_self,
    gain_dec_kv, key_dec, value_dec, dec_query, gain_dec_q, query_dec, out_dec, gain_final,
    logit_cot,
):
    me = lax.axis_index("blk")
    half = byte_ids.shape[1]
    total = position.shape[0]
    vocab = embedding.shape[0]
    latents = latent_init.shape[0]
    reducer = Reducer()
    k = reducer.k
    order_yx = [0, "y", 1] + list(range(2, k))
    order_xy = [0, 1, "y"] + list(range(2, k))

    def swap(x):
        return lax.ppermute(x, "blk", [(0, 1), (1, 0)])

    def own_item(x):
        mine = lax.dynamic_index_in_dim(x, me, 0, keepdims=False)
        got = swap(lax.dynamic_index_in_dim(x, 1 - me, 0, keepdims=False))
        low_half = jnp.where(me == 0, mine, got)
        high_half = jnp.where(me == 0, got, mine)
        return jnp.concatenate([low_half, high_half], axis=0)

    ids = own_item(byte_ids)
    cot = own_item(logit_cot)
    starts = lax.dynamic_index_in_dim(span_start, me, 0, keepdims=False)
    lengths = lax.dynamic_index_in_dim(span_len, me, 0, keepdims=False)

    places = lax.iota(jnp.int32, total)
    inside = (places[None, :] >= starts[:, None]) & (places[None, :] < (starts + lengths)[:, None])
    codes = jnp.where(jnp.any(inside, axis=0), vocab, ids)
    padded = -(-(vocab + 1) // 128) * 128
    table = jnp.concatenate(
        [embedding, mask_vector[None, :], jnp.zeros((padded - vocab - 1, embedding.shape[1]), BF16)], axis=0
    )
    onehot = (codes[:, None] == lax.iota(jnp.int32, padded)[None, :]).astype(BF16)
    bytes_in = nn(onehot, table) + position.astype(F32)
    nb, hat_b, rstd_b = norm_forward(bytes_in, gain_bytes)

    latent32 = latent_init.astype(F32)
    nl, hat_l, rstd_l = norm_forward(latent32, gain_latent)
    q_e = nn(nl, query_enc).astype(BF16)
    scale_e = q_e.shape[1] ** (-0.5)
    qk_e = nt(q_e, key_enc).astype(BF16)
    soft_e = softmax(nt(qk_e, nb) * scale_e)
    p_e = soft_e.astype(BF16)
    pn_e = nn(p_e, nb).astype(BF16)
    a_e = nn(pn_e, value_enc).astype(BF16)
    after_enc = latent32 + nn(a_e, out_enc)
    n1, hat1, rstd1 = norm_forward(after_enc, gain_enc_mlp)
    u1 = nn(n1, up_enc)
    h1 = gelu_forward(u1)
    encoded = after_enc + nn(h1, down_enc)
    n2, hat2, rstd2 = norm_forward(encoded, gain_self)
    q_s = nn(n2, query_self).astype(BF16)
    k_s = nn(n2, key_self).astype(BF16)
    v_s = nn(n2, value_self).astype(BF16)

    def heads(x):
        return x.reshape(latents, HEADS, -1).transpose(1, 0, 2)

    def bdot(a, b, ca, cb):
        return lax.dot_general(a, b, (((ca,), (cb,)), ((0,), (0,))), preferred_element_type=F32)

    qh, kh, vh = heads(q_s), heads(k_s), heads(v_s)
    scale_s = qh.shape[2] ** (-0.5)
    soft_s = softmax(bdot(qh, kh, 2, 2) * scale_s)
    p_s = soft_s.astype(BF16)
    ah = bdot(p_s, vh, 2, 1).astype(BF16)
    a_s = ah.transpose(1, 0, 2).reshape(latents, -1)
    after_self = encoded + nn(a_s, out_self)
    n3, hat3, rstd3 = norm_forward(after_self, gain_self_mlp)
    u2 = nn(n3, up_self)
    h2 = gelu_forward(u2)
    latent_out = after_self + nn(h2, down_self)
    n4, hat4, rstd4 = norm_forward(latent_out, gain_dec_kv)
    k_d = nn(n4, key_dec).astype(BF16)
    v_d = nn(n4, value_dec).astype(BF16)

    query32 = dec_query.astype(F32)
    nq, hat_q, rstd_q = norm_forward(query32, gain_dec_q)
    scale_d = k_d.shape[1] ** (-0.5)
    kq_d = nt(k_d, query_dec).astype(BF16)
    soft_d = softmax(nt(nq, kq_d) * scale_d)
    p_d = soft_d.astype(BF16)
    vo_d = nn(v_d, out_dec)
    decoded = query32 + nn(p_d, vo_d.astype(BF16))
    nf, hat_f, rstd_f = norm_forward(decoded, gain_final)
    logits = nt(nf, embedding).astype(BF16)

    low_rows, high_rows = logits[:half], logits[half:]
    logits_got = swap(jnp.where(me == 0, high_rows, low_rows))
    logits_own = jnp.where(me == 0, low_rows, high_rows)
    logits_out = jnp.stack([jnp.where(me == 0, logits_own, logits_got), jnp.where(me == 0, logits_got, logits_own)])

    dnf = nn(cot, embedding)
    g_emb_out = tn(nf, jnp.pad(cot, ((0, 0), (0, padded - vocab))))
    ddec, g_gain_final = norm_backward(dnf, hat_f, rstd_f, gain_final)
    ddec16 = ddec.astype(BF16)
    centered_vo = (vo_d - jnp.mean(vo_d, axis=0, keepdims=True)).astype(BF16)
    ds = softmax_backward(nt(ddec16, centered_vo), soft_d, scale_d)
    pd_d = tn(p_d, ddec16).astype(BF16)
    dv_d = nt(pd_d, out_dec).astype(BF16)
    g_out_dec = tn(v_d, pd_d)
    dn_d = tn(ds, nq).astype(BF16)
    dk_d = nn(dn_d, query_dec).astype(BF16)
    g_query_dec = tn(dn_d, k_d)
    dnq, g_gain_dec_q = norm_backward(nn(ds, kq_d), hat_q, rstd_q, gain_dec_q)
    g_dec_query = ddec + dnq

    dlat, g_gain_dec_kv = norm_backward(nt(dk_d, key_dec) + nt(dv_d, value_dec), hat4, rstd4, gain_dec_kv)
    dlat16 = dlat.astype(BF16)
    du2 = gelu_backward(nt(dlat16, down_self), u2).astype(BF16)
    dx3, g_gain_self_mlp = norm_backward(nt(du2, up_self), hat3, rstd3, gain_self_mlp)
    dafter_self = dlat + dx3
    das16 = dafter_self.astype(BF16)
    da_s = heads(nt(das16, out_self))
    dah16 = da_s.astype(BF16)
    dvh = bdot(p_s, dah16, 1, 1)
    dps = bdot(dah16, vh, 2, 2)
    dss = softmax_backward(dps, soft_s, scale_s)
    dqh = bdot(dss, kh, 2, 1)
    dkh = bdot(dss, qh, 1, 1)

    def unheads(x):
        return x.transpose(1, 0, 2).reshape(latents, -1).astype(BF16)

    dq_s, dk_s, dv_s = unheads(dqh), unheads(dkh), unheads(dvh)
    dn2 = nt(dq_s, query_self) + nt(dk_s, key_self) + nt(dv_s, value_self)
    dx2, g_gain_self = norm_backward(dn2, hat2, rstd2, gain_self)
    denc = dafter_self + dx2
    denc16 = denc.astype(BF16)
    du1 = gelu_backward(nt(denc16, down_enc), u1).astype(BF16)
    dx1, g_gain_enc_mlp = norm_backward(nt(du1, up_enc), hat1, rstd1, gain_enc_mlp)
    dafter = denc + dx1
    daft16 = dafter.astype(BF16)
    da_e = nt(daft16, out_enc)
    dae16 = da_e.astype(BF16)
    vd_e = nt(dae16, value_enc).astype(BF16)
    dse = softmax_backward(nt(vd_e, nb), soft_e, scale_e)
    dn_e = nn(dse, nb).astype(BF16)
    dq_e = nn(dn_e, key_enc).astype(BF16)
    dxl, g_gain_latent = norm_backward(nt(dq_e, query_enc), hat_l, rstd_l, gain_latent)
    g_latent = dafter + dxl

    g_key_enc = tn(dn_e, q_e)
    g_value_enc = tn(pn_e, dae16)
    dnb = tn(p_e, vd_e) + tn(dse, qk_e)
    dbytes, g_gain_bytes = norm_backward(dnb, hat_b, rstd_b, gain_bytes)
    g_table = tn(dbytes.astype(BF16), onehot) + g_emb_out
    wide_gains = [g_gain_latent, g_gain_enc_mlp, g_gain_self, g_gain_self_mlp, g_gain_dec_kv]
    byte_gains = [g_gain_bytes, g_gain_dec_q, g_gain_final]
    count = reducer.count
    lanes = 128
    vectors = jnp.stack(
        [jnp.pad(g.reshape(count, -1), ((0, 0), (0, lanes - g.shape[0] // count))) for g in wide_gains + byte_gains],
        axis=1,
    ).reshape(count * len(wide_gains + byte_gains), lanes)
    sizes = [g.shape[0] // count for g in wide_gains + byte_gains]

    def low(g):
        return g.astype(BF16)

    if reducer.n_items == 16:
        first_side = [(n1, [du1]), (a_e, [daft16]), (n3, [du2]), (n2, [dv_s, dk_s])]
        second_side = [
            (h1, [denc16]), (h2, [dlat16]), (a_s, [das16]), (n4, [dv_d, dk_d]), (n2, [dq_s]), (nl, [dq_e]),
        ]
        others = [
            (low(g_dec_query), "xy"), (low(dbytes), "yx"), (low(g_value_enc), "xy"), (low(g_out_dec), "yx"),
            (low(g_table), "yx"), (low(g_key_enc), "xy"), (low(g_query_dec), "yx"), (low(g_latent), "xy"),
            (vectors, "yx"),
        ]
        (
            r_up_enc, r_out_enc, r_up_self, r_value_self, r_key_self,
            r_down_enc, r_down_self, r_out_self, r_value_dec, r_key_dec, r_query_self, r_query_enc,
        ), (
            r_dec_query, r_position, r_value_enc, r_out_dec, r_emb, r_key_enc, r_query_dec, r_latent, r_vectors,
        ) = reduce_all((first_side, second_side), others)
    else:
        r_dec_query, r_out_dec, r_value_dec = reducer.reduce([g_dec_query, g_out_dec, tn(n4, dv_d)], order_yx)
        r_down_self, r_up_self, r_out_self = reducer.reduce(
            [tn(h2, dlat16), tn(n3, du2), tn(a_s, das16)], order_xy
        )
        r_value_self, r_down_enc = reducer.reduce([tn(n2, dv_s), tn(h1, denc16)], order_yx)
        r_up_enc, r_out_enc = reducer.reduce([tn(n1, du1), tn(a_e, daft16)], order_xy)
        r_query_dec, r_key_dec, r_query_self, r_key_self = reducer.reduce(
            [g_query_dec, tn(n4, dk_d), tn(n2, dq_s), tn(n2, dk_s)], order_xy
        )
        r_value_enc, r_latent = reducer.reduce([g_value_enc, g_latent], order_xy)
        (r_position,) = reducer.reduce([dbytes], order_yx)
        r_key_enc, r_query_enc = reducer.reduce([g_key_enc, tn(nl, dq_e)], order_yx)
        (r_emb,) = reducer.reduce([g_table], order_yx)
        (r_vectors,) = reducer.reduce([vectors], order_xy)

    plain = [
        r_position, r_key_enc, r_value_enc, r_latent, r_query_enc, r_out_enc, r_up_enc, r_down_enc,
        r_query_self, r_key_self, r_value_self, r_out_self, r_up_self, r_down_self, r_key_dec, r_value_dec,
        r_dec_query, r_query_dec, r_out_dec,
    ]
    plain, r_embedding, r_mask, gains = finish(plain, r_emb, r_vectors, sizes, vocab)
    (
        r_position, r_key_enc, r_value_enc, r_latent, r_query_enc, r_out_enc, r_up_enc, r_down_enc,
        r_query_self, r_key_self, r_value_self, r_out_self, r_up_self, r_down_self, r_key_dec, r_value_dec,
        r_dec_query, r_query_dec, r_out_dec,
    ) = plain
    (
        r_gain_latent, r_gain_enc_mlp, r_gain_self, r_gain_self_mlp, r_gain_dec_kv,
        r_gain_bytes, r_gain_dec_q, r_gain_final,
    ) = gains
    return (
        logits_out, r_embedding, r_position, r_mask, r_gain_bytes, r_key_enc, r_value_enc,
        r_latent, r_gain_latent, r_query_enc, r_out_enc, r_gain_enc_mlp, r_up_enc, r_down_enc, r_gain_self,
        r_query_self, r_key_self, r_value_self, r_out_self, r_gain_self_mlp, r_up_self, r_down_self,
        r_gain_dec_kv, r_key_dec, r_value_dec, r_dec_query, r_gain_dec_q, r_query_dec, r_out_dec, r_gain_final,
    )


def solution(mesh):
    split = P("items", "blk")
    rows = P(("items", "blk"))
    outs = [P("items", "blk", None), P(None, ("items", "blk"))] + [rows] * 28
    return jax.shard_map(
        local,
        mesh=mesh,
        in_specs=(split, P("items", None), P("items", None)) + (P(),) * 29 + (P("items", "blk", None),),
        out_specs=tuple(outs),
        check_vma=False,
    )
```

```python
import jax
import jax.numpy as jnp
from jax import lax
from jax.experimental import pallas as pl
from jax.experimental.pallas import tpu as pltpu
from jax.sharding import PartitionSpec as P

HEADS = 8
EPS = 1e-05
F32 = jnp.float32
BF16 = jnp.bfloat16
GELU_C = 0.7978845608028654
GELU_A = 0.044715


def nn(a, b):
    return lax.dot_general(a, b, (((1,), (0,)), ((), ())), preferred_element_type=F32)


def nt(a, b):
    return lax.dot_general(a, b, (((1,), (1,)), ((), ())), preferred_element_type=F32)


def tn(a, b):
    return lax.dot_general(a, b, (((0,), (0,)), ((), ())), preferred_element_type=F32)


def norm_forward(x, gain):
    centered = x - jnp.mean(x, axis=-1, keepdims=True)
    variance = jnp.mean(centered * centered, axis=-1, keepdims=True)
    rstd = lax.rsqrt(variance + EPS)
    hat = centered * rstd
    return (hat * gain.astype(F32)).astype(BF16), hat, rstd


def norm_backward(dy, hat, rstd, gain):
    dgain = jnp.sum(dy * hat, axis=0, keepdims=True)
    dhat = dy * gain.astype(F32)
    first = jnp.mean(dhat, axis=-1, keepdims=True)
    second = jnp.mean(dhat * hat, axis=-1, keepdims=True)
    return rstd * (dhat - first - hat * second), dgain


def gelu_forward(u):
    t = jnp.tanh(GELU_C * (u + GELU_A * u * u * u))
    return (0.5 * u * (1.0 + t)).astype(BF16)


def gelu_backward(dh, u):
    t = jnp.tanh(GELU_C * (u + GELU_A * u * u * u))
    slope = 0.5 * (1.0 + t) + 0.5 * u * (1.0 - t * t) * GELU_C * (1.0 + 3.0 * GELU_A * u * u)
    return dh * slope


def softmax(s):
    e = jnp.exp(s - jnp.max(s, axis=-1, keepdims=True))
    return e / jnp.sum(e, axis=-1, keepdims=True)


def softmax_backward(dp, soft, scale):
    inner = jnp.sum(dp * soft, axis=-1, keepdims=True)
    return (soft * (dp - inner) * scale).astype(BF16)


class Reducer:
    def __init__(self):
        n_items = lax.axis_size("items")
        self.count = n_items * lax.axis_size("blk")
        self.k = n_items.bit_length() - 1
        self.n_items = n_items

    def bit(self, name):
        if name == "y":
            return lax.axis_index("blk")
        return (lax.axis_index("items") >> name) & 1

    def exchange(self, x, name):
        if name == "y":
            return lax.ppermute(x, "blk", [(0, 1), (1, 0)])
        return lax.ppermute(x, "items", [(i, i ^ (1 << name)) for i in range(self.n_items)])

    def split(self, g):
        rows, width = g.shape
        return g.astype(BF16).reshape((2,) * (self.k + 1) + (rows // self.count, width))

    def reduce(self, grads, order):
        dims = list(range(self.k - 1, -1, -1)) + ["y"]
        parts = [self.split(g) for g in grads]
        heights = [p.shape[-2] for p in parts]
        for number, name in enumerate(order):
            axis = dims.index(name)
            mine = self.bit(name)
            send = [lax.dynamic_index_in_dim(p, 1 - mine, axis, keepdims=False) for p in parts]
            keep = [lax.dynamic_index_in_dim(p, mine, axis, keepdims=False) for p in parts]
            if number == 0:
                send = [jnp.concatenate(send, axis=-2)] if len(send) > 1 else send
                keep = [jnp.concatenate(keep, axis=-2)] if len(keep) > 1 else keep
            got = self.exchange(send[0], name)
            total = keep[0].astype(F32) + got.astype(F32)
            last = number == len(order) - 1
            parts = [total if last else total.astype(BF16)]
            dims.pop(axis)
        out, at = [], 0
        for height in heights:
            out.append(parts[0][at : at + height])
            at += height
        return out


CHUNK = 256
LAG = 2
MESH = pl.DeviceIdType.MESH
STAGES = {
    "xy": ("c", "x", "y", "z0", "z1"),
    "yx": ("c", "y", "x", "z0", "z1"),
}
ITEM_BIT = {"c": 0, "x": 1, "z0": 2, "z1": 3}


def padded_rows(r):
    return -(-r // 16) * 16


def my_bit(name):
    if name == "y":
        return lax.axis_index("blk")
    return (lax.axis_index("items") // 2 ** ITEM_BIT[name]) % 2


def partner(name):
    if name == "y":
        return {"blk": 1 - lax.axis_index("blk")}
    return {"items": lax.axis_index("items") + (1 - 2 * my_bit(name)) * 2 ** ITEM_BIT[name]}


def divide(first, second, mine, r, by_rows):
    if by_rows:
        first, second = (
            jnp.concatenate([first[:r], second[:r]], axis=0),
            jnp.concatenate([first[r:], second[r:]], axis=0),
        )
    return jnp.where(mine == 0, first, second), jnp.where(mine == 0, second, first)


class Chunk:
    def __init__(self, bufs, at, sems, r, width, order):
        self.rc, self.r1, self.r2, self.r3, self.s4, self.r4, self.out = [b.at[at] for b in bufs]
        self.send, self.recv, self.at = sems[0], sems[1], at
        self.r, self.width, self.order = r, width, order
        self.step = 256 if r <= 40 and width % 256 == 0 else 128

    def copy(self, stage, source=None):
        src, dst = (
            (source, self.rc),
            (self.rc.at[:, :, 1], self.r1),
            (self.rc.at[:, 1, 0], self.r2),
            (self.rc.at[1, 0, 0], self.r3),
            (self.s4, self.r4),
        )[stage]
        return pltpu.make_async_remote_copy(
            src_ref=dst if src is None else src,
            dst_ref=dst,
            send_sem=self.send.at[self.at, stage],
            recv_sem=self.recv.at[self.at, stage],
            device_id=partner(STAGES[self.order][stage]),
            device_id_type=MESH,
        )

    def loop(self, pairs, body):
        columns = self.width // self.step

        def run(i, carry):
            body(i // columns, pl.ds(pl.multiple_of((i % columns) * self.step, self.step), self.step))
            return carry

        lax.fori_loop(0, pairs * columns, run, 0)

    def advance(self, stage, loaded=None):
        self.copy(stage).wait_recv()
        names = STAGES[self.order]
        r, kind, rc = self.r, self.rc.dtype, self.rc
        mine = my_bit(names[stage + 1]) if stage < 4 else None

        def total(a, b):
            return a.astype(F32) + b.astype(F32)

        def stage0(p, cols):
            q, z = p // 2, p % 2
            first = total(rc[q, z, 0, :, cols], loaded[q, z, 0, :, cols])
            second = total(rc[q, z, 1, :, cols], loaded[q, z, 1, :, cols])
            keep, send = divide(first, second, mine, r, names[1] == "y")
            rc[q, z, 0, :, cols] = keep.astype(kind)
            rc[q, z, 1, :, cols] = send.astype(kind)

        def stage1(q, cols):
            first = total(rc[q, 0, 0, :, cols], self.r1[q, 0, :, cols])
            second = total(rc[q, 1, 0, :, cols], self.r1[q, 1, :, cols])
            keep, send = divide(first, second, mine, r, True)
            rc[q, 0, 0, :, cols] = keep.astype(kind)
            rc[q, 1, 0, :, cols] = send.astype(kind)

        def stage2(q, cols):
            first = total(rc[0, 0, 0, :, cols], self.r2[0, :, cols])
            second = total(rc[1, 0, 0, :, cols], self.r2[1, :, cols])
            keep, send = divide(first, second, mine, r, True)
            rc[0, 0, 0, :, cols] = keep.astype(kind)
            rc[1, 0, 0, :, cols] = send.astype(kind)

        def stage3(q, cols):
            both = total(rc[0, 0, 0, :, cols], self.r3[:, cols])
            keep = jnp.where(mine == 0, both[:r], both[r:])
            send = jnp.where(mine == 0, both[r:], both[:r])
            extra = padded_rows(r) - r
            if extra:
                send = jnp.concatenate([send, jnp.zeros((extra, send.shape[1]), F32)], axis=0)
            self.s4[:, cols] = send.astype(kind)
            self.out[:, cols] = keep

        def stage4(q, cols):
            self.out[:, cols] = self.out[:, cols] + self.r4[:, cols].astype(F32)[:r]

        self.loop((4, 2, 1, 1, 1)[stage], (stage0, stage1, stage2, stage3, stage4)[stage])
        if stage < 4:
            self.copy(stage + 1).start()


def when(condition, action):
    if isinstance(condition, bool):
        if condition:
            action()
    else:
        pl.when(condition)(action)


SLOTS = 4
AHEAD = 3
B_SLOTS = 3


def reduce_kernel(plan, *refs):
    sides, steps, n_act, n_cot, widths, others = plan
    n_a, n_o = len(widths), len(others)
    acts, refs = refs[:n_act], refs[n_act:]
    cots, refs = refs[:n_cot], refs[n_cot:]
    o_src, refs = refs[:n_o], refs[n_o:]
    a_out, o_out = refs[:n_a], refs[n_a : n_a + n_o]
    refs = refs[n_a + n_o :]
    a_bufs, refs = refs[:7], refs[7:]
    act_in, act_t, cot_in, made = refs[:4]
    refs = refs[4:]
    o_bufs, refs = [refs[8 * i : 8 * i + 8] for i in range(n_o)], refs[8 * n_o :]
    a_sems, o_sems = refs[0:2], refs[2:4]
    act_sem, cot_sem, o_load_sem, a_out_sem, o_out_sem = refs[4:]
    core = my_bit("c")
    rows = act_t.shape[1] // 4

    barrier = pltpu.get_barrier_semaphore()
    for name in ("c", "x", "y", "z0", "z1"):
        pl.semaphore_signal(barrier, inc=1, device_id=partner(name), device_id_type=MESH)
    pl.semaphore_wait(barrier, 5)

    def chunk(step, side):
        return Chunk(a_bufs, 2 * step + side, a_sems, 40, CHUNK, ("xy", "yx")[side])

    def act_copy(side, group):
        return pltpu.make_async_copy(acts[sides[side][0][group][1]], act_in.at[side], act_sem.at[side])

    def cot_copy(side, step):
        source, number, _ = sides[side][1][step]
        slot = step % B_SLOTS
        return pltpu.make_async_copy(
            cots[source].at[:, pl.ds(number * CHUNK, CHUNK)], cot_in.at[side, slot], cot_sem.at[side, slot]
        )

    def first_copy(step, side):
        return chunk(step, side).copy(0, made.at[side, step % SLOTS, 1 - core])

    def produce(step):
        for side in range(2):
            groups = sides[side][0]
            for g, (start, _) in enumerate(groups):

                def fresh(g=g, side=side, groups=groups):
                    act_copy(side, g).wait()

                    def turn(i, carry):
                        at = pl.ds(pl.multiple_of(i * 256, 256), 256)
                        act_t[side, at, :] = act_in[side, :, at].T
                        return carry

                    lax.fori_loop(0, act_in.shape[2] // 256, turn, 0)
                    if g + 1 < len(groups):
                        act_copy(side, g + 1).start()

                when(step == start, fresh)
            for later in range(B_SLOTS - 1, steps):
                when(step == later - (B_SLOTS - 1), lambda later=later, side=side: cot_copy(side, later).start())
            slot = step % B_SLOTS
            pltpu.make_async_copy(
                cots[0].at[:, pl.ds(0, CHUNK)], cot_in.at[side, slot], cot_sem.at[side, slot]
            ).wait()
            when(step >= SLOTS, lambda side=side: first_copy(step - SLOTS, side).wait_send())

            def product(i, carry, side=side, slot=slot):
                part = act_t[side, pl.ds(pl.multiple_of(i * rows, rows), rows), :]
                result = jnp.dot(part, cot_in[side, slot], preferred_element_type=F32)
                height = rows // 4
                for x in range(2):
                    for c in range(2):
                        at = (2 * x + c) * height
                        made[side, step % SLOTS, c, i // 2, i % 2, x] = result[at : at + height].astype(BF16)
                return carry

            lax.fori_loop(0, 4, product, 0)
            first_copy(step, side).start()

    small = []
    for i, (r, width, order) in enumerate(others):
        item = Chunk([b.at[0:1] for b in o_bufs[i][:7]], 0, o_sems, r, width, order)
        item.at = i
        small.append(item)
        item.copy(0, o_src[i].at[:, :, :, 1 - core]).start()
        pltpu.make_async_copy(o_src[i].at[:, :, :, core], o_bufs[i][7], o_load_sem.at[i]).start()
    for side in range(2):
        act_copy(side, 0).start()
        for step in range(B_SLOTS - 1):
            cot_copy(side, step).start()

    def begin(step, carry):
        produce(step)
        return carry

    lax.fori_loop(0, AHEAD, begin, 0)
    for i, item in enumerate(small):
        pltpu.make_async_copy(o_src[i].at[:, :, :, core], o_bufs[i][7], o_load_sem.at[i]).wait()
        item.advance(0, o_bufs[i][7])

    def run(step, carry):
        pl.when(step + AHEAD < steps)(lambda: produce(step + AHEAD))

        def enter():
            for side in range(2):
                chunk(step, side).advance(0, made.at[side, step % SLOTS, core])

        pl.when(step < steps)(enter)
        for stage in range(4, 0, -1):
            old = step - stage * LAG

            def act(old=old, stage=stage):
                for side in range(2):
                    chunk(old, side).advance(stage)

            pl.when(jnp.logical_and(old >= 0, old < steps))(act)
        for number in range(4):

            def others_on(number=number):
                for item in small:
                    item.advance(number + 1)

            pl.when(step == 4 + 5 * number)(others_on)
        return carry

    lax.fori_loop(0, steps + 4 * LAG, run, 0)

    outs = []
    for side in range(2):
        for step in range(steps):
            _, number, target = sides[side][1][step]
            at = 2 * step + side
            outs.append(
                pltpu.make_async_copy(
                    a_bufs[6].at[at], a_out[target].at[:, pl.ds(number * CHUNK, CHUNK)], a_out_sem.at[at]
                )
            )
    for i in range(n_o):
        outs.append(pltpu.make_async_copy(o_bufs[i][6].at[0], o_out[i], o_out_sem.at[i]))
    for copy in outs:
        copy.start()
    for step in range(steps - SLOTS, steps):
        for side in range(2):
            first_copy(step, side).wait_send()
    for i, item in enumerate(small):
        item.copy(0, o_src[i].at[:, :, :, 1 - core]).wait_send()
        for stage in range(1, 5):
            item.copy(stage).wait_send()

    def wait_sent(step, carry):
        for side in range(2):
            for stage in range(1, 5):
                chunk(step, side).copy(stage).wait_send()
        return carry

    lax.fori_loop(0, steps, wait_sent, 0)
    for copy in outs:
        copy.wait()


def buffers(count, r, width, kind):
    rp = padded_rows(r)
    return [
        pltpu.VMEM((count, 2, 2, 2, 2 * r, width), kind),
        pltpu.VMEM((count, 2, 2, 2 * r, width), kind),
        pltpu.VMEM((count, 2, 2 * r, width), kind),
        pltpu.VMEM((count, 2 * r, width), kind),
        pltpu.VMEM((count, rp, width), kind),
        pltpu.VMEM((count, rp, width), kind),
        pltpu.VMEM((count, r, width), F32),
    ]


def reduce_all(products, others):
    acts, cots, sides, widths = [], [], [], []
    for side in products:
        groups, sequence = [], []
        for act, own in side:
            groups.append((len(sequence), len(acts)))
            acts.append(act)
            for cot in own:
                for number in range(cot.shape[1] // CHUNK):
                    sequence.append((len(cots), number, len(widths)))
                cots.append(cot)
                widths.append(cot.shape[1])
        sides.append((tuple(groups), tuple(sequence)))
    steps = len(sides[0][1])
    assert steps == len(sides[1][1])

    def view(g):
        return g.reshape(2, 2, 2, 2, g.shape[0] // 16, g.shape[1])

    plan = (
        tuple(sides), steps, len(acts), len(cots), tuple(widths),
        tuple((g.shape[0] // 32, g.shape[1], order) for g, order in others),
    )
    depth, features = acts[0].shape
    scratch = buffers(2 * steps, 40, CHUNK, BF16)
    scratch += [
        pltpu.VMEM((2, depth, features), BF16),
        pltpu.VMEM((2, features, depth), BF16),
        pltpu.VMEM((2, B_SLOTS, depth, CHUNK), BF16),
        pltpu.VMEM((2, SLOTS, 2, 2, 2, 2, 80, CHUNK), BF16),
    ]
    for g, order in others:
        r = g.shape[0] // 32
        scratch += buffers(1, r, g.shape[1], g.dtype)
        scratch.append(pltpu.VMEM((2, 2, 2, 2 * r, g.shape[1]), g.dtype))
    dma = pltpu.SemaphoreType.DMA
    scratch += [dma((2 * steps, 5)), dma((2 * steps, 5)), dma((len(others), 5)), dma((len(others), 5))]
    scratch += [dma((2,)), dma((2, B_SLOTS)), dma((len(others),)), dma((2 * steps,)), dma((len(others),))]
    anywhere = pl.BlockSpec(memory_space=pl.ANY)
    arrays = acts + cots + [view(g) for g, order in others]
    results = pl.pallas_call(
        lambda *refs: reduce_kernel(plan, *refs),
        out_shape=[jax.ShapeDtypeStruct((features // 32, w), F32) for w in widths]
        + [jax.ShapeDtypeStruct((g.shape[0] // 32, g.shape[1]), F32) for g, order in others],
        in_specs=[anywhere] * len(arrays),
        out_specs=[anywhere] * (len(widths) + len(others)),
        scratch_shapes=scratch,
        compiler_params=pltpu.CompilerParams(
            collective_id=0, has_side_effects=True, vmem_limit_bytes=62 * 1024 * 1024
        ),
    )(*arrays)
    return results[: len(widths)], results[len(widths) :]


def finish(plain, table, vectors, vocab, vector_count):
    count = len(plain)
    width = table.shape[0]

    def kernel(*refs):
        sources, refs = refs[:count], refs[count:]
        table_ref, vectors_ref = refs[:2]
        refs = refs[2:]
        targets, refs = refs[:count], refs[count:]
        emb_ref, row_refs, refs = refs[0], refs[1:5], refs[5:]
        gain_refs, refs = refs[:vector_count], refs[vector_count:]
        staged, (in_sem, out_sem) = refs[:count], refs[count:]
        inward = [pltpu.make_async_copy(sources[i], staged[i], in_sem.at[i]) for i in range(count)]
        outward = [pltpu.make_async_copy(staged[i], targets[i], out_sem.at[i]) for i in range(count)]
        for copy in inward:
            copy.start()
        turned = table_ref[...].T
        emb_ref[...] = table_ref[:, :vocab]
        vector_rows = vectors_ref[...].T
        for i, row_ref in enumerate(row_refs):
            row_ref[...] = turned[vocab + i]
        for i, gain_ref in enumerate(gain_refs):
            gain_ref[...] = vector_rows[i]
        for i in range(count):
            inward[i].wait()
            outward[i].start()
        for copy in outward:
            copy.wait()

    anywhere = pl.BlockSpec(memory_space=pl.ANY)
    local_memory = pl.BlockSpec(memory_space=pltpu.VMEM)
    shapes = [jax.ShapeDtypeStruct(p.shape, F32) for p in plain]
    shapes += [jax.ShapeDtypeStruct((width, vocab), F32)] + [jax.ShapeDtypeStruct((width,), F32)] * 4
    shapes += [jax.ShapeDtypeStruct(vectors.shape[:1], F32)] * vector_count
    results = pl.pallas_call(
        kernel,
        out_shape=shapes,
        in_specs=[anywhere] * count + [local_memory] * 2,
        out_specs=[anywhere] * count + [local_memory] * (5 + vector_count),
        scratch_shapes=[pltpu.VMEM(p.shape, F32) for p in plain] + [pltpu.SemaphoreType.DMA((count,))] * 2,
    )(*plain, table, vectors)
    return results[:count], results[count], results[count + 1 : count + 5], results[count + 5 :]


def center(x):
    hat = x - jnp.mean(x, axis=-1, keepdims=True)
    rstd = lax.rsqrt(jnp.mean(hat * hat, axis=-1, keepdims=True) + EPS)
    return hat * rstd, rstd


def center_backward(dhat, hat, rstd):
    first = jnp.mean(dhat, axis=-1, keepdims=True)
    second = jnp.mean(dhat * hat, axis=-1, keepdims=True)
    return rstd * (dhat - first - hat * second)


def decoder_kernel(
    scale, query, cot, emb, key, value, w_query, w_out, gain_q, gain_f,
    logits, dquery, g_emb, g_gains, dkey, dvalue, g_query, g_out,
    g_pd, g_dn, kq, vo, vo_mid,
):
    @pl.when(pl.program_id(0) == 0)
    def _():
        for ref in (g_emb, g_pd, g_dn, g_gains):
            ref[...] = jnp.zeros_like(ref)
        kq[...] = nt(key[...], w_query[...]).astype(BF16)
        out = nn(value[...], w_out[...])
        vo[...] = out.astype(BF16)
        vo_mid[...] = (out - jnp.mean(out, axis=0, keepdims=True)).astype(BF16)

    x = query[...].astype(F32)
    hat_q, rstd_q = center(x)
    gq, gf = gain_q[...].astype(F32), gain_f[...].astype(F32)
    nq = (hat_q * gq).astype(BF16)
    soft = softmax(nt(nq, kq[...]) * scale)
    p = soft.astype(BF16)
    hat_f, rstd_f = center(x + nn(p, vo[...]))
    nf = (hat_f * gf).astype(BF16)
    logits[...] = nt(emb[...], nf).astype(BF16)
    dnf = nn(cot[...].T, emb[...])
    g_emb[...] += nn(cot[...], nf)
    g_gains[0:1] += jnp.sum(dnf * hat_f, axis=0, keepdims=True)
    ddec = center_backward(dnf * gf, hat_f, rstd_f)
    ddec16 = ddec.astype(BF16)
    g_pd[...] += nn(p.T, ddec16)
    ds = softmax_backward(nt(ddec16, vo_mid[...]), soft, scale)
    g_dn[...] += nn(ds.T, nq)
    dnq = nn(ds, kq[...])
    g_gains[1:2] += jnp.sum(dnq * hat_q, axis=0, keepdims=True)
    dquery[...] = (ddec + center_backward(dnq * gq, hat_q, rstd_q)).astype(BF16)

    @pl.when(pl.program_id(0) == pl.num_programs(0) - 1)
    def _():
        pd, dn = g_pd[...].astype(BF16), g_dn[...].astype(BF16)
        dvalue[...] = nt(pd, w_out[...]).astype(BF16)
        dkey[...] = nn(dn, w_query[...]).astype(BF16)
        g_out[...] = nn(value[...].T, pd).astype(BF16)
        g_query[...] = nn(dn.T, key[...]).astype(BF16)


def decoder_pass(query, cot, emb, key, value, w_query, w_out, gain_q, gain_f, scale):
    rows, width = query.shape
    vocab, latents, block = emb.shape[0], key.shape[0], 512

    def whole(x):
        return pl.BlockSpec(x.shape, lambda i: (0, 0))

    sums = jax.ShapeDtypeStruct((latents, width), F32)
    shapes = [
        jax.ShapeDtypeStruct((vocab, rows), BF16),
        jax.ShapeDtypeStruct((rows, width), BF16),
        jax.ShapeDtypeStruct((vocab, width), F32),
        jax.ShapeDtypeStruct((8, width), F32),
    ] + [jax.ShapeDtypeStruct(x.shape, BF16) for x in (key, value, w_query, w_out)]
    small = (gain_q[None, :], gain_f[None, :])
    return pl.pallas_call(
        lambda *refs: decoder_kernel(scale, *refs),
        grid=(rows // block,),
        out_shape=shapes,
        in_specs=[
            pl.BlockSpec((block, width), lambda i: (i, 0)),
            pl.BlockSpec((vocab, block), lambda i: (0, i)),
        ]
        + [whole(x) for x in (emb, key, value, w_query, w_out) + small],
        out_specs=[
            pl.BlockSpec((vocab, block), lambda i: (0, i)),
            pl.BlockSpec((block, width), lambda i: (i, 0)),
        ]
        + [whole(x) for x in shapes[2:]],
        scratch_shapes=[pltpu.VMEM(sums.shape, F32)] * 2 + [pltpu.VMEM(sums.shape, BF16)] * 3,
        compiler_params=pltpu.CompilerParams(vmem_limit_bytes=56 * 1024 * 1024),
    )(query, cot, emb, key, value, w_query, w_out, *small)


def bytes_kernel(at, p, ds, vd, qk, nb, rstd, gain, codes, emb, sums, wide, dbytes, table, turned, total):
    i = pl.program_id(0)

    @pl.when(i == 0)
    def _():
        total[...] = jnp.zeros_like(total)
        total[: emb.shape[0]] = emb[...]
        total[at + 1 : at + 2] = sums[1:2]
        total[at + 2 : at + 3] = sums[0:1]
        turned[...] = jnp.zeros_like(turned)
        turned[:, : wide.shape[0]] = wide[...].T

    g = gain[...].astype(F32)
    dnb = nn(p[...].T, vd[...]) + nn(ds[...].T, qk[...])
    hat = nb[...].astype(F32) / g
    dx = center_backward(dnb * g, hat, rstd[...]).astype(BF16)
    dbytes[...] = dx
    rows = lax.broadcasted_iota(jnp.int32, (total.shape[0], codes.shape[1]), 0)
    onehot = (rows == codes[...]).astype(BF16)
    total[...] += nn(onehot, dx)
    total[at : at + 1] += jnp.sum(dnb * hat, axis=0, keepdims=True)

    @pl.when(i == pl.num_programs(0) - 1)
    def _():
        table[...] = total[...].T.astype(BF16)


def bytes_backward(p, ds, vd, qk, nb, rstd, gain, codes, emb, sums, wide, at):
    rows, width = nb.shape
    latents, block, entries = p.shape[0], 256, -(-emb.shape[0] // 128) * 128
    features = wide.shape[1]
    return pl.pallas_call(
        lambda *refs: bytes_kernel(at, *refs),
        grid=(rows // block,),
        out_shape=[
            jax.ShapeDtypeStruct((rows, width), BF16),
            jax.ShapeDtypeStruct((width, entries), BF16),
            jax.ShapeDtypeStruct((features, 128), F32),
        ],
        in_specs=[
            pl.BlockSpec((latents, block), lambda i: (0, i)),
            pl.BlockSpec((latents, block), lambda i: (0, i)),
            pl.BlockSpec((latents, width), lambda i: (0, 0)),
            pl.BlockSpec((latents, width), lambda i: (0, 0)),
            pl.BlockSpec((block, width), lambda i: (i, 0)),
            pl.BlockSpec((block, 1), lambda i: (i, 0)),
            pl.BlockSpec((1, width), lambda i: (0, 0)),
            pl.BlockSpec((1, block), lambda i: (0, i)),
            pl.BlockSpec(emb.shape, lambda i: (0, 0)),
            pl.BlockSpec(sums.shape, lambda i: (0, 0)),
            pl.BlockSpec(wide.shape, lambda i: (0, 0)),
        ],
        out_specs=[
            pl.BlockSpec((block, width), lambda i: (i, 0)),
            pl.BlockSpec((width, entries), lambda i: (0, 0)),
            pl.BlockSpec((features, 128), lambda i: (0, 0)),
        ],
        scratch_shapes=[pltpu.VMEM((entries, width), F32)],
        compiler_params=pltpu.CompilerParams(vmem_limit_bytes=48 * 1024 * 1024),
    )(p, ds, vd, qk, nb, rstd, gain[None, :], codes[None, :], emb, sums, wide)


def head_columns(head, width):
    each = width // HEADS
    low, high = head * each // 128 * 128, -(-(head + 1) * each // 128) * 128
    place = low + lax.broadcasted_iota(jnp.int32, (1, high - low), 1)
    return slice(low, high), jnp.logical_and(place >= head * each, place < (head + 1) * each)


def pick(mask, x):
    return jnp.where(mask, x, jnp.zeros_like(x))


def head_softmax(head, q, k):
    columns, mask = head_columns(head, q.shape[1])
    scale = (q.shape[1] // HEADS) ** (-0.5)
    return softmax(nt(pick(mask, q[:, columns]), k[:, columns]) * scale), scale


def self_forward_kernel(q, k, v, out, total):
    total[...] = jnp.zeros_like(total)
    for head in range(HEADS):
        p = head_softmax(head, q, k)[0].astype(BF16)
        columns, mask = head_columns(head, v.shape[1])
        total[:, columns] += nn(p, pick(mask, v[:, columns]))
    out[...] = total[...].astype(BF16)


def self_backward_kernel(q, k, v, da, dq, dk, dv, dq_sum, dk_sum, dv_sum):
    for ref in (dq_sum, dk_sum, dv_sum):
        ref[...] = jnp.zeros_like(ref)
    for head in range(HEADS):
        soft, scale = head_softmax(head, q, k)
        columns, mask = head_columns(head, v.shape[1])
        da_head = pick(mask, da[:, columns])
        ds = softmax_backward(nt(da_head, v[:, columns]), soft, scale)
        dv_sum[:, columns] += nn(soft.astype(BF16).T, da_head)
        columns, mask = head_columns(head, q.shape[1])
        dq_sum[:, columns] += nn(ds, pick(mask, k[:, columns]))
        dk_sum[:, columns] += nn(ds.T, pick(mask, q[:, columns]))
    dq[...] = dq_sum[...].astype(BF16)
    dk[...] = dk_sum[...].astype(BF16)
    dv[...] = dv_sum[...].astype(BF16)


def self_forward(q, k, v):
    return pl.pallas_call(
        self_forward_kernel,
        out_shape=jax.ShapeDtypeStruct(v.shape, BF16),
        scratch_shapes=[pltpu.VMEM(v.shape, F32)],
        compiler_params=pltpu.CompilerParams(vmem_limit_bytes=32 * 1024 * 1024),
    )(q, k, v)


def self_backward(q, k, v, da):
    return pl.pallas_call(
        self_backward_kernel,
        out_shape=[jax.ShapeDtypeStruct(x.shape, BF16) for x in (q, k, v)],
        scratch_shapes=[pltpu.VMEM(x.shape, F32) for x in (q, k, v)],
        compiler_params=pltpu.CompilerParams(vmem_limit_bytes=32 * 1024 * 1024),
    )(q, k, v, da)


def local(
    byte_ids, span_start, span_len, embedding, position, mask_vector, gain_bytes, key_enc,
    value_enc, latent_init, gain_latent, query_enc, out_enc, gain_enc_mlp, up_enc, down_enc,
    gain_self, query_self, key_self, value_self, out_self, gain_self_mlp, up_self, down_self,
    gain_dec_kv, key_dec, value_dec, dec_query, gain_dec_q, query_dec, out_dec, gain_final,
    logit_cot,
):
    me = lax.axis_index("blk")
    half = byte_ids.shape[1]
    total = position.shape[0]
    vocab = embedding.shape[0]
    latents = latent_init.shape[0]
    reducer = Reducer()
    k = reducer.k
    order_yx = [0, "y", 1] + list(range(2, k))
    order_xy = [0, 1, "y"] + list(range(2, k))

    def swap(x):
        return lax.ppermute(x, "blk", [(0, 1), (1, 0)])

    def own_item(x, axis):
        mine = lax.dynamic_index_in_dim(x, me, axis, keepdims=False)
        got = swap(lax.dynamic_index_in_dim(x, 1 - me, axis, keepdims=False))
        low_half = jnp.where(me == 0, mine, got)
        high_half = jnp.where(me == 0, got, mine)
        return jnp.concatenate([low_half, high_half], axis=-1)

    ids = own_item(byte_ids, 0)
    cot = own_item(logit_cot.transpose(2, 0, 1), 1)
    entries = -(-(vocab + 4) // 16) * 16
    cot = jnp.pad(cot, ((0, entries - vocab), (0, 0)))
    emb_rows = jnp.pad(embedding, ((0, entries - vocab), (0, 0)))
    starts = lax.dynamic_index_in_dim(span_start, me, 0, keepdims=False)
    lengths = lax.dynamic_index_in_dim(span_len, me, 0, keepdims=False)

    places = lax.iota(jnp.int32, total)
    inside = (places[None, :] >= starts[:, None]) & (places[None, :] < (starts + lengths)[:, None])
    codes = jnp.where(jnp.any(inside, axis=0), vocab, ids)
    padded = -(-(vocab + 4) // 128) * 128
    table = jnp.concatenate(
        [embedding, mask_vector[None, :], jnp.zeros((padded - vocab - 1, embedding.shape[1]), BF16)], axis=0
    )
    onehot = (codes[:, None] == lax.iota(jnp.int32, padded)[None, :]).astype(BF16)
    bytes_in = nn(onehot, table) + position.astype(F32)
    nb, hat_b, rstd_b = norm_forward(bytes_in, gain_bytes)

    latent32 = latent_init.astype(F32)
    nl, hat_l, rstd_l = norm_forward(latent32, gain_latent)
    q_e = nn(nl, query_enc).astype(BF16)
    scale_e = q_e.shape[1] ** (-0.5)
    qk_e = nt(q_e, key_enc).astype(BF16)
    soft_e = softmax(nt(qk_e, nb) * scale_e)
    p_e = soft_e.astype(BF16)
    pn_e = nn(p_e, nb).astype(BF16)
    a_e = nn(pn_e, value_enc).astype(BF16)
    after_enc = latent32 + nn(a_e, out_enc)
    n1, hat1, rstd1 = norm_forward(after_enc, gain_enc_mlp)
    u1 = nn(n1, up_enc)
    h1 = gelu_forward(u1)
    encoded = after_enc + nn(h1, down_enc)
    n2, hat2, rstd2 = norm_forward(encoded, gain_self)
    q_s = nn(n2, query_self).astype(BF16)
    k_s = nn(n2, key_self).astype(BF16)
    v_s = nn(n2, value_self).astype(BF16)

    a_s = self_forward(q_s, k_s, v_s)
    after_self = encoded + nn(a_s, out_self)
    n3, hat3, rstd3 = norm_forward(after_self, gain_self_mlp)
    u2 = nn(n3, up_self)
    h2 = gelu_forward(u2)
    latent_out = after_self + nn(h2, down_self)
    n4, hat4, rstd4 = norm_forward(latent_out, gain_dec_kv)
    k_d = nn(n4, key_dec).astype(BF16)
    v_d = nn(n4, value_dec).astype(BF16)

    scale_d = k_d.shape[1] ** (-0.5)
    logits, g_dec_query, g_emb_out, gain_sums, dk_d, dv_d, g_query_dec, g_out_dec = decoder_pass(
        dec_query, cot, emb_rows, k_d, v_d, query_dec, out_dec, gain_dec_q, gain_final, scale_d
    )
    logits = logits[:vocab]
    logits_got = swap(jnp.where(me == 0, logits[:, half:], logits[:, :half]))
    logits_own = jnp.where(me == 0, logits[:, :half], logits[:, half:])
    side = lax.broadcasted_iota(jnp.int32, (1, 2, 1), 1)
    logits_out = jnp.where(side == me, logits_own[:, None, :], logits_got[:, None, :]).transpose(1, 2, 0)

    dlat, g_gain_dec_kv = norm_backward(nt(dk_d, key_dec) + nt(dv_d, value_dec), hat4, rstd4, gain_dec_kv)
    dlat16 = dlat.astype(BF16)
    du2 = gelu_backward(nt(dlat16, down_self), u2).astype(BF16)
    dx3, g_gain_self_mlp = norm_backward(nt(du2, up_self), hat3, rstd3, gain_self_mlp)
    dafter_self = dlat + dx3
    das16 = dafter_self.astype(BF16)
    dq_s, dk_s, dv_s = self_backward(q_s, k_s, v_s, nt(das16, out_self).astype(BF16))
    dn2 = nt(dq_s, query_self) + nt(dk_s, key_self) + nt(dv_s, value_self)
    dx2, g_gain_self = norm_backward(dn2, hat2, rstd2, gain_self)
    denc = dafter_self + dx2
    denc16 = denc.astype(BF16)
    du1 = gelu_backward(nt(denc16, down_enc), u1).astype(BF16)
    dx1, g_gain_enc_mlp = norm_backward(nt(du1, up_enc), hat1, rstd1, gain_enc_mlp)
    dafter = denc + dx1
    daft16 = dafter.astype(BF16)
    da_e = nt(daft16, out_enc)
    dae16 = da_e.astype(BF16)
    vd_e = nt(dae16, value_enc).astype(BF16)
    dse = softmax_backward(nt(vd_e, nb), soft_e, scale_e)
    dn_e = nn(dse, nb).astype(BF16)
    dq_e = nn(dn_e, key_enc).astype(BF16)
    dxl, g_gain_latent = norm_backward(nt(dq_e, query_enc), hat_l, rstd_l, gain_latent)
    g_latent = dafter + dxl

    g_key_enc = tn(dn_e, q_e)
    g_value_enc = tn(pn_e, dae16)
    wide_gains = [g_gain_latent, g_gain_enc_mlp, g_gain_self, g_gain_self_mlp, g_gain_dec_kv]
    wide = jnp.concatenate(wide_gains + [jnp.zeros((3, latent_init.shape[1]), F32)], axis=0)
    dbytes, g_table, vectors = bytes_backward(
        p_e, dse, vd_e, qk_e, nb, rstd_b, gain_bytes, codes, g_emb_out, gain_sums, wide, vocab + 1
    )

    def low(g):
        return g.astype(BF16)

    if reducer.n_items == 16:
        first_side = [(n1, [du1]), (a_e, [daft16]), (n3, [du2]), (n2, [dv_s, dk_s])]
        second_side = [
            (h1, [denc16]), (h2, [dlat16]), (a_s, [das16]), (n4, [dv_d, dk_d]), (n2, [dq_s]), (nl, [dq_e]),
        ]
        others = [
            (low(g_dec_query), "xy"), (low(dbytes), "yx"), (low(g_value_enc), "xy"), (low(g_out_dec), "yx"),
            (low(g_table), "yx"), (low(g_key_enc), "xy"), (low(g_query_dec), "yx"), (low(g_latent), "xy"),
            (low(vectors), "yx"),
        ]
        (
            r_up_enc, r_out_enc, r_up_self, r_value_self, r_key_self,
            r_down_enc, r_down_self, r_out_self, r_value_dec, r_key_dec, r_query_self, r_query_enc,
        ), (
            r_dec_query, r_position, r_value_enc, r_out_dec, r_emb, r_key_enc, r_query_dec, r_latent, r_vectors,
        ) = reduce_all((first_side, second_side), others)
    else:
        r_dec_query, r_out_dec, r_value_dec = reducer.reduce([g_dec_query, g_out_dec, tn(n4, dv_d)], order_yx)
        r_down_self, r_up_self, r_out_self = reducer.reduce(
            [tn(h2, dlat16), tn(n3, du2), tn(a_s, das16)], order_xy
        )
        r_value_self, r_down_enc = reducer.reduce([tn(n2, dv_s), tn(h1, denc16)], order_yx)
        r_up_enc, r_out_enc = reducer.reduce([tn(n1, du1), tn(a_e, daft16)], order_xy)
        r_query_dec, r_key_dec, r_query_self, r_key_self = reducer.reduce(
            [g_query_dec, tn(n4, dk_d), tn(n2, dq_s), tn(n2, dk_s)], order_xy
        )
        r_value_enc, r_latent = reducer.reduce([g_value_enc, g_latent], order_xy)
        (r_position,) = reducer.reduce([dbytes], order_yx)
        r_key_enc, r_query_enc = reducer.reduce([g_key_enc, tn(nl, dq_e)], order_yx)
        (r_emb,) = reducer.reduce([g_table], order_yx)
        (r_vectors,) = reducer.reduce([vectors], order_xy)

    plain = [
        r_position, r_key_enc, r_value_enc, r_latent, r_query_enc, r_out_enc, r_up_enc, r_down_enc,
        r_query_self, r_key_self, r_value_self, r_out_self, r_up_self, r_down_self, r_key_dec, r_value_dec,
        r_dec_query, r_query_dec, r_out_dec,
    ]
    plain, r_embedding, (r_mask, r_gain_bytes, r_gain_dec_q, r_gain_final), gains = finish(plain, r_emb, r_vectors, vocab, len(wide_gains))
    (
        r_position, r_key_enc, r_value_enc, r_latent, r_query_enc, r_out_enc, r_up_enc, r_down_enc,
        r_query_self, r_key_self, r_value_self, r_out_self, r_up_self, r_down_self, r_key_dec, r_value_dec,
        r_dec_query, r_query_dec, r_out_dec,
    ) = plain
    (
        r_gain_latent, r_gain_enc_mlp, r_gain_self, r_gain_self_mlp, r_gain_dec_kv,
    ) = gains
    return (
        logits_out, r_embedding.T, r_position, r_mask, r_gain_bytes, r_key_enc, r_value_enc,
        r_latent, r_gain_latent, r_query_enc, r_out_enc, r_gain_enc_mlp, r_up_enc, r_down_enc, r_gain_self,
        r_query_self, r_key_self, r_value_self, r_out_self, r_gain_self_mlp, r_up_self, r_down_self,
        r_gain_dec_kv, r_key_dec, r_value_dec, r_dec_query, r_gain_dec_q, r_query_dec, r_out_dec, r_gain_final,
    )


def solution(mesh):
    split = P("items", "blk")
    rows = P(("items", "blk"))
    outs = [P("items", "blk", None), P(None, ("items", "blk"))] + [rows] * 28
    return jax.shard_map(
        local,
        mesh=mesh,
        in_specs=(split, P("items", None), P("items", None)) + (P(),) * 29 + (P("items", "blk", None),),
        out_specs=tuple(outs),
        check_vma=False,
    )
```

```python
import jax
import jax.numpy as jnp
from jax import lax
from jax.experimental import pallas as pl
from jax.experimental.pallas import tpu as pltpu
from jax.sharding import PartitionSpec as P

HEADS = 8
EPS = 1e-05
F32 = jnp.float32
BF16 = jnp.bfloat16
GELU_C = 0.7978845608028654
GELU_A = 0.044715


def nn(a, b):
    return lax.dot_general(a, b, (((1,), (0,)), ((), ())), preferred_element_type=F32)


def nt(a, b):
    return lax.dot_general(a, b, (((1,), (1,)), ((), ())), preferred_element_type=F32)


def tn(a, b):
    return lax.dot_general(a, b, (((0,), (0,)), ((), ())), preferred_element_type=F32)


def norm_forward(x, gain):
    centered = x - jnp.mean(x, axis=-1, keepdims=True)
    variance = jnp.mean(centered * centered, axis=-1, keepdims=True)
    rstd = lax.rsqrt(variance + EPS)
    hat = centered * rstd
    return (hat * gain.astype(F32)).astype(BF16), hat, rstd


def norm_backward(dy, hat, rstd, gain):
    dgain = jnp.sum(dy * hat, axis=0, keepdims=True)
    dhat = dy * gain.astype(F32)
    first = jnp.mean(dhat, axis=-1, keepdims=True)
    second = jnp.mean(dhat * hat, axis=-1, keepdims=True)
    return rstd * (dhat - first - hat * second), dgain


def gelu_forward(u):
    t = jnp.tanh(GELU_C * (u + GELU_A * u * u * u))
    return (0.5 * u * (1.0 + t)).astype(BF16)


def gelu_backward(dh, u):
    t = jnp.tanh(GELU_C * (u + GELU_A * u * u * u))
    slope = 0.5 * (1.0 + t) + 0.5 * u * (1.0 - t * t) * GELU_C * (1.0 + 3.0 * GELU_A * u * u)
    return dh * slope


def softmax(s):
    e = jnp.exp(s - jnp.max(s, axis=-1, keepdims=True))
    return e / jnp.sum(e, axis=-1, keepdims=True)


def softmax_backward(dp, soft, scale):
    inner = jnp.sum(dp * soft, axis=-1, keepdims=True)
    return (soft * (dp - inner) * scale).astype(BF16)


class Reducer:
    def __init__(self):
        n_items = lax.axis_size("items")
        self.count = n_items * lax.axis_size("blk")
        self.k = n_items.bit_length() - 1
        self.n_items = n_items

    def bit(self, name):
        if name == "y":
            return lax.axis_index("blk")
        return (lax.axis_index("items") >> name) & 1

    def exchange(self, x, name):
        if name == "y":
            return lax.ppermute(x, "blk", [(0, 1), (1, 0)])
        return lax.ppermute(x, "items", [(i, i ^ (1 << name)) for i in range(self.n_items)])

    def split(self, g):
        rows, width = g.shape
        return g.astype(BF16).reshape((2,) * (self.k + 1) + (rows // self.count, width))

    def reduce(self, grads, order):
        dims = list(range(self.k - 1, -1, -1)) + ["y"]
        parts = [self.split(g) for g in grads]
        heights = [p.shape[-2] for p in parts]
        for number, name in enumerate(order):
            axis = dims.index(name)
            mine = self.bit(name)
            send = [lax.dynamic_index_in_dim(p, 1 - mine, axis, keepdims=False) for p in parts]
            keep = [lax.dynamic_index_in_dim(p, mine, axis, keepdims=False) for p in parts]
            if number == 0:
                send = [jnp.concatenate(send, axis=-2)] if len(send) > 1 else send
                keep = [jnp.concatenate(keep, axis=-2)] if len(keep) > 1 else keep
            got = self.exchange(send[0], name)
            total = keep[0].astype(F32) + got.astype(F32)
            last = number == len(order) - 1
            parts = [total if last else total.astype(BF16)]
            dims.pop(axis)
        out, at = [], 0
        for height in heights:
            out.append(parts[0][at : at + height])
            at += height
        return out


CHUNK = 256
LAG = 2
MESH = pl.DeviceIdType.MESH
STAGES = {
    "xy": ("c", "x", "y", "z0", "z1"),
    "yx": ("c", "y", "x", "z0", "z1"),
}
ITEM_BIT = {"c": 0, "x": 1, "z0": 2, "z1": 3}


def padded_rows(r):
    return -(-r // 16) * 16


def my_bit(name):
    if name == "y":
        return lax.axis_index("blk")
    return (lax.axis_index("items") // 2 ** ITEM_BIT[name]) % 2


def partner(name):
    if name == "y":
        return {"blk": 1 - lax.axis_index("blk")}
    return {"items": lax.axis_index("items") + (1 - 2 * my_bit(name)) * 2 ** ITEM_BIT[name]}


def divide(first, second, mine, r, by_rows):
    if by_rows:
        first, second = (
            jnp.concatenate([first[:r], second[:r]], axis=0),
            jnp.concatenate([first[r:], second[r:]], axis=0),
        )
    return jnp.where(mine == 0, first, second), jnp.where(mine == 0, second, first)


def tie(values, after):
    count = len(values)
    anywhere = pl.BlockSpec(memory_space=pl.ANY)
    return pl.pallas_call(
        lambda *refs: None,
        out_shape=[jax.ShapeDtypeStruct(v.shape, v.dtype) for v in values],
        in_specs=[anywhere] * (count + len(after)),
        out_specs=[anywhere] * count,
        input_output_aliases={i: i for i in range(count)},
    )(*values, *after)


class Chunk:
    def __init__(self, bufs, at, sems, r, width, order):
        self.rc, self.r1, self.r2, self.r3, self.s4, self.r4, self.out = [b.at[at] for b in bufs]
        self.send, self.recv, self.at = sems[0], sems[1], at
        self.r, self.width, self.order = r, width, order
        self.step = 256 if r <= 40 and width % 256 == 0 else 128

    def copy(self, stage, source=None):
        src, dst = (
            (source, self.rc),
            (self.rc.at[:, :, 1], self.r1),
            (self.rc.at[:, 1, 0], self.r2),
            (self.rc.at[1, 0, 0], self.r3),
            (self.s4, self.r4),
        )[stage]
        return pltpu.make_async_remote_copy(
            src_ref=dst if src is None else src,
            dst_ref=dst,
            send_sem=self.send.at[self.at, stage],
            recv_sem=self.recv.at[self.at, stage],
            device_id=partner(STAGES[self.order][stage]),
            device_id_type=MESH,
        )

    def loop(self, pairs, body):
        columns = self.width // self.step

        def run(i, carry):
            body(i // columns, pl.ds(pl.multiple_of((i % columns) * self.step, self.step), self.step))
            return carry

        lax.fori_loop(0, pairs * columns, run, 0)

    def advance(self, stage, loaded=None):
        self.copy(stage).wait_recv()
        names = STAGES[self.order]
        r, kind, rc = self.r, self.rc.dtype, self.rc
        mine = my_bit(names[stage + 1]) if stage < 4 else None

        def total(a, b):
            return a.astype(F32) + b.astype(F32)

        def stage0(p, cols):
            q, z = p // 2, p % 2
            first = total(rc[q, z, 0, :, cols], loaded[q, z, 0, :, cols])
            second = total(rc[q, z, 1, :, cols], loaded[q, z, 1, :, cols])
            keep, send = divide(first, second, mine, r, names[1] == "y")
            rc[q, z, 0, :, cols] = keep.astype(kind)
            rc[q, z, 1, :, cols] = send.astype(kind)

        def stage1(q, cols):
            first = total(rc[q, 0, 0, :, cols], self.r1[q, 0, :, cols])
            second = total(rc[q, 1, 0, :, cols], self.r1[q, 1, :, cols])
            keep, send = divide(first, second, mine, r, True)
            rc[q, 0, 0, :, cols] = keep.astype(kind)
            rc[q, 1, 0, :, cols] = send.astype(kind)

        def stage2(q, cols):
            first = total(rc[0, 0, 0, :, cols], self.r2[0, :, cols])
            second = total(rc[1, 0, 0, :, cols], self.r2[1, :, cols])
            keep, send = divide(first, second, mine, r, True)
            rc[0, 0, 0, :, cols] = keep.astype(kind)
            rc[1, 0, 0, :, cols] = send.astype(kind)

        def stage3(q, cols):
            both = total(rc[0, 0, 0, :, cols], self.r3[:, cols])
            keep = jnp.where(mine == 0, both[:r], both[r:])
            send = jnp.where(mine == 0, both[r:], both[:r])
            extra = padded_rows(r) - r
            if extra:
                send = jnp.concatenate([send, jnp.zeros((extra, send.shape[1]), F32)], axis=0)
            self.s4[:, cols] = send.astype(kind)
            self.out[:, cols] = keep

        def stage4(q, cols):
            self.out[:, cols] = self.out[:, cols] + self.r4[:, cols].astype(F32)[:r]

        self.loop((4, 2, 1, 1, 1)[stage], (stage0, stage1, stage2, stage3, stage4)[stage])
        if stage < 4:
            self.copy(stage + 1).start()


def when(condition, action):
    if isinstance(condition, bool):
        if condition:
            action()
    else:
        pl.when(condition)(action)


SLOTS = 4
AHEAD = 3
B_SLOTS = 3


def reduce_kernel(plan, *refs):
    sides, steps, n_act, n_cot, widths, others = plan
    n_a, n_o = len(widths), len(others)
    acts, refs = refs[:n_act], refs[n_act:]
    cots, refs = refs[:n_cot], refs[n_cot:]
    o_src, refs = refs[:n_o], refs[n_o:]
    a_out, o_out = refs[:n_a], refs[n_a : n_a + n_o]
    refs = refs[n_a + n_o :]
    a_bufs, refs = refs[:7], refs[7:]
    act_in, act_t, cot_in, made = refs[:4]
    refs = refs[4:]
    o_bufs, refs = [refs[8 * i : 8 * i + 8] for i in range(n_o)], refs[8 * n_o :]
    a_sems, o_sems = refs[0:2], refs[2:4]
    act_sem, cot_sem, o_load_sem, a_out_sem, o_out_sem = refs[4:]
    core = my_bit("c")
    rows = act_t.shape[1] // 4

    barrier = pltpu.get_barrier_semaphore()
    for name in ("c", "x", "y", "z0", "z1"):
        pl.semaphore_signal(barrier, inc=1, device_id=partner(name), device_id_type=MESH)
    pl.semaphore_wait(barrier, 5)

    def chunk(step, side):
        return Chunk(a_bufs, 2 * step + side, a_sems, 40, CHUNK, ("xy", "yx")[side])

    def act_copy(side, group):
        return pltpu.make_async_copy(acts[sides[side][0][group][1]], act_in.at[side], act_sem.at[side])

    def cot_copy(side, step):
        source, number, _ = sides[side][1][step]
        slot = step % B_SLOTS
        return pltpu.make_async_copy(
            cots[source].at[:, pl.ds(number * CHUNK, CHUNK)], cot_in.at[side, slot], cot_sem.at[side, slot]
        )

    def first_copy(step, side):
        return chunk(step, side).copy(0, made.at[side, step % SLOTS, 1 - core])

    def produce(step):
        for side in range(2):
            groups = sides[side][0]
            for g, (start, _) in enumerate(groups):

                def fresh(g=g, side=side, groups=groups):
                    act_copy(side, g).wait()

                    def turn(i, carry):
                        at = pl.ds(pl.multiple_of(i * 256, 256), 256)
                        act_t[side, at, :] = act_in[side, :, at].T
                        return carry

                    lax.fori_loop(0, act_in.shape[2] // 256, turn, 0)
                    if g + 1 < len(groups):
                        act_copy(side, g + 1).start()

                when(step == start, fresh)
            for later in range(B_SLOTS - 1, steps):
                when(step == later - (B_SLOTS - 1), lambda later=later, side=side: cot_copy(side, later).start())
            slot = step % B_SLOTS
            pltpu.make_async_copy(
                cots[0].at[:, pl.ds(0, CHUNK)], cot_in.at[side, slot], cot_sem.at[side, slot]
            ).wait()
            when(step >= SLOTS, lambda side=side: first_copy(step - SLOTS, side).wait_send())

            def product(i, carry, side=side, slot=slot):
                part = act_t[side, pl.ds(pl.multiple_of(i * rows, rows), rows), :]
                result = jnp.dot(part, cot_in[side, slot], preferred_element_type=F32)
                height = rows // 4
                for x in range(2):
                    for c in range(2):
                        at = (2 * x + c) * height
                        made[side, step % SLOTS, c, i // 2, i % 2, x] = result[at : at + height].astype(BF16)
                return carry

            lax.fori_loop(0, 4, product, 0)
            first_copy(step, side).start()

    small = []
    for i, (r, width, order) in enumerate(others):
        item = Chunk([b.at[0:1] for b in o_bufs[i][:7]], 0, o_sems, r, width, order)
        item.at = i
        small.append(item)
        item.copy(0, o_src[i].at[:, :, :, 1 - core]).start()
        pltpu.make_async_copy(o_src[i].at[:, :, :, core], o_bufs[i][7], o_load_sem.at[i]).start()
    for side in range(2):
        act_copy(side, 0).start()
        for step in range(B_SLOTS - 1):
            cot_copy(side, step).start()

    def begin(step, carry):
        produce(step)
        return carry

    lax.fori_loop(0, AHEAD, begin, 0)
    for i, item in enumerate(small):
        pltpu.make_async_copy(o_src[i].at[:, :, :, core], o_bufs[i][7], o_load_sem.at[i]).wait()
        item.advance(0, o_bufs[i][7])

    def run(step, carry):
        pl.when(step + AHEAD < steps)(lambda: produce(step + AHEAD))

        def enter():
            for side in range(2):
                chunk(step, side).advance(0, made.at[side, step % SLOTS, core])

        pl.when(step < steps)(enter)
        for stage in range(4, 0, -1):
            old = step - stage * LAG

            def act(old=old, stage=stage):
                for side in range(2):
                    chunk(old, side).advance(stage)

            pl.when(jnp.logical_and(old >= 0, old < steps))(act)
        for number in range(4):

            def others_on(number=number):
                for item in small:
                    item.advance(number + 1)

            pl.when(step == 4 + 5 * number)(others_on)
        return carry

    lax.fori_loop(0, steps + 4 * LAG, run, 0)

    outs = []
    for side in range(2):
        for step in range(steps):
            _, number, target = sides[side][1][step]
            at = 2 * step + side
            outs.append(
                pltpu.make_async_copy(
                    a_bufs[6].at[at], a_out[target].at[:, pl.ds(number * CHUNK, CHUNK)], a_out_sem.at[at]
                )
            )
    for i in range(n_o):
        outs.append(pltpu.make_async_copy(o_bufs[i][6].at[0], o_out[i], o_out_sem.at[i]))
    for copy in outs:
        copy.start()
    for step in range(steps - SLOTS, steps):
        for side in range(2):
            first_copy(step, side).wait_send()
    for i, item in enumerate(small):
        item.copy(0, o_src[i].at[:, :, :, 1 - core]).wait_send()
        for stage in range(1, 5):
            item.copy(stage).wait_send()

    def wait_sent(step, carry):
        for side in range(2):
            for stage in range(1, 5):
                chunk(step, side).copy(stage).wait_send()
        return carry

    lax.fori_loop(0, steps, wait_sent, 0)
    for copy in outs:
        copy.wait()


def buffers(count, r, width, kind):
    rp = padded_rows(r)
    return [
        pltpu.VMEM((count, 2, 2, 2, 2 * r, width), kind),
        pltpu.VMEM((count, 2, 2, 2 * r, width), kind),
        pltpu.VMEM((count, 2, 2 * r, width), kind),
        pltpu.VMEM((count, 2 * r, width), kind),
        pltpu.VMEM((count, rp, width), kind),
        pltpu.VMEM((count, rp, width), kind),
        pltpu.VMEM((count, r, width), F32),
    ]


def reduce_all(products, others):
    acts, cots, sides, widths = [], [], [], []
    for side in products:
        groups, sequence = [], []
        for act, own in side:
            groups.append((len(sequence), len(acts)))
            acts.append(act)
            for cot in own:
                for number in range(cot.shape[1] // CHUNK):
                    sequence.append((len(cots), number, len(widths)))
                cots.append(cot)
                widths.append(cot.shape[1])
        sides.append((tuple(groups), tuple(sequence)))
    steps = len(sides[0][1])
    assert steps == len(sides[1][1])

    def view(g):
        return g.reshape(2, 2, 2, 2, g.shape[0] // 16, g.shape[1])

    plan = (
        tuple(sides), steps, len(acts), len(cots), tuple(widths),
        tuple((g.shape[0] // 32, g.shape[1], order) for g, order in others),
    )
    depth, features = acts[0].shape
    scratch = buffers(2 * steps, 40, CHUNK, BF16)
    scratch += [
        pltpu.VMEM((2, depth, features), BF16),
        pltpu.VMEM((2, features, depth), BF16),
        pltpu.VMEM((2, B_SLOTS, depth, CHUNK), BF16),
        pltpu.VMEM((2, SLOTS, 2, 2, 2, 2, 80, CHUNK), BF16),
    ]
    for g, order in others:
        r = g.shape[0] // 32
        scratch += buffers(1, r, g.shape[1], g.dtype)
        scratch.append(pltpu.VMEM((2, 2, 2, 2 * r, g.shape[1]), g.dtype))
    dma = pltpu.SemaphoreType.DMA
    scratch += [dma((2 * steps, 5)), dma((2 * steps, 5)), dma((len(others), 5)), dma((len(others), 5))]
    scratch += [dma((2,)), dma((2, B_SLOTS)), dma((len(others),)), dma((2 * steps,)), dma((len(others),))]
    anywhere = pl.BlockSpec(memory_space=pl.ANY)
    arrays = acts + cots + [view(g) for g, order in others]
    results = pl.pallas_call(
        lambda *refs: reduce_kernel(plan, *refs),
        out_shape=[jax.ShapeDtypeStruct((features // 32, w), F32) for w in widths]
        + [jax.ShapeDtypeStruct((g.shape[0] // 32, g.shape[1]), F32) for g, order in others],
        in_specs=[anywhere] * len(arrays),
        out_specs=[anywhere] * (len(widths) + len(others)),
        scratch_shapes=scratch,
        compiler_params=pltpu.CompilerParams(
            collective_id=0, has_side_effects=True, vmem_limit_bytes=62 * 1024 * 1024
        ),
    )(*arrays)
    return results[: len(widths)], results[len(widths) :]


def finish(plain, table, vectors, vocab, vector_count):
    count = len(plain)
    width = table.shape[0]

    def kernel(*refs):
        sources, refs = refs[:count], refs[count:]
        table_ref, vectors_ref = refs[:2]
        refs = refs[2:]
        targets, refs = refs[:count], refs[count:]
        emb_ref, row_refs, refs = refs[0], refs[1:5], refs[5:]
        gain_refs, refs = refs[:vector_count], refs[vector_count:]
        staged, (in_sem, out_sem) = refs[:count], refs[count:]
        inward = [pltpu.make_async_copy(sources[i], staged[i], in_sem.at[i]) for i in range(count)]
        outward = [pltpu.make_async_copy(staged[i], targets[i], out_sem.at[i]) for i in range(count)]
        for copy in inward:
            copy.start()
        turned = table_ref[...].T
        emb_ref[...] = table_ref[:, :vocab]
        vector_rows = vectors_ref[...].T
        for i, row_ref in enumerate(row_refs):
            row_ref[...] = turned[vocab + i]
        for i, gain_ref in enumerate(gain_refs):
            gain_ref[...] = vector_rows[i]
        for i in range(count):
            inward[i].wait()
            outward[i].start()
        for copy in outward:
            copy.wait()

    anywhere = pl.BlockSpec(memory_space=pl.ANY)
    local_memory = pl.BlockSpec(memory_space=pltpu.VMEM)
    shapes = [jax.ShapeDtypeStruct(p.shape, F32) for p in plain]
    shapes += [jax.ShapeDtypeStruct((width, vocab), F32)] + [jax.ShapeDtypeStruct((width,), F32)] * 4
    shapes += [jax.ShapeDtypeStruct(vectors.shape[:1], F32)] * vector_count
    results = pl.pallas_call(
        kernel,
        out_shape=shapes,
        in_specs=[anywhere] * count + [local_memory] * 2,
        out_specs=[anywhere] * count + [local_memory] * (5 + vector_count),
        scratch_shapes=[pltpu.VMEM(p.shape, F32) for p in plain] + [pltpu.SemaphoreType.DMA((count,))] * 2,
    )(*plain, table, vectors)
    return results[:count], results[count], results[count + 1 : count + 5], results[count + 5 :]


def center(x):
    hat = x - jnp.mean(x, axis=-1, keepdims=True)
    rstd = lax.rsqrt(jnp.mean(hat * hat, axis=-1, keepdims=True) + EPS)
    return hat * rstd, rstd


def center_backward(dhat, hat, rstd):
    first = jnp.mean(dhat, axis=-1, keepdims=True)
    second = jnp.mean(dhat * hat, axis=-1, keepdims=True)
    return rstd * (dhat - first - hat * second)


def decoder_kernel(
    scale, query, cot, emb, key, value, w_query, w_out, gain_q, gain_f,
    logits, dquery, g_emb, g_gains, dkey, dvalue, g_query, g_out,
    g_pd, g_dn, kq, vo, vo_mid,
):
    @pl.when(pl.program_id(0) == 0)
    def _():
        for ref in (g_emb, g_pd, g_dn, g_gains):
            ref[...] = jnp.zeros_like(ref)
        kq[...] = nt(key[...], w_query[...]).astype(BF16)
        out = nn(value[...], w_out[...])
        vo[...] = out.astype(BF16)
        vo_mid[...] = (out - jnp.mean(out, axis=0, keepdims=True)).astype(BF16)

    x = query[...].astype(F32)
    hat_q, rstd_q = center(x)
    gq, gf = gain_q[...].astype(F32), gain_f[...].astype(F32)
    nq = (hat_q * gq).astype(BF16)
    soft = softmax(nt(nq, kq[...]) * scale)
    p = soft.astype(BF16)
    hat_f, rstd_f = center(x + nn(p, vo[...]))
    nf = (hat_f * gf).astype(BF16)
    logits[...] = nt(emb[...], nf).astype(BF16)
    dnf = nn(cot[...].T, emb[...])
    g_emb[...] += nn(cot[...], nf)
    g_gains[0:1] += jnp.sum(dnf * hat_f, axis=0, keepdims=True)
    ddec = center_backward(dnf * gf, hat_f, rstd_f)
    ddec16 = ddec.astype(BF16)
    g_pd[...] += nn(p.T, ddec16)
    ds = softmax_backward(nt(ddec16, vo_mid[...]), soft, scale)
    g_dn[...] += nn(ds.T, nq)
    dnq = nn(ds, kq[...])
    g_gains[1:2] += jnp.sum(dnq * hat_q, axis=0, keepdims=True)
    dquery[...] = (ddec + center_backward(dnq * gq, hat_q, rstd_q)).astype(BF16)

    @pl.when(pl.program_id(0) == pl.num_programs(0) - 1)
    def _():
        pd, dn = g_pd[...].astype(BF16), g_dn[...].astype(BF16)
        dvalue[...] = nt(pd, w_out[...]).astype(BF16)
        dkey[...] = nn(dn, w_query[...]).astype(BF16)
        g_out[...] = nn(value[...].T, pd).astype(BF16)
        g_query[...] = nn(dn.T, key[...]).astype(BF16)


def decoder_pass(query, cot, emb, key, value, w_query, w_out, gain_q, gain_f, scale):
    rows, width = query.shape
    vocab, latents, block = emb.shape[0], key.shape[0], 512

    def whole(x):
        return pl.BlockSpec(x.shape, lambda i: (0, 0))

    sums = jax.ShapeDtypeStruct((latents, width), F32)
    shapes = [
        jax.ShapeDtypeStruct((vocab, rows), BF16),
        jax.ShapeDtypeStruct((rows, width), BF16),
        jax.ShapeDtypeStruct((vocab, width), F32),
        jax.ShapeDtypeStruct((8, width), F32),
    ] + [jax.ShapeDtypeStruct(x.shape, BF16) for x in (key, value, w_query, w_out)]
    small = (gain_q[None, :], gain_f[None, :])
    return pl.pallas_call(
        lambda *refs: decoder_kernel(scale, *refs),
        grid=(rows // block,),
        out_shape=shapes,
        in_specs=[
            pl.BlockSpec((block, width), lambda i: (i, 0)),
            pl.BlockSpec((vocab, block), lambda i: (0, i)),
        ]
        + [whole(x) for x in (emb, key, value, w_query, w_out) + small],
        out_specs=[
            pl.BlockSpec((vocab, block), lambda i: (0, i)),
            pl.BlockSpec((block, width), lambda i: (i, 0)),
        ]
        + [whole(x) for x in shapes[2:]],
        scratch_shapes=[pltpu.VMEM(sums.shape, F32)] * 2 + [pltpu.VMEM(sums.shape, BF16)] * 3,
        compiler_params=pltpu.CompilerParams(vmem_limit_bytes=56 * 1024 * 1024),
    )(query, cot, emb, key, value, w_query, w_out, *small)


def bytes_kernel(
    at, scale, p, soft, vd, qk, nb, rstd, gain, codes, emb, sums, wide,
    pn, q, dae, daft, nl, rstd_l, gain_l, w_key, w_query,
    dbytes, table, turned, dq, g_key, g_value, g_latent,
    total, ds,
):
    i = pl.program_id(0)
    block = codes.shape[1]

    @pl.when(i == 0)
    def _():
        total[...] = jnp.zeros_like(total)
        total[: emb.shape[0]] = emb[...]
        total[at + 1 : at + 2] = sums[1:2]
        total[at + 2 : at + 3] = sums[0:1]
        ds[...] = softmax_backward(nt(vd[...], nb[...]), soft[...], scale)
        dn = nn(ds[...], nb[...]).astype(BF16)
        g_key[...] = nn(dn.T, q[...]).astype(BF16)
        g_value[...] = nn(pn[...].T, dae[...]).astype(BF16)
        dq[...] = nn(dn, w_key[...]).astype(BF16)
        dnl = nt(dq[...], w_query[...])
        g = gain_l[...].astype(F32)
        hat = nl[...].astype(F32) / g
        g_latent[...] = (daft[...] + center_backward(dnl * g, hat, rstd_l[...])).astype(BF16)
        first = jnp.sum(dnl * hat, axis=0, keepdims=True)
        own = lax.broadcasted_iota(jnp.int32, wide.shape, 0) == 0
        turned[...] = jnp.zeros_like(turned)
        turned[:, : wide.shape[0]] = jnp.where(own, first, wide[...]).T.astype(BF16)

    rows = pl.ds(pl.multiple_of(i * block, block), block)
    g = gain[...].astype(F32)
    normed = nb[rows, :]
    dnb = nn(p[...].T, vd[...]) + nn(ds[:, rows].T, qk[...])
    hat = normed.astype(F32) / g
    dx = center_backward(dnb * g, hat, rstd[...]).astype(BF16)
    dbytes[...] = dx
    entry = lax.broadcasted_iota(jnp.int32, (total.shape[0], block), 0)
    onehot = (entry == codes[...]).astype(BF16)
    total[...] += nn(onehot, dx)
    total[at : at + 1] += jnp.sum(dnb * hat, axis=0, keepdims=True)

    @pl.when(i == pl.num_programs(0) - 1)
    def _():
        table[...] = total[...].T.astype(BF16)


def bytes_backward(at, scale, p, soft, vd, qk, nb, rstd, gain, codes, emb, sums, wide, rest):
    rows, width = nb.shape
    latents, block, entries = p.shape[0], 256, -(-emb.shape[0] // 128) * 128
    features = wide.shape[1]
    qk_width = rest[1].shape[1]

    def whole(x):
        return pl.BlockSpec(x.shape, lambda i: (0, 0))

    shapes = [
        jax.ShapeDtypeStruct((rows, width), BF16),
        jax.ShapeDtypeStruct((width, entries), BF16),
        jax.ShapeDtypeStruct((features, 128), BF16),
        jax.ShapeDtypeStruct((latents, qk_width), BF16),
        jax.ShapeDtypeStruct((width, qk_width), BF16),
        jax.ShapeDtypeStruct((width, features), BF16),
        jax.ShapeDtypeStruct((latents, features), BF16),
    ]
    arrays = (p, soft, vd, qk, nb, rstd, gain[None, :], codes[None, :], emb, sums, wide) + rest
    specs = [whole(x) for x in arrays]
    specs[0] = pl.BlockSpec((latents, block), lambda i: (0, i))
    specs[5] = pl.BlockSpec((block, 1), lambda i: (i, 0))
    specs[7] = pl.BlockSpec((1, block), lambda i: (0, i))
    return pl.pallas_call(
        lambda *refs: bytes_kernel(at, scale, *refs),
        grid=(rows // block,),
        out_shape=shapes,
        in_specs=specs,
        out_specs=[pl.BlockSpec((block, width), lambda i: (i, 0))] + [whole(x) for x in shapes[1:]],
        scratch_shapes=[pltpu.VMEM((entries, width), F32), pltpu.VMEM((latents, rows), BF16)],
        compiler_params=pltpu.CompilerParams(vmem_limit_bytes=60 * 1024 * 1024),
    )(*arrays)


def head_columns(head, width):
    each = width // HEADS
    low, high = head * each // 128 * 128, -(-(head + 1) * each // 128) * 128
    place = low + lax.broadcasted_iota(jnp.int32, (1, high - low), 1)
    return slice(low, high), jnp.logical_and(place >= head * each, place < (head + 1) * each)


def pick(mask, x):
    return jnp.where(mask, x, jnp.zeros_like(x))


def head_softmax(head, q, k):
    columns, mask = head_columns(head, q.shape[1])
    scale = (q.shape[1] // HEADS) ** (-0.5)
    return softmax(nt(pick(mask, q[:, columns]), k[:, columns]) * scale), scale


def self_forward_heads(q, k, v, total):
    total[...] = jnp.zeros_like(total)
    for head in range(HEADS):
        p = head_softmax(head, q, k)[0].astype(BF16)
        columns, mask = head_columns(head, v.shape[1])
        total[:, columns] += nn(p, pick(mask, v[:, columns]))


def self_backward_heads(q, k, v, da, dq_sum, dk_sum, dv_sum):
    for ref in (dq_sum, dk_sum, dv_sum):
        ref[...] = jnp.zeros_like(ref)
    for head in range(HEADS):
        soft, scale = head_softmax(head, q, k)
        columns, mask = head_columns(head, v.shape[1])
        da_head = pick(mask, da[:, columns])
        ds = softmax_backward(nt(da_head, v[:, columns]), soft, scale)
        dv_sum[:, columns] += nn(soft.astype(BF16).T, da_head)
        columns, mask = head_columns(head, q.shape[1])
        dq_sum[:, columns] += nn(ds, pick(mask, k[:, columns]))
        dk_sum[:, columns] += nn(ds.T, pick(mask, q[:, columns]))


class Stream:
    def __init__(self, sources, targets, sem):
        self.copies = [pltpu.make_async_copy(a, b, sem.at[i]) for i, (a, b) in enumerate(zip(sources, targets))]
        self.targets, self.arrived = targets, set()
        for copy in self.copies:
            copy.start()

    def __getitem__(self, i):
        if i not in self.arrived:
            self.copies[i].wait()
            self.arrived.add(i)
        return self.targets[i][...]


class Results:
    def __init__(self, stage, targets, sem):
        self.stage, self.targets, self.sem, self.copies = stage, targets, sem, []

    def put(self, value):
        i = len(self.copies)
        self.stage[i][...] = value.astype(self.stage[i].dtype)
        copy = pltpu.make_async_copy(self.stage[i], self.targets[i], self.sem.at[i])
        copy.start()
        self.copies.append(copy)
        return self.stage[i]

    def finish(self):
        for copy in self.copies:
            copy.wait()


def streamed(body, small, large, shapes, extra):
    n_s, n_l, n_o = len(small), len(large), len(shapes)

    def kernel(*refs):
        ins, refs = refs[: n_s + n_l], refs[n_s + n_l :]
        outs, refs = refs[:n_o], refs[n_o:]
        held, refs = refs[:n_l], refs[n_l:]
        stage, refs = refs[:n_o], refs[n_o:]
        stream = Stream(ins[n_s:], held, refs[0])
        results = Results(stage, outs, refs[1])
        body(ins[:n_s], stream, results, refs[2:])
        results.finish()

    anywhere = pl.BlockSpec(memory_space=pl.ANY)
    return pl.pallas_call(
        kernel,
        out_shape=shapes,
        in_specs=[pl.BlockSpec(memory_space=pltpu.VMEM)] * n_s + [anywhere] * n_l,
        out_specs=[anywhere] * n_o,
        scratch_shapes=[pltpu.VMEM(x.shape, x.dtype) for x in large]
        + [pltpu.VMEM(x.shape, x.dtype) for x in shapes]
        + [pltpu.SemaphoreType.DMA((n_l,)), pltpu.SemaphoreType.DMA((n_o,))]
        + extra,
        compiler_params=pltpu.CompilerParams(vmem_limit_bytes=60 * 1024 * 1024),
    )(*small, *large)


def spread(column):
    return jnp.broadcast_to(column, (column.shape[0], 128))


def latent_forward(latent, pn, gains, weights):
    rows, width = latent.shape
    wide, narrow = (rows, width), (rows, weights[4].shape[1])

    def body(small, w, results, extra):
        latent_ref, pn_ref, g1, g2, g3, g4 = small
        (total,) = extra
        put = results.put

        def norm(x, gain):
            hat, rstd = center(x)
            return put(hat * gain[...].astype(F32)), rstd

        a_e = put(nn(pn_ref[...], w[0]))
        x = latent_ref[...].astype(F32) + nn(a_e[...], w[1])
        n1, r1 = norm(x, g1)
        u1 = put(nn(n1[...], w[2]))
        h1 = put(gelu_forward(u1[...]))
        x = x + nn(h1[...], w[3])
        n2, r2 = norm(x, g2)
        q, k, v = put(nn(n2[...], w[4])), put(nn(n2[...], w[5])), put(nn(n2[...], w[6]))
        self_forward_heads(q, k, v, total)
        a_s = put(total[...])
        x = x + nn(a_s[...], w[7])
        n3, r3 = norm(x, g3)
        u2 = put(nn(n3[...], w[8]))
        h2 = put(gelu_forward(u2[...]))
        x = x + nn(h2[...], w[9])
        n4, r4 = norm(x, g4)
        put(nn(n4[...], w[10]))
        put(nn(n4[...], w[11]))
        for r in (r1, r2, r3, r4):
            put(spread(r))

    def low(shape):
        return jax.ShapeDtypeStruct(shape, BF16)

    full = jax.ShapeDtypeStruct(wide, F32)
    shapes = [low(wide), low(wide), full, low(wide), low(wide), low(narrow), low(narrow), low(wide)]
    shapes += [low(wide), low(wide), full, low(wide), low(wide)]
    shapes += [low((rows, weights[10].shape[1])), low((rows, weights[11].shape[1]))]
    shapes += [jax.ShapeDtypeStruct((rows, 128), F32)] * 4
    small = [latent, pn] + [g[None, :] for g in gains]
    return streamed(body, small, weights, shapes, [pltpu.VMEM(wide, F32)])


def latent_backward(dk_d, dv_d, gains, kept, weights):
    rows, width = kept[0].shape
    count = len(weights)

    def body(small, stream, results, extra):
        dk_ref, dv_ref, g1, g2, g3, g4 = small
        dq_sum, dk_sum, dv_sum, sums = extra
        put = results.put
        w = stream
        sums[...] = jnp.zeros_like(sums)

        def norm(dy, normed, rstd, gain, row):
            g = gain[...].astype(F32)
            hat = normed.astype(F32) / g
            sums[row : row + 1] = jnp.sum(dy * hat, axis=0, keepdims=True)
            return center_backward(dy * g, hat, rstd[:, :1])

        n4, u2, n3, q, k, v, n2, u1, n1, r4, r3, r2, r1 = range(count, count + 13)
        dlat = norm(nt(dk_ref[...], w[0]) + nt(dv_ref[...], w[1]), w[n4], w[r4], g4, 4)
        dlat16 = put(dlat)
        du2 = put(gelu_backward(nt(dlat16[...], w[2]), w[u2]))
        das = dlat + norm(nt(du2[...], w[3]), w[n3], w[r3], g3, 3)
        das16 = put(das)
        da = nt(das16[...], w[4]).astype(BF16)
        w[q], w[k], w[v]
        self_backward_heads(w.targets[q], w.targets[k], w.targets[v], da, dq_sum, dk_sum, dv_sum)
        dq, dk, dv = put(dq_sum[...]), put(dk_sum[...]), put(dv_sum[...])
        dn2 = nt(dq[...], w[5]) + nt(dk[...], w[6]) + nt(dv[...], w[7])
        denc = das + norm(dn2, w[n2], w[r2], g2, 2)
        denc16 = put(denc)
        du1 = put(gelu_backward(nt(denc16[...], w[8]), w[u1]))
        daft = denc + norm(nt(du1[...], w[9]), w[n1], w[r1], g1, 1)
        daft16 = put(daft)
        put(daft)
        dae = put(nt(daft16[...], w[10]))
        put(nt(dae[...], w[11]))
        put(sums[...])

    wide = (rows, width)
    low, narrow = jax.ShapeDtypeStruct(wide, BF16), jax.ShapeDtypeStruct(kept[3].shape, BF16)
    shapes = [low, low, low, narrow, narrow, low, low, low, low, jax.ShapeDtypeStruct(wide, F32), low]
    shapes += [jax.ShapeDtypeStruct((rows, weights[11].shape[0]), BF16), jax.ShapeDtypeStruct((8, width), F32)]
    extra = [pltpu.VMEM(x.shape, F32) for x in kept[3:6]] + [pltpu.VMEM((8, width), F32)]
    large = list(weights) + list(kept)
    order = [0, 1, count, count + 9, 2, count + 1, 3, count + 2, count + 10, 4, count + 3, count + 4, count + 5]
    order += [5, 6, 7, count + 6, count + 11, 8, count + 7, 9, count + 8, count + 12, 10, 11]
    place = {old: new for new, old in enumerate(order)}

    class Ordered:
        def __init__(self, stream):
            self.stream, self.targets = stream, {old: stream.targets[new] for old, new in place.items()}

        def __getitem__(self, i):
            return self.stream[place[i]]

    small = [dk_d, dv_d] + [g[None, :] for g in gains]
    return streamed(
        lambda a, b, c, d: body(a, Ordered(b), c, d), small, [large[i] for i in order], shapes, extra
    )


def local(
    byte_ids, span_start, span_len, embedding, position, mask_vector, gain_bytes, key_enc,
    value_enc, latent_init, gain_latent, query_enc, out_enc, gain_enc_mlp, up_enc, down_enc,
    gain_self, query_self, key_self, value_self, out_self, gain_self_mlp, up_self, down_self,
    gain_dec_kv, key_dec, value_dec, dec_query, gain_dec_q, query_dec, out_dec, gain_final,
    logit_cot,
):
    me = lax.axis_index("blk")
    half = byte_ids.shape[1]
    total = position.shape[0]
    vocab = embedding.shape[0]
    reducer = Reducer()
    k = reducer.k
    order_yx = [0, "y", 1] + list(range(2, k))
    order_xy = [0, 1, "y"] + list(range(2, k))

    def swap(x):
        return lax.ppermute(x, "blk", [(0, 1), (1, 0)])

    def own_item(first, second, after=()):
        mine = jnp.where(me == 0, first, second)
        send = jnp.where(me == 0, second, first)
        if after:
            (send,) = tie([send], after)
        got = swap(send)
        low_half = jnp.where(me == 0, mine, got)
        high_half = jnp.where(me == 0, got, mine)
        return jnp.concatenate([low_half, high_half], axis=-1)

    ids = own_item(byte_ids[0], byte_ids[1])
    cot_rows = logit_cot.transpose(2, 0, 1)
    cot = own_item(cot_rows[:, 0], cot_rows[:, 1], [ids])
    entries = -(-(vocab + 4) // 16) * 16
    cot = jnp.pad(cot, ((0, entries - vocab), (0, 0)))
    emb_rows = jnp.pad(embedding, ((0, entries - vocab), (0, 0)))
    starts = lax.dynamic_index_in_dim(span_start, me, 0, keepdims=False)
    lengths = lax.dynamic_index_in_dim(span_len, me, 0, keepdims=False)

    places = lax.iota(jnp.int32, total)
    inside = (places[None, :] >= starts[:, None]) & (places[None, :] < (starts + lengths)[:, None])
    codes = jnp.where(jnp.any(inside, axis=0), vocab, ids)
    padded = -(-(vocab + 4) // 128) * 128
    table = jnp.concatenate(
        [embedding, mask_vector[None, :], jnp.zeros((padded - vocab - 1, embedding.shape[1]), BF16)], axis=0
    )
    onehot = (codes[:, None] == lax.iota(jnp.int32, padded)[None, :]).astype(BF16)
    bytes_in = nn(onehot, table) + position.astype(F32)
    nb, hat_b, rstd_b = norm_forward(bytes_in, gain_bytes)

    latent32 = latent_init.astype(F32)
    nl, hat_l, rstd_l = norm_forward(latent32, gain_latent)
    q_e = nn(nl, query_enc).astype(BF16)
    scale_e = q_e.shape[1] ** (-0.5)
    qk_e = nt(q_e, key_enc).astype(BF16)
    soft_e = softmax(nt(qk_e, nb) * scale_e)
    p_e = soft_e.astype(BF16)
    pn_e = nn(p_e, nb).astype(BF16)
    gains = (gain_enc_mlp, gain_self, gain_self_mlp, gain_dec_kv)
    (
        a_e, n1, u1, h1, n2, q_s, k_s, v_s, a_s, n3, u2, h2, n4, k_d, v_d, rstd1, rstd2, rstd3, rstd4,
    ) = latent_forward(
        latent_init, pn_e, gains,
        [
            value_enc, out_enc, up_enc, down_enc, query_self, key_self, value_self, out_self, up_self,
            down_self, key_dec, value_dec,
        ],
    )

    scale_d = k_d.shape[1] ** (-0.5)
    logits, g_dec_query, g_emb_out, gain_sums, dk_d, dv_d, g_query_dec, g_out_dec = decoder_pass(
        dec_query, cot, emb_rows, k_d, v_d, query_dec, out_dec, gain_dec_q, gain_final, scale_d
    )
    logits = logits[:vocab]
    logits_got = swap(jnp.where(me == 0, logits[:, half:], logits[:, :half]))
    logits_own = jnp.where(me == 0, logits[:, :half], logits[:, half:])
    side = lax.broadcasted_iota(jnp.int32, (1, 2, 1), 1)
    logits_out = jnp.where(side == me, logits_own[:, None, :], logits_got[:, None, :]).transpose(1, 2, 0)

    dlat16, du2, das16, dq_s, dk_s, dv_s, denc16, du1, daft16, dafter, dae16, vd_e, wide = latent_backward(
        dk_d, dv_d, gains, [n4, u2, n3, q_s, k_s, v_s, n2, u1, n1, rstd4, rstd3, rstd2, rstd1],
        [
            key_dec, value_dec, down_self, up_self, out_self, query_self, key_self, value_self, down_enc,
            up_enc, out_enc, value_enc,
        ],
    )

    dbytes, g_table, vectors, dq_e, g_key_enc, g_value_enc, g_latent = bytes_backward(
        vocab + 1, scale_e, p_e, soft_e, vd_e, qk_e, nb, rstd_b, gain_bytes, codes, g_emb_out, gain_sums, wide,
        (pn_e, q_e, dae16, dafter, nl, rstd_l, gain_latent[None, :], key_enc, query_enc),
    )

    def low(g):
        return g.astype(BF16)

    if reducer.n_items == 16:
        first_side = [(n1, [du1]), (a_e, [daft16]), (n3, [du2]), (n2, [dv_s, dk_s])]
        second_side = [
            (h1, [denc16]), (h2, [dlat16]), (a_s, [das16]), (n4, [dv_d, dk_d]), (n2, [dq_s]), (nl, [dq_e]),
        ]
        others = [
            (low(g_dec_query), "xy"), (low(dbytes), "yx"), (low(g_value_enc), "xy"), (low(g_out_dec), "yx"),
            (low(g_table), "yx"), (low(g_key_enc), "xy"), (low(g_query_dec), "yx"), (low(g_latent), "xy"),
            (low(vectors), "yx"),
        ]
        (
            r_up_enc, r_out_enc, r_up_self, r_value_self, r_key_self,
            r_down_enc, r_down_self, r_out_self, r_value_dec, r_key_dec, r_query_self, r_query_enc,
        ), (
            r_dec_query, r_position, r_value_enc, r_out_dec, r_emb, r_key_enc, r_query_dec, r_latent, r_vectors,
        ) = reduce_all((first_side, second_side), others)
    else:
        r_dec_query, r_out_dec, r_value_dec = reducer.reduce([g_dec_query, g_out_dec, tn(n4, dv_d)], order_yx)
        r_down_self, r_up_self, r_out_self = reducer.reduce(
            [tn(h2, dlat16), tn(n3, du2), tn(a_s, das16)], order_xy
        )
        r_value_self, r_down_enc = reducer.reduce([tn(n2, dv_s), tn(h1, denc16)], order_yx)
        r_up_enc, r_out_enc = reducer.reduce([tn(n1, du1), tn(a_e, daft16)], order_xy)
        r_query_dec, r_key_dec, r_query_self, r_key_self = reducer.reduce(
            [g_query_dec, tn(n4, dk_d), tn(n2, dq_s), tn(n2, dk_s)], order_xy
        )
        r_value_enc, r_latent = reducer.reduce([g_value_enc, g_latent], order_xy)
        (r_position,) = reducer.reduce([dbytes], order_yx)
        r_key_enc, r_query_enc = reducer.reduce([g_key_enc, tn(nl, dq_e)], order_yx)
        (r_emb,) = reducer.reduce([g_table], order_yx)
        (r_vectors,) = reducer.reduce([vectors], order_xy)

    plain = [
        r_position, r_key_enc, r_value_enc, r_latent, r_query_enc, r_out_enc, r_up_enc, r_down_enc,
        r_query_self, r_key_self, r_value_self, r_out_self, r_up_self, r_down_self, r_key_dec, r_value_dec,
        r_dec_query, r_query_dec, r_out_dec,
    ]
    plain, r_embedding, (r_mask, r_gain_bytes, r_gain_dec_q, r_gain_final), gains = finish(plain, r_emb, r_vectors, vocab, 1 + len(gains))
    (
        r_position, r_key_enc, r_value_enc, r_latent, r_query_enc, r_out_enc, r_up_enc, r_down_enc,
        r_query_self, r_key_self, r_value_self, r_out_self, r_up_self, r_down_self, r_key_dec, r_value_dec,
        r_dec_query, r_query_dec, r_out_dec,
    ) = plain
    (
        r_gain_latent, r_gain_enc_mlp, r_gain_self, r_gain_self_mlp, r_gain_dec_kv,
    ) = gains
    return (
        logits_out, r_embedding.T, r_position, r_mask, r_gain_bytes, r_key_enc, r_value_enc,
        r_latent, r_gain_latent, r_query_enc, r_out_enc, r_gain_enc_mlp, r_up_enc, r_down_enc, r_gain_self,
        r_query_self, r_key_self, r_value_self, r_out_self, r_gain_self_mlp, r_up_self, r_down_self,
        r_gain_dec_kv, r_key_dec, r_value_dec, r_dec_query, r_gain_dec_q, r_query_dec, r_out_dec, r_gain_final,
    )


def solution(mesh):
    split = P("items", "blk")
    rows = P(("items", "blk"))
    outs = [P("items", "blk", None), P(None, ("items", "blk"))] + [rows] * 28
    return jax.shard_map(
        local,
        mesh=mesh,
        in_specs=(split, P("items", None), P("items", None)) + (P(),) * 29 + (P("items", "blk", None),),
        out_specs=tuple(outs),
        check_vma=False,
    )
```

```python
import jax
import jax.numpy as jnp
from jax import lax
from jax.experimental import pallas as pl
from jax.experimental.pallas import tpu as pltpu
from jax.sharding import PartitionSpec as P

HEADS = 8
EPS = 1e-05
F32 = jnp.float32
BF16 = jnp.bfloat16
GELU_C = 0.7978845608028654
GELU_A = 0.044715


def nn(a, b):
    return lax.dot_general(a, b, (((1,), (0,)), ((), ())), preferred_element_type=F32)


def nt(a, b):
    return lax.dot_general(a, b, (((1,), (1,)), ((), ())), preferred_element_type=F32)


def tn(a, b):
    return lax.dot_general(a, b, (((0,), (0,)), ((), ())), preferred_element_type=F32)


def norm_forward(x, gain):
    centered = x - jnp.mean(x, axis=-1, keepdims=True)
    variance = jnp.mean(centered * centered, axis=-1, keepdims=True)
    rstd = lax.rsqrt(variance + EPS)
    hat = centered * rstd
    return (hat * gain.astype(F32)).astype(BF16), hat, rstd


def norm_backward(dy, hat, rstd, gain):
    dgain = jnp.sum(dy * hat, axis=0, keepdims=True)
    dhat = dy * gain.astype(F32)
    first = jnp.mean(dhat, axis=-1, keepdims=True)
    second = jnp.mean(dhat * hat, axis=-1, keepdims=True)
    return rstd * (dhat - first - hat * second), dgain


def gelu_forward(u):
    t = jnp.tanh(GELU_C * (u + GELU_A * u * u * u))
    return (0.5 * u * (1.0 + t)).astype(BF16)


def gelu_backward(dh, u):
    t = jnp.tanh(GELU_C * (u + GELU_A * u * u * u))
    slope = 0.5 * (1.0 + t) + 0.5 * u * (1.0 - t * t) * GELU_C * (1.0 + 3.0 * GELU_A * u * u)
    return dh * slope


def softmax(s):
    e = jnp.exp(s - jnp.max(s, axis=-1, keepdims=True))
    return e / jnp.sum(e, axis=-1, keepdims=True)


def softmax_backward(dp, soft, scale):
    inner = jnp.sum(dp * soft, axis=-1, keepdims=True)
    return (soft * (dp - inner) * scale).astype(BF16)


class Reducer:
    def __init__(self):
        n_items = lax.axis_size("items")
        self.count = n_items * lax.axis_size("blk")
        self.k = n_items.bit_length() - 1
        self.n_items = n_items

    def bit(self, name):
        if name == "y":
            return lax.axis_index("blk")
        return (lax.axis_index("items") >> name) & 1

    def exchange(self, x, name):
        if name == "y":
            return lax.ppermute(x, "blk", [(0, 1), (1, 0)])
        return lax.ppermute(x, "items", [(i, i ^ (1 << name)) for i in range(self.n_items)])

    def split(self, g):
        rows, width = g.shape
        return g.astype(BF16).reshape((2,) * (self.k + 1) + (rows // self.count, width))

    def reduce(self, grads, order):
        dims = list(range(self.k - 1, -1, -1)) + ["y"]
        parts = [self.split(g) for g in grads]
        heights = [p.shape[-2] for p in parts]
        for number, name in enumerate(order):
            axis = dims.index(name)
            mine = self.bit(name)
            send = [lax.dynamic_index_in_dim(p, 1 - mine, axis, keepdims=False) for p in parts]
            keep = [lax.dynamic_index_in_dim(p, mine, axis, keepdims=False) for p in parts]
            if number == 0:
                send = [jnp.concatenate(send, axis=-2)] if len(send) > 1 else send
                keep = [jnp.concatenate(keep, axis=-2)] if len(keep) > 1 else keep
            got = self.exchange(send[0], name)
            total = keep[0].astype(F32) + got.astype(F32)
            last = number == len(order) - 1
            parts = [total if last else total.astype(BF16)]
            dims.pop(axis)
        out, at = [], 0
        for height in heights:
            out.append(parts[0][at : at + height])
            at += height
        return out


CHUNK = 256
LAG = 2
MESH = pl.DeviceIdType.MESH
STAGES = {
    "xy": ("c", "x", "y", "z0", "z1"),
    "yx": ("c", "y", "x", "z0", "z1"),
}
ITEM_BIT = {"c": 0, "x": 1, "z0": 2, "z1": 3}


def padded_rows(r):
    return -(-r // 16) * 16


def my_bit(name):
    if name == "y":
        return lax.axis_index("blk")
    return (lax.axis_index("items") // 2 ** ITEM_BIT[name]) % 2


def partner(name):
    if name == "y":
        return {"blk": 1 - lax.axis_index("blk")}
    return {"items": lax.axis_index("items") + (1 - 2 * my_bit(name)) * 2 ** ITEM_BIT[name]}


def divide(first, second, mine, r, by_rows):
    if by_rows:
        first, second = (
            jnp.concatenate([first[:r], second[:r]], axis=0),
            jnp.concatenate([first[r:], second[r:]], axis=0),
        )
    return jnp.where(mine == 0, first, second), jnp.where(mine == 0, second, first)


def tie(values, after):
    count = len(values)
    anywhere = pl.BlockSpec(memory_space=pl.ANY)
    return pl.pallas_call(
        lambda *refs: None,
        out_shape=[jax.ShapeDtypeStruct(v.shape, v.dtype) for v in values],
        in_specs=[anywhere] * (count + len(after)),
        out_specs=[anywhere] * count,
        input_output_aliases={i: i for i in range(count)},
    )(*values, *after)


class Chunk:
    def __init__(self, bufs, at, sems, r, width, order):
        self.rc, self.r1, self.r2, self.r3, self.s4, self.r4, self.out = [b.at[at] for b in bufs]
        self.send, self.recv, self.at = sems[0], sems[1], at
        self.r, self.width, self.order = r, width, order
        self.step = 256 if r <= 40 and width % 256 == 0 else 128

    def copy(self, stage, source=None):
        src, dst = (
            (source, self.rc),
            (self.rc.at[:, :, 1], self.r1),
            (self.rc.at[:, 1, 0], self.r2),
            (self.rc.at[1, 0, 0], self.r3),
            (self.s4, self.r4),
        )[stage]
        return pltpu.make_async_remote_copy(
            src_ref=dst if src is None else src,
            dst_ref=dst,
            send_sem=self.send.at[self.at, stage],
            recv_sem=self.recv.at[self.at, stage],
            device_id=partner(STAGES[self.order][stage]),
            device_id_type=MESH,
        )

    def loop(self, pairs, body):
        columns = self.width // self.step

        def run(i, carry):
            body(i // columns, pl.ds(pl.multiple_of((i % columns) * self.step, self.step), self.step))
            return carry

        lax.fori_loop(0, pairs * columns, run, 0)

    def advance(self, stage, loaded=None):
        self.copy(stage).wait_recv()
        names = STAGES[self.order]
        r, kind, rc = self.r, self.rc.dtype, self.rc
        mine = my_bit(names[stage + 1]) if stage < 4 else None

        def total(a, b):
            return a.astype(F32) + b.astype(F32)

        def stage0(p, cols):
            q, z = p // 2, p % 2
            first = total(rc[q, z, 0, :, cols], loaded[q, z, 0, :, cols])
            second = total(rc[q, z, 1, :, cols], loaded[q, z, 1, :, cols])
            keep, send = divide(first, second, mine, r, names[1] == "y")
            rc[q, z, 0, :, cols] = keep.astype(kind)
            rc[q, z, 1, :, cols] = send.astype(kind)

        def stage1(q, cols):
            first = total(rc[q, 0, 0, :, cols], self.r1[q, 0, :, cols])
            second = total(rc[q, 1, 0, :, cols], self.r1[q, 1, :, cols])
            keep, send = divide(first, second, mine, r, True)
            rc[q, 0, 0, :, cols] = keep.astype(kind)
            rc[q, 1, 0, :, cols] = send.astype(kind)

        def stage2(q, cols):
            first = total(rc[0, 0, 0, :, cols], self.r2[0, :, cols])
            second = total(rc[1, 0, 0, :, cols], self.r2[1, :, cols])
            keep, send = divide(first, second, mine, r, True)
            rc[0, 0, 0, :, cols] = keep.astype(kind)
            rc[1, 0, 0, :, cols] = send.astype(kind)

        def stage3(q, cols):
            both = total(rc[0, 0, 0, :, cols], self.r3[:, cols])
            keep = jnp.where(mine == 0, both[:r], both[r:])
            send = jnp.where(mine == 0, both[r:], both[:r])
            extra = padded_rows(r) - r
            if extra:
                send = jnp.concatenate([send, jnp.zeros((extra, send.shape[1]), F32)], axis=0)
            self.s4[:, cols] = send.astype(kind)
            self.out[:, cols] = keep

        def stage4(q, cols):
            self.out[:, cols] = self.out[:, cols] + self.r4[:, cols].astype(F32)[:r]

        self.loop((4, 2, 1, 1, 1)[stage], (stage0, stage1, stage2, stage3, stage4)[stage])
        if stage < 4:
            self.copy(stage + 1).start()


def when(condition, action):
    if isinstance(condition, bool):
        if condition:
            action()
    else:
        pl.when(condition)(action)


SLOTS = 4
AHEAD = 3
B_SLOTS = 3


def reduce_kernel(plan, *refs):
    sides, steps, n_act, n_cot, widths, others = plan
    n_a, n_o = len(widths), len(others)
    acts, refs = refs[:n_act], refs[n_act:]
    cots, refs = refs[:n_cot], refs[n_cot:]
    o_src, refs = refs[:n_o], refs[n_o:]
    a_out, o_out = refs[:n_a], refs[n_a : n_a + n_o]
    refs = refs[n_a + n_o :]
    a_bufs, refs = refs[:7], refs[7:]
    act_in, act_t, cot_in, made = refs[:4]
    refs = refs[4:]
    o_bufs, refs = [refs[8 * i : 8 * i + 8] for i in range(n_o)], refs[8 * n_o :]
    a_sems, o_sems = refs[0:2], refs[2:4]
    act_sem, cot_sem, o_load_sem, a_out_sem, o_out_sem = refs[4:]
    core = my_bit("c")
    rows = act_t.shape[1] // 4

    barrier = pltpu.get_barrier_semaphore()
    for name in ("c", "x", "y", "z0", "z1"):
        pl.semaphore_signal(barrier, inc=1, device_id=partner(name), device_id_type=MESH)
    pl.semaphore_wait(barrier, 5)

    def chunk(step, side):
        return Chunk(a_bufs, 2 * step + side, a_sems, 40, CHUNK, ("xy", "yx")[side])

    def act_copy(side, group):
        return pltpu.make_async_copy(acts[sides[side][0][group][1]], act_in.at[side], act_sem.at[side])

    def cot_copy(side, step):
        source, number, _ = sides[side][1][step]
        slot = step % B_SLOTS
        return pltpu.make_async_copy(
            cots[source].at[:, pl.ds(number * CHUNK, CHUNK)], cot_in.at[side, slot], cot_sem.at[side, slot]
        )

    def first_copy(step, side):
        return chunk(step, side).copy(0, made.at[side, step % SLOTS, 1 - core])

    def produce(step):
        for side in range(2):
            groups = sides[side][0]
            for g, (start, _) in enumerate(groups):

                def fresh(g=g, side=side, groups=groups):
                    act_copy(side, g).wait()

                    def turn(i, carry):
                        at = pl.ds(pl.multiple_of(i * 256, 256), 256)
                        act_t[side, at, :] = act_in[side, :, at].T
                        return carry

                    lax.fori_loop(0, act_in.shape[2] // 256, turn, 0)
                    if g + 1 < len(groups):
                        act_copy(side, g + 1).start()

                when(step == start, fresh)
            for later in range(B_SLOTS - 1, steps):
                when(step == later - (B_SLOTS - 1), lambda later=later, side=side: cot_copy(side, later).start())
            slot = step % B_SLOTS
            pltpu.make_async_copy(
                cots[0].at[:, pl.ds(0, CHUNK)], cot_in.at[side, slot], cot_sem.at[side, slot]
            ).wait()
            when(step >= SLOTS, lambda side=side: first_copy(step - SLOTS, side).wait_send())

            def product(i, carry, side=side, slot=slot):
                part = act_t[side, pl.ds(pl.multiple_of(i * rows, rows), rows), :]
                result = jnp.dot(part, cot_in[side, slot], preferred_element_type=F32)
                height = rows // 4
                for x in range(2):
                    for c in range(2):
                        at = (2 * x + c) * height
                        made[side, step % SLOTS, c, i // 2, i % 2, x] = result[at : at + height].astype(BF16)
                return carry

            lax.fori_loop(0, 4, product, 0)
            first_copy(step, side).start()

    small = []
    for i, (r, width, order) in enumerate(others):
        item = Chunk([b.at[0:1] for b in o_bufs[i][:7]], 0, o_sems, r, width, order)
        item.at = i
        small.append(item)
        item.copy(0, o_src[i].at[:, :, :, 1 - core]).start()
        pltpu.make_async_copy(o_src[i].at[:, :, :, core], o_bufs[i][7], o_load_sem.at[i]).start()
    for side in range(2):
        act_copy(side, 0).start()
        for step in range(B_SLOTS - 1):
            cot_copy(side, step).start()

    def begin(step, carry):
        produce(step)
        return carry

    lax.fori_loop(0, AHEAD, begin, 0)
    for i, item in enumerate(small):
        pltpu.make_async_copy(o_src[i].at[:, :, :, core], o_bufs[i][7], o_load_sem.at[i]).wait()
        item.advance(0, o_bufs[i][7])

    def run(step, carry):
        pl.when(step + AHEAD < steps)(lambda: produce(step + AHEAD))

        def enter():
            for side in range(2):
                chunk(step, side).advance(0, made.at[side, step % SLOTS, core])

        pl.when(step < steps)(enter)
        for stage in range(4, 0, -1):
            old = step - stage * LAG

            def act(old=old, stage=stage):
                for side in range(2):
                    chunk(old, side).advance(stage)

            pl.when(jnp.logical_and(old >= 0, old < steps))(act)
        for number in range(4):

            def others_on(number=number):
                for item in small:
                    item.advance(number + 1)

            pl.when(step == 4 + 5 * number)(others_on)
        return carry

    lax.fori_loop(0, steps + 4 * LAG, run, 0)

    outs = []
    for side in range(2):
        for step in range(steps):
            _, number, target = sides[side][1][step]
            at = 2 * step + side
            outs.append(
                pltpu.make_async_copy(
                    a_bufs[6].at[at], a_out[target].at[:, pl.ds(number * CHUNK, CHUNK)], a_out_sem.at[at]
                )
            )
    for i in range(n_o):
        outs.append(pltpu.make_async_copy(o_bufs[i][6].at[0], o_out[i], o_out_sem.at[i]))
    for copy in outs:
        copy.start()
    for step in range(steps - SLOTS, steps):
        for side in range(2):
            first_copy(step, side).wait_send()
    for i, item in enumerate(small):
        item.copy(0, o_src[i].at[:, :, :, 1 - core]).wait_send()
        for stage in range(1, 5):
            item.copy(stage).wait_send()

    def wait_sent(step, carry):
        for side in range(2):
            for stage in range(1, 5):
                chunk(step, side).copy(stage).wait_send()
        return carry

    lax.fori_loop(0, steps, wait_sent, 0)
    for copy in outs:
        copy.wait()


def buffers(count, r, width, kind):
    rp = padded_rows(r)
    return [
        pltpu.VMEM((count, 2, 2, 2, 2 * r, width), kind),
        pltpu.VMEM((count, 2, 2, 2 * r, width), kind),
        pltpu.VMEM((count, 2, 2 * r, width), kind),
        pltpu.VMEM((count, 2 * r, width), kind),
        pltpu.VMEM((count, rp, width), kind),
        pltpu.VMEM((count, rp, width), kind),
        pltpu.VMEM((count, r, width), F32),
    ]


def reduce_all(products, others):
    acts, cots, sides, widths = [], [], [], []
    for side in products:
        groups, sequence = [], []
        for act, own in side:
            groups.append((len(sequence), len(acts)))
            acts.append(act)
            for cot in own:
                for number in range(cot.shape[1] // CHUNK):
                    sequence.append((len(cots), number, len(widths)))
                cots.append(cot)
                widths.append(cot.shape[1])
        sides.append((tuple(groups), tuple(sequence)))
    steps = len(sides[0][1])
    assert steps == len(sides[1][1])

    def view(g):
        return g.reshape(2, 2, 2, 2, g.shape[0] // 16, g.shape[1])

    plan = (
        tuple(sides), steps, len(acts), len(cots), tuple(widths),
        tuple((g.shape[0] // 32, g.shape[1], order) for g, order in others),
    )
    depth, features = acts[0].shape
    scratch = buffers(2 * steps, 40, CHUNK, BF16)
    scratch += [
        pltpu.VMEM((2, depth, features), BF16),
        pltpu.VMEM((2, features, depth), BF16),
        pltpu.VMEM((2, B_SLOTS, depth, CHUNK), BF16),
        pltpu.VMEM((2, SLOTS, 2, 2, 2, 2, 80, CHUNK), BF16),
    ]
    for g, order in others:
        r = g.shape[0] // 32
        scratch += buffers(1, r, g.shape[1], g.dtype)
        scratch.append(pltpu.VMEM((2, 2, 2, 2 * r, g.shape[1]), g.dtype))
    dma = pltpu.SemaphoreType.DMA
    scratch += [dma((2 * steps, 5)), dma((2 * steps, 5)), dma((len(others), 5)), dma((len(others), 5))]
    scratch += [dma((2,)), dma((2, B_SLOTS)), dma((len(others),)), dma((2 * steps,)), dma((len(others),))]
    anywhere = pl.BlockSpec(memory_space=pl.ANY)
    arrays = acts + cots + [view(g) for g, order in others]
    results = pl.pallas_call(
        lambda *refs: reduce_kernel(plan, *refs),
        out_shape=[jax.ShapeDtypeStruct((features // 32, w), F32) for w in widths]
        + [jax.ShapeDtypeStruct((g.shape[0] // 32, g.shape[1]), F32) for g, order in others],
        in_specs=[anywhere] * len(arrays),
        out_specs=[anywhere] * (len(widths) + len(others)),
        scratch_shapes=scratch,
        compiler_params=pltpu.CompilerParams(
            collective_id=0, has_side_effects=True, vmem_limit_bytes=62 * 1024 * 1024
        ),
    )(*arrays)
    return results[: len(widths)], results[len(widths) :]


def finish(plain, table, vectors, vocab, vector_count):
    count = len(plain)
    width = table.shape[0]

    def kernel(*refs):
        sources, refs = refs[:count], refs[count:]
        table_ref, vectors_ref = refs[:2]
        refs = refs[2:]
        targets, refs = refs[:count], refs[count:]
        emb_ref, row_refs, refs = refs[0], refs[1:5], refs[5:]
        gain_refs, refs = refs[:vector_count], refs[vector_count:]
        staged, (in_sem, out_sem) = refs[:count], refs[count:]
        inward = [pltpu.make_async_copy(sources[i], staged[i], in_sem.at[i]) for i in range(count)]
        outward = [pltpu.make_async_copy(staged[i], targets[i], out_sem.at[i]) for i in range(count)]
        for copy in inward:
            copy.start()
        turned = table_ref[...].T
        emb_ref[...] = table_ref[:, :vocab]
        vector_rows = vectors_ref[...].T
        for i, row_ref in enumerate(row_refs):
            row_ref[...] = turned[vocab + i]
        for i, gain_ref in enumerate(gain_refs):
            gain_ref[...] = vector_rows[i]
        for i in range(count):
            inward[i].wait()
            outward[i].start()
        for copy in outward:
            copy.wait()

    anywhere = pl.BlockSpec(memory_space=pl.ANY)
    local_memory = pl.BlockSpec(memory_space=pltpu.VMEM)
    shapes = [jax.ShapeDtypeStruct(p.shape, F32) for p in plain]
    shapes += [jax.ShapeDtypeStruct((width, vocab), F32)] + [jax.ShapeDtypeStruct((width,), F32)] * 4
    shapes += [jax.ShapeDtypeStruct(vectors.shape[:1], F32)] * vector_count
    results = pl.pallas_call(
        kernel,
        out_shape=shapes,
        in_specs=[anywhere] * count + [local_memory] * 2,
        out_specs=[anywhere] * count + [local_memory] * (5 + vector_count),
        scratch_shapes=[pltpu.VMEM(p.shape, F32) for p in plain] + [pltpu.SemaphoreType.DMA((count,))] * 2,
    )(*plain, table, vectors)
    return results[:count], results[count], results[count + 1 : count + 5], results[count + 5 :]


def center(x):
    hat = x - jnp.mean(x, axis=-1, keepdims=True)
    rstd = lax.rsqrt(jnp.mean(hat * hat, axis=-1, keepdims=True) + EPS)
    return hat * rstd, rstd


def center_backward(dhat, hat, rstd):
    first = jnp.mean(dhat, axis=-1, keepdims=True)
    second = jnp.mean(dhat * hat, axis=-1, keepdims=True)
    return rstd * (dhat - first - hat * second)


def bytes_kernel(
    at, scale, p, soft, vd, qk, nb, rstd, gain, codes, emb, sums, wide,
    pn, q, dae, daft, nl, rstd_l, gain_l, w_key, w_query,
    dbytes, table, turned, dq, g_key, g_value, g_latent,
    total, ds,
):
    i = pl.program_id(0)
    block = codes.shape[1]

    @pl.when(i == 0)
    def _():
        total[...] = jnp.zeros_like(total)
        total[: emb.shape[0]] = emb[...]
        total[at + 1 : at + 2] = sums[1:2]
        total[at + 2 : at + 3] = sums[0:1]
        ds[...] = softmax_backward(nt(vd[...], nb[...]), soft[...], scale)
        dn = nn(ds[...], nb[...]).astype(BF16)
        g_key[...] = nn(dn.T, q[...]).astype(BF16)
        g_value[...] = nn(pn[...].T, dae[...]).astype(BF16)
        dq[...] = nn(dn, w_key[...]).astype(BF16)
        dnl = nt(dq[...], w_query[...])
        g = gain_l[...].astype(F32)
        hat = nl[...].astype(F32) / g
        g_latent[...] = (daft[...] + center_backward(dnl * g, hat, rstd_l[...])).astype(BF16)
        first = jnp.sum(dnl * hat, axis=0, keepdims=True)
        own = lax.broadcasted_iota(jnp.int32, wide.shape, 0) == 0
        turned[...] = jnp.zeros_like(turned)
        turned[:, : wide.shape[0]] = jnp.where(own, first, wide[...]).T.astype(BF16)

    rows = pl.ds(pl.multiple_of(i * block, block), block)
    g = gain[...].astype(F32)
    normed = nb[rows, :]
    dnb = nn(p[...].T, vd[...]) + nn(ds[:, rows].T, qk[...])
    hat = normed.astype(F32) / g
    dx = center_backward(dnb * g, hat, rstd[...]).astype(BF16)
    dbytes[...] = dx
    entry = lax.broadcasted_iota(jnp.int32, (total.shape[0], block), 0)
    onehot = (entry == codes[...]).astype(BF16)
    total[...] += nn(onehot, dx)
    total[at : at + 1] += jnp.sum(dnb * hat, axis=0, keepdims=True)

    @pl.when(i == pl.num_programs(0) - 1)
    def _():
        table[...] = total[...].T.astype(BF16)


def bytes_backward(at, scale, p, soft, vd, qk, nb, rstd, gain, codes, emb, sums, wide, rest):
    rows, width = nb.shape
    latents, block, entries = p.shape[0], 256, -(-emb.shape[0] // 128) * 128
    features = wide.shape[1]
    qk_width = rest[1].shape[1]

    def whole(x):
        return pl.BlockSpec(x.shape, lambda i: (0, 0))

    shapes = [
        jax.ShapeDtypeStruct((rows, width), BF16),
        jax.ShapeDtypeStruct((width, entries), BF16),
        jax.ShapeDtypeStruct((features, 128), BF16),
        jax.ShapeDtypeStruct((latents, qk_width), BF16),
        jax.ShapeDtypeStruct((width, qk_width), BF16),
        jax.ShapeDtypeStruct((width, features), BF16),
        jax.ShapeDtypeStruct((latents, features), BF16),
    ]
    arrays = (p, soft, vd, qk, nb, rstd, gain[None, :], codes[None, :], emb, sums, wide) + rest
    specs = [whole(x) for x in arrays]
    specs[0] = pl.BlockSpec((latents, block), lambda i: (0, i))
    specs[5] = pl.BlockSpec((block, 1), lambda i: (i, 0))
    specs[7] = pl.BlockSpec((1, block), lambda i: (0, i))
    return pl.pallas_call(
        lambda *refs: bytes_kernel(at, scale, *refs),
        grid=(rows // block,),
        out_shape=shapes,
        in_specs=specs,
        out_specs=[pl.BlockSpec((block, width), lambda i: (i, 0))] + [whole(x) for x in shapes[1:]],
        scratch_shapes=[pltpu.VMEM((entries, width), F32), pltpu.VMEM((latents, rows), BF16)],
        compiler_params=pltpu.CompilerParams(vmem_limit_bytes=60 * 1024 * 1024),
    )(*arrays)


def head_columns(head, width):
    each = width // HEADS
    low, high = head * each // 128 * 128, -(-(head + 1) * each // 128) * 128
    place = low + lax.broadcasted_iota(jnp.int32, (1, high - low), 1)
    return slice(low, high), jnp.logical_and(place >= head * each, place < (head + 1) * each)


def pick(mask, x):
    return jnp.where(mask, x, jnp.zeros_like(x))


def head_softmax(head, q, k):
    columns, mask = head_columns(head, q.shape[1])
    scale = (q.shape[1] // HEADS) ** (-0.5)
    return softmax(nt(pick(mask, q[:, columns]), k[:, columns]) * scale), scale


def self_forward_heads(q, k, v, total):
    total[...] = jnp.zeros_like(total)
    for head in range(HEADS):
        p = head_softmax(head, q, k)[0].astype(BF16)
        columns, mask = head_columns(head, v.shape[1])
        total[:, columns] += nn(p, pick(mask, v[:, columns]))


def self_backward_heads(q, k, v, da, dq_sum, dk_sum, dv_sum):
    for ref in (dq_sum, dk_sum, dv_sum):
        ref[...] = jnp.zeros_like(ref)
    for head in range(HEADS):
        soft, scale = head_softmax(head, q, k)
        columns, mask = head_columns(head, v.shape[1])
        da_head = pick(mask, da[:, columns])
        ds = softmax_backward(nt(da_head, v[:, columns]), soft, scale)
        dv_sum[:, columns] += nn(soft.astype(BF16).T, da_head)
        columns, mask = head_columns(head, q.shape[1])
        dq_sum[:, columns] += nn(ds, pick(mask, k[:, columns]))
        dk_sum[:, columns] += nn(ds.T, pick(mask, q[:, columns]))


class Stream:
    def __init__(self, sources, targets, sem):
        self.copies = [pltpu.make_async_copy(a, b, sem.at[i]) for i, (a, b) in enumerate(zip(sources, targets))]
        self.targets, self.arrived = targets, set()
        for copy in self.copies:
            copy.start()

    def __getitem__(self, i):
        if i not in self.arrived:
            self.copies[i].wait()
            self.arrived.add(i)
        return self.targets[i][...]


class Results:
    def __init__(self, stage, targets, sem):
        self.stage, self.targets, self.sem, self.copies, self.left = stage, targets, sem, [], set()

    def put(self, value, over=None):
        i = len(self.copies)
        buffer = self.stage[i if over is None else over]
        if over is not None:
            self.copies[over].wait()
            self.left.add(over)
        buffer[...] = value.astype(buffer.dtype)
        copy = pltpu.make_async_copy(buffer, self.targets[i], self.sem.at[i])
        copy.start()
        self.copies.append(copy)
        return buffer

    def send(self, source):
        i = len(self.copies)
        copy = pltpu.make_async_copy(source, self.targets[i], self.sem.at[i])
        copy.start()
        self.copies.append(copy)

    def finish(self):
        for i, copy in enumerate(self.copies):
            if i not in self.left:
                copy.wait()


def streamed(body, small, large, shapes, extra, unstaged):
    n_s, n_l, n_o = len(small), len(large), len(shapes)

    def kernel(*refs):
        ins, refs = refs[: n_s + n_l], refs[n_s + n_l :]
        outs, refs = refs[:n_o], refs[n_o:]
        held, refs = refs[:n_l], refs[n_l:]
        kept, refs = list(refs[: n_o - len(unstaged)]), refs[n_o - len(unstaged) :]
        stage = [None if i in unstaged else kept.pop(0) for i in range(n_o)]
        stream = Stream(ins[n_s:], held, refs[0])
        results = Results(stage, outs, refs[1])
        body(ins[:n_s], stream, results, refs[2:])
        results.finish()

    anywhere = pl.BlockSpec(memory_space=pl.ANY)
    return pl.pallas_call(
        kernel,
        out_shape=shapes,
        in_specs=[pl.BlockSpec(memory_space=pltpu.VMEM)] * n_s + [anywhere] * n_l,
        out_specs=[anywhere] * n_o,
        scratch_shapes=[pltpu.VMEM(x.shape, x.dtype) for x in large]
        + [pltpu.VMEM(x.shape, x.dtype) for i, x in enumerate(shapes) if i not in unstaged]
        + [pltpu.SemaphoreType.DMA((n_l,)), pltpu.SemaphoreType.DMA((n_o,))]
        + extra,
        compiler_params=pltpu.CompilerParams(vmem_limit_bytes=63 * 1024 * 1024),
    )(*small, *large)


def middle_pass(latent, pn, gains, byte_gains, weights, scale):
    rows, width = latent.shape
    emb, queries, cot = weights[14:]
    entries, depth = emb.shape
    block = 256
    qk = weights[4].shape[1]

    def body(small, w, results, extra):
        latent_ref, pn_ref, g1, g2, g3, g4, gain_q, gain_f = small
        total, dq_sum, dk_sum, sums, u1, u2, q, k, v, k_d, v_d, kq, vo, vo_mid, g_pd, g_dn, g_emb, g_byte = extra
        put = results.put

        def norm(x, gain):
            hat, rstd = center(x)
            return put(hat * gain[...].astype(F32)), rstd

        a_e = put(nn(pn_ref[...], w[0]))
        x = latent_ref[...].astype(F32) + nn(a_e[...], w[1])
        n1, r1 = norm(x, g1)
        u1[...] = nn(n1[...], w[2])
        h1 = put(gelu_forward(u1[...]))
        x = x + nn(h1[...], w[3])
        n2, r2 = norm(x, g2)
        q[...] = nn(n2[...], w[4]).astype(BF16)
        k[...] = nn(n2[...], w[5]).astype(BF16)
        v[...] = nn(n2[...], w[6]).astype(BF16)
        self_forward_heads(q, k, v, total)
        a_s = put(total[...])
        x = x + nn(a_s[...], w[7])
        n3, r3 = norm(x, g3)
        u2[...] = nn(n3[...], w[8])
        h2 = put(gelu_forward(u2[...]))
        x = x + nn(h2[...], w[9])
        n4, r4 = norm(x, g4)
        k_d[...] = nn(n4[...], w[10]).astype(BF16)
        v_d[...] = nn(n4[...], w[11]).astype(BF16)

        w_query, w_out = w[12], w[13]
        kq[...] = nt(k_d[...], w_query).astype(BF16)
        out = nn(v_d[...], w_out)
        vo[...] = out.astype(BF16)
        vo_mid[...] = (out - jnp.mean(out, axis=0, keepdims=True)).astype(BF16)
        for ref in (g_pd, g_dn, g_emb, g_byte):
            ref[...] = jnp.zeros_like(ref)
        w[14], w[15], w[16]
        emb_ref, query_ref, cot_ref = w.targets[14:]

        def decode(i, carry):
            at = pl.ds(pl.multiple_of(i * block, block), block)
            x = query_ref[at, :].astype(F32)
            hat_q, rstd_q = center(x)
            gq, gf = gain_q[...].astype(F32), gain_f[...].astype(F32)
            nq = (hat_q * gq).astype(BF16)
            soft = softmax(nt(nq, kq[...]) * scale)
            p = soft.astype(BF16)
            hat_f, rstd_f = center(x + nn(p, vo[...]))
            nf = (hat_f * gf).astype(BF16)
            cot_part = cot_ref[:, at]
            dnf = nn(cot_part.T, emb_ref[...])
            g_emb[...] += nn(cot_part, nf)
            cot_ref[:, at] = nt(emb_ref[...], nf).astype(BF16)
            g_byte[0:1] += jnp.sum(dnf * hat_f, axis=0, keepdims=True)
            ddec = center_backward(dnf * gf, hat_f, rstd_f)
            ddec16 = ddec.astype(BF16)
            g_pd[...] += nn(p.T, ddec16)
            ds = softmax_backward(nt(ddec16, vo_mid[...]), soft, scale)
            g_dn[...] += nn(ds.T, nq)
            dnq = nn(ds, kq[...])
            g_byte[1:2] += jnp.sum(dnq * hat_q, axis=0, keepdims=True)
            query_ref[at, :] = (ddec + center_backward(dnq * gq, hat_q, rstd_q)).astype(BF16)
            return carry

        lax.fori_loop(0, queries.shape[0] // block, decode, 0)
        results.send(query_ref)
        results.send(cot_ref)
        results.send(g_emb)
        results.send(g_byte)
        pd, dn = g_pd[...].astype(BF16), g_dn[...].astype(BF16)
        dk_d = nn(dn, w.targets[12][...]).astype(BF16)
        dv_d = nt(pd, w.targets[13][...]).astype(BF16)
        put(dk_d)
        put(dv_d)
        put(nn(dn.T, k_d[...]))
        put(nn(v_d[...].T, pd))

        sums[...] = jnp.zeros_like(sums)

        def back(dy, normed, rstd, gain, row):
            g = gain[...].astype(F32)
            hat = normed[...].astype(F32) / g
            sums[row : row + 1] = jnp.sum(dy * hat, axis=0, keepdims=True)
            return center_backward(dy * g, hat, rstd)

        dlat = back(nt(dk_d, w[10]) + nt(dv_d, w[11]), n4, r4, g4, 4)
        dlat16 = put(dlat, 0)
        du2 = put(gelu_backward(nt(dlat16[...], w[9]), u2[...]), 2)
        das = dlat + back(nt(du2[...], w[8]), n3, r3, g3, 3)
        das16 = put(das, 4)
        da = nt(das16[...], w[7]).astype(BF16)
        self_backward_heads(q, k, v, da, dq_sum, dk_sum, total)
        dq, dk, dv = put(dq_sum[...]), put(dk_sum[...]), put(total[...], 6)
        dn2 = nt(dq[...], w[4]) + nt(dk[...], w[5]) + nt(dv[...], w[6])
        denc = das + back(dn2, n2, r2, g2, 2)
        denc16 = put(denc, 7)
        du1 = put(gelu_backward(nt(denc16[...], w[3]), u1[...]), 5)
        daft = denc + back(nt(du1[...], w[2]), n1, r1, g1, 1)
        daft16 = put(daft, 3)
        u1[...] = daft
        results.send(u1)
        dae = put(nt(daft16[...], w[1]), 1)
        put(nt(dae[...], w[0]))
        results.send(sums)

    wide = (rows, width)

    def low(*shape):
        return jax.ShapeDtypeStruct(shape, BF16)

    def full(*shape):
        return jax.ShapeDtypeStruct(shape, F32)

    shapes = [low(*wide)] * 8
    shapes += [low(*queries.shape), low(*cot.shape), full(entries, depth), full(8, depth)]
    shapes += [low(rows, qk), low(rows, depth), low(depth, qk), low(depth, depth)]
    shapes += [low(*wide)] * 3 + [low(rows, qk)] * 2 + [low(*wide)] * 4
    shapes += [full(*wide), low(*wide), low(rows, depth), full(8, width)]
    unstaged = {8, 9, 10, 11, 16, 17, 18, 21, 22, 23, 24, 25, 26, 28}
    vmem = pltpu.VMEM
    extra = [vmem(wide, F32), vmem((rows, qk), F32), vmem((rows, qk), F32), vmem((8, width), F32)]
    extra += [vmem(wide, F32)] * 2 + [vmem((rows, qk), BF16)] * 2 + [vmem(wide, BF16)]
    extra += [vmem((rows, qk), BF16)] + [vmem((rows, depth), BF16)] * 4 + [vmem((rows, depth), F32)] * 2
    extra += [vmem((entries, depth), F32), vmem((8, depth), F32)]
    small = [latent, pn] + [g[None, :] for g in gains + byte_gains]
    return streamed(body, small, weights, shapes, extra, unstaged)


def local(
    byte_ids, span_start, span_len, embedding, position, mask_vector, gain_bytes, key_enc,
    value_enc, latent_init, gain_latent, query_enc, out_enc, gain_enc_mlp, up_enc, down_enc,
    gain_self, query_self, key_self, value_self, out_self, gain_self_mlp, up_self, down_self,
    gain_dec_kv, key_dec, value_dec, dec_query, gain_dec_q, query_dec, out_dec, gain_final,
    logit_cot,
):
    me = lax.axis_index("blk")
    half = byte_ids.shape[1]
    total = position.shape[0]
    vocab = embedding.shape[0]
    reducer = Reducer()
    k = reducer.k
    order_yx = [0, "y", 1] + list(range(2, k))
    order_xy = [0, 1, "y"] + list(range(2, k))

    def swap(x):
        return lax.ppermute(x, "blk", [(0, 1), (1, 0)])

    def own_item(first, second, after=()):
        mine = jnp.where(me == 0, first, second)
        send = jnp.where(me == 0, second, first)
        if after:
            (send,) = tie([send], after)
        got = swap(send)
        low_half = jnp.where(me == 0, mine, got)
        high_half = jnp.where(me == 0, got, mine)
        return jnp.concatenate([low_half, high_half], axis=-1)

    ids = own_item(byte_ids[0], byte_ids[1])
    cot_rows = logit_cot.transpose(2, 0, 1)
    cot = own_item(cot_rows[:, 0], cot_rows[:, 1], [ids])
    entries = -(-(vocab + 4) // 16) * 16
    cot = jnp.pad(cot, ((0, entries - vocab), (0, 0)))
    emb_rows = jnp.pad(embedding, ((0, entries - vocab), (0, 0)))
    starts = lax.dynamic_index_in_dim(span_start, me, 0, keepdims=False)
    lengths = lax.dynamic_index_in_dim(span_len, me, 0, keepdims=False)

    places = lax.iota(jnp.int32, total)
    inside = (places[None, :] >= starts[:, None]) & (places[None, :] < (starts + lengths)[:, None])
    codes = jnp.where(jnp.any(inside, axis=0), vocab, ids)
    padded = -(-(vocab + 4) // 128) * 128
    table = jnp.concatenate(
        [embedding, mask_vector[None, :], jnp.zeros((padded - vocab - 1, embedding.shape[1]), BF16)], axis=0
    )
    onehot = (codes[:, None] == lax.iota(jnp.int32, padded)[None, :]).astype(BF16)
    bytes_in = nn(onehot, table) + position.astype(F32)
    nb, hat_b, rstd_b = norm_forward(bytes_in, gain_bytes)

    latent32 = latent_init.astype(F32)
    nl, hat_l, rstd_l = norm_forward(latent32, gain_latent)
    q_e = nn(nl, query_enc).astype(BF16)
    scale_e = q_e.shape[1] ** (-0.5)
    qk_e = nt(q_e, key_enc).astype(BF16)
    soft_e = softmax(nt(qk_e, nb) * scale_e)
    p_e = soft_e.astype(BF16)
    pn_e = nn(p_e, nb).astype(BF16)
    gains = (gain_enc_mlp, gain_self, gain_self_mlp, gain_dec_kv)
    (
        a_e, n1, h1, n2, a_s, n3, h2, n4,
        g_dec_query, logits, g_emb_out, gain_sums, dk_d, dv_d, g_query_dec, g_out_dec,
        dlat16, du2, das16, dq_s, dk_s, dv_s, denc16, du1, daft16, dafter, dae16, vd_e, wide,
    ) = middle_pass(
        latent_init, pn_e, gains, (gain_dec_q, gain_final),
        [
            value_enc, out_enc, up_enc, down_enc, query_self, key_self, value_self, out_self, up_self,
            down_self, key_dec, value_dec, query_dec, out_dec, emb_rows, dec_query, cot,
        ],
        query_dec.shape[1] ** (-0.5),
    )
    logits = logits[:vocab]
    logits_got = swap(jnp.where(me == 0, logits[:, half:], logits[:, :half]))
    logits_own = jnp.where(me == 0, logits[:, :half], logits[:, half:])
    side = lax.broadcasted_iota(jnp.int32, (1, 2, 1), 1)
    logits_out = jnp.where(side == me, logits_own[:, None, :], logits_got[:, None, :]).transpose(1, 2, 0)

    dbytes, g_table, vectors, dq_e, g_key_enc, g_value_enc, g_latent = bytes_backward(
        vocab + 1, scale_e, p_e, soft_e, vd_e, qk_e, nb, rstd_b, gain_bytes, codes, g_emb_out, gain_sums, wide,
        (pn_e, q_e, dae16, dafter, nl, rstd_l, gain_latent[None, :], key_enc, query_enc),
    )

    def low(g):
        return g.astype(BF16)

    if reducer.n_items == 16:
        first_side = [(n1, [du1]), (a_e, [daft16]), (n3, [du2]), (n2, [dv_s, dk_s])]
        second_side = [
            (h1, [denc16]), (h2, [dlat16]), (a_s, [das16]), (n4, [dv_d, dk_d]), (n2, [dq_s]), (nl, [dq_e]),
        ]
        others = [
            (low(g_dec_query), "xy"), (low(dbytes), "yx"), (low(g_value_enc), "xy"), (low(g_out_dec), "yx"),
            (low(g_table), "yx"), (low(g_key_enc), "xy"), (low(g_query_dec), "yx"), (low(g_latent), "xy"),
            (low(vectors), "yx"),
        ]
        (
            r_up_enc, r_out_enc, r_up_self, r_value_self, r_key_self,
            r_down_enc, r_down_self, r_out_self, r_value_dec, r_key_dec, r_query_self, r_query_enc,
        ), (
            r_dec_query, r_position, r_value_enc, r_out_dec, r_emb, r_key_enc, r_query_dec, r_latent, r_vectors,
        ) = reduce_all((first_side, second_side), others)
    else:
        r_dec_query, r_out_dec, r_value_dec = reducer.reduce([g_dec_query, g_out_dec, tn(n4, dv_d)], order_yx)
        r_down_self, r_up_self, r_out_self = reducer.reduce(
            [tn(h2, dlat16), tn(n3, du2), tn(a_s, das16)], order_xy
        )
        r_value_self, r_down_enc = reducer.reduce([tn(n2, dv_s), tn(h1, denc16)], order_yx)
        r_up_enc, r_out_enc = reducer.reduce([tn(n1, du1), tn(a_e, daft16)], order_xy)
        r_query_dec, r_key_dec, r_query_self, r_key_self = reducer.reduce(
            [g_query_dec, tn(n4, dk_d), tn(n2, dq_s), tn(n2, dk_s)], order_xy
        )
        r_value_enc, r_latent = reducer.reduce([g_value_enc, g_latent], order_xy)
        (r_position,) = reducer.reduce([dbytes], order_yx)
        r_key_enc, r_query_enc = reducer.reduce([g_key_enc, tn(nl, dq_e)], order_yx)
        (r_emb,) = reducer.reduce([g_table], order_yx)
        (r_vectors,) = reducer.reduce([vectors], order_xy)

    plain = [
        r_position, r_key_enc, r_value_enc, r_latent, r_query_enc, r_out_enc, r_up_enc, r_down_enc,
        r_query_self, r_key_self, r_value_self, r_out_self, r_up_self, r_down_self, r_key_dec, r_value_dec,
        r_dec_query, r_query_dec, r_out_dec,
    ]
    plain, r_embedding, (r_mask, r_gain_bytes, r_gain_dec_q, r_gain_final), gains = finish(plain, r_emb, r_vectors, vocab, 1 + len(gains))
    (
        r_position, r_key_enc, r_value_enc, r_latent, r_query_enc, r_out_enc, r_up_enc, r_down_enc,
        r_query_self, r_key_self, r_value_self, r_out_self, r_up_self, r_down_self, r_key_dec, r_value_dec,
        r_dec_query, r_query_dec, r_out_dec,
    ) = plain
    (
        r_gain_latent, r_gain_enc_mlp, r_gain_self, r_gain_self_mlp, r_gain_dec_kv,
    ) = gains
    return (
        logits_out, r_embedding.T, r_position, r_mask, r_gain_bytes, r_key_enc, r_value_enc,
        r_latent, r_gain_latent, r_query_enc, r_out_enc, r_gain_enc_mlp, r_up_enc, r_down_enc, r_gain_self,
        r_query_self, r_key_self, r_value_self, r_out_self, r_gain_self_mlp, r_up_self, r_down_self,
        r_gain_dec_kv, r_key_dec, r_value_dec, r_dec_query, r_gain_dec_q, r_query_dec, r_out_dec, r_gain_final,
    )


def solution(mesh):
    split = P("items", "blk")
    rows = P(("items", "blk"))
    outs = [P("items", "blk", None), P(None, ("items", "blk"))] + [rows] * 28
    return jax.shard_map(
        local,
        mesh=mesh,
        in_specs=(split, P("items", None), P("items", None)) + (P(),) * 29 + (P("items", "blk", None),),
        out_specs=tuple(outs),
        check_vma=False,
    )
```

```python
import jax
import jax.numpy as jnp
from jax import lax
from jax.experimental import pallas as pl
from jax.experimental.pallas import tpu as pltpu
from jax.sharding import PartitionSpec as P

HEADS = 8
EPS = 1e-05
F32 = jnp.float32
BF16 = jnp.bfloat16
GELU_C = 0.7978845608028654
GELU_A = 0.044715


def nn(a, b):
    return lax.dot_general(a, b, (((1,), (0,)), ((), ())), preferred_element_type=F32)


def nt(a, b):
    return lax.dot_general(a, b, (((1,), (1,)), ((), ())), preferred_element_type=F32)


def tn(a, b):
    return lax.dot_general(a, b, (((0,), (0,)), ((), ())), preferred_element_type=F32)


def norm_forward(x, gain):
    centered = x - jnp.mean(x, axis=-1, keepdims=True)
    variance = jnp.mean(centered * centered, axis=-1, keepdims=True)
    rstd = lax.rsqrt(variance + EPS)
    hat = centered * rstd
    return (hat * gain.astype(F32)).astype(BF16), hat, rstd


def norm_backward(dy, hat, rstd, gain):
    dgain = jnp.sum(dy * hat, axis=0, keepdims=True)
    dhat = dy * gain.astype(F32)
    first = jnp.mean(dhat, axis=-1, keepdims=True)
    second = jnp.mean(dhat * hat, axis=-1, keepdims=True)
    return rstd * (dhat - first - hat * second), dgain


def gelu_forward(u):
    t = jnp.tanh(GELU_C * (u + GELU_A * u * u * u))
    return (0.5 * u * (1.0 + t)).astype(BF16)


def gelu_backward(dh, u):
    t = jnp.tanh(GELU_C * (u + GELU_A * u * u * u))
    slope = 0.5 * (1.0 + t) + 0.5 * u * (1.0 - t * t) * GELU_C * (1.0 + 3.0 * GELU_A * u * u)
    return dh * slope


def softmax(s):
    e = jnp.exp(s - jnp.max(s, axis=-1, keepdims=True))
    return e / jnp.sum(e, axis=-1, keepdims=True)


def softmax_backward(dp, soft, scale):
    inner = jnp.sum(dp * soft, axis=-1, keepdims=True)
    return (soft * (dp - inner) * scale).astype(BF16)


class Reducer:
    def __init__(self):
        n_items = lax.axis_size("items")
        self.count = n_items * lax.axis_size("blk")
        self.k = n_items.bit_length() - 1
        self.n_items = n_items

    def bit(self, name):
        if name == "y":
            return lax.axis_index("blk")
        return (lax.axis_index("items") >> name) & 1

    def exchange(self, x, name):
        if name == "y":
            return lax.ppermute(x, "blk", [(0, 1), (1, 0)])
        return lax.ppermute(x, "items", [(i, i ^ (1 << name)) for i in range(self.n_items)])

    def split(self, g):
        rows, width = g.shape
        return g.astype(BF16).reshape((2,) * (self.k + 1) + (rows // self.count, width))

    def reduce(self, grads, order):
        dims = list(range(self.k - 1, -1, -1)) + ["y"]
        parts = [self.split(g) for g in grads]
        heights = [p.shape[-2] for p in parts]
        for number, name in enumerate(order):
            axis = dims.index(name)
            mine = self.bit(name)
            send = [lax.dynamic_index_in_dim(p, 1 - mine, axis, keepdims=False) for p in parts]
            keep = [lax.dynamic_index_in_dim(p, mine, axis, keepdims=False) for p in parts]
            if number == 0:
                send = [jnp.concatenate(send, axis=-2)] if len(send) > 1 else send
                keep = [jnp.concatenate(keep, axis=-2)] if len(keep) > 1 else keep
            got = self.exchange(send[0], name)
            total = keep[0].astype(F32) + got.astype(F32)
            last = number == len(order) - 1
            parts = [total if last else total.astype(BF16)]
            dims.pop(axis)
        out, at = [], 0
        for height in heights:
            out.append(parts[0][at : at + height])
            at += height
        return out


CHUNK = 256
LAG = 2
MESH = pl.DeviceIdType.MESH
STAGES = {
    "xy": ("c", "x", "y", "z0", "z1"),
    "yx": ("c", "y", "x", "z0", "z1"),
}
ITEM_BIT = {"c": 0, "x": 1, "z0": 2, "z1": 3}


def padded_rows(r):
    return -(-r // 16) * 16


def my_bit(name):
    if name == "y":
        return lax.axis_index("blk")
    return (lax.axis_index("items") // 2 ** ITEM_BIT[name]) % 2


def partner(name):
    if name == "y":
        return {"blk": 1 - lax.axis_index("blk")}
    return {"items": lax.axis_index("items") + (1 - 2 * my_bit(name)) * 2 ** ITEM_BIT[name]}


def divide(first, second, mine, r, by_rows):
    if by_rows:
        first, second = (
            jnp.concatenate([first[:r], second[:r]], axis=0),
            jnp.concatenate([first[r:], second[r:]], axis=0),
        )
    return jnp.where(mine == 0, first, second), jnp.where(mine == 0, second, first)


def tie(values, after):
    count = len(values)
    anywhere = pl.BlockSpec(memory_space=pl.ANY)
    return pl.pallas_call(
        lambda *refs: None,
        out_shape=[jax.ShapeDtypeStruct(v.shape, v.dtype) for v in values],
        in_specs=[anywhere] * (count + len(after)),
        out_specs=[anywhere] * count,
        input_output_aliases={i: i for i in range(count)},
    )(*values, *after)


class Chunk:
    def __init__(self, bufs, at, sems, r, width, order):
        self.rc, self.r1, self.r2, self.r3, self.s4, self.r4, self.out = [b.at[at] for b in bufs]
        self.send, self.recv, self.at = sems[0], sems[1], at
        self.r, self.width, self.order = r, width, order
        self.step = 256 if r <= 40 and width % 256 == 0 else 128

    def copy(self, stage, source=None):
        src, dst = (
            (source, self.rc),
            (self.rc.at[:, :, 1], self.r1),
            (self.rc.at[:, 1, 0], self.r2),
            (self.rc.at[1, 0, 0], self.r3),
            (self.s4, self.r4),
        )[stage]
        return pltpu.make_async_remote_copy(
            src_ref=dst if src is None else src,
            dst_ref=dst,
            send_sem=self.send.at[self.at, stage],
            recv_sem=self.recv.at[self.at, stage],
            device_id=partner(STAGES[self.order][stage]),
            device_id_type=MESH,
        )

    def loop(self, pairs, body):
        columns = self.width // self.step

        def run(i, carry):
            body(i // columns, pl.ds(pl.multiple_of((i % columns) * self.step, self.step), self.step))
            return carry

        lax.fori_loop(0, pairs * columns, run, 0)

    def advance(self, stage, loaded=None):
        self.copy(stage).wait_recv()
        names = STAGES[self.order]
        r, kind, rc = self.r, self.rc.dtype, self.rc
        mine = my_bit(names[stage + 1]) if stage < 4 else None

        def total(a, b):
            return a.astype(F32) + b.astype(F32)

        def stage0(p, cols):
            q, z = p // 2, p % 2
            first = total(rc[q, z, 0, :, cols], loaded[q, z, 0, :, cols])
            second = total(rc[q, z, 1, :, cols], loaded[q, z, 1, :, cols])
            keep, send = divide(first, second, mine, r, names[1] == "y")
            rc[q, z, 0, :, cols] = keep.astype(kind)
            rc[q, z, 1, :, cols] = send.astype(kind)

        def stage1(q, cols):
            first = total(rc[q, 0, 0, :, cols], self.r1[q, 0, :, cols])
            second = total(rc[q, 1, 0, :, cols], self.r1[q, 1, :, cols])
            keep, send = divide(first, second, mine, r, True)
            rc[q, 0, 0, :, cols] = keep.astype(kind)
            rc[q, 1, 0, :, cols] = send.astype(kind)

        def stage2(q, cols):
            first = total(rc[0, 0, 0, :, cols], self.r2[0, :, cols])
            second = total(rc[1, 0, 0, :, cols], self.r2[1, :, cols])
            keep, send = divide(first, second, mine, r, True)
            rc[0, 0, 0, :, cols] = keep.astype(kind)
            rc[1, 0, 0, :, cols] = send.astype(kind)

        def stage3(q, cols):
            both = total(rc[0, 0, 0, :, cols], self.r3[:, cols])
            keep = jnp.where(mine == 0, both[:r], both[r:])
            send = jnp.where(mine == 0, both[r:], both[:r])
            extra = padded_rows(r) - r
            if extra:
                send = jnp.concatenate([send, jnp.zeros((extra, send.shape[1]), F32)], axis=0)
            self.s4[:, cols] = send.astype(kind)
            self.out[:, cols] = keep

        def stage4(q, cols):
            self.out[:, cols] = self.out[:, cols] + self.r4[:, cols].astype(F32)[:r]

        self.loop((4, 2, 1, 1, 1)[stage], (stage0, stage1, stage2, stage3, stage4)[stage])
        if stage < 4:
            self.copy(stage + 1).start()


def when(condition, action):
    if isinstance(condition, bool):
        if condition:
            action()
    else:
        pl.when(condition)(action)


SLOTS = 4
AHEAD = 3
B_SLOTS = 3


def reduce_kernel(plan, *refs):
    sides, steps, n_act, n_cot, widths, others = plan
    n_a, n_o = len(widths), len(others)
    acts, refs = refs[:n_act], refs[n_act:]
    cots, refs = refs[:n_cot], refs[n_cot:]
    o_src, refs = refs[:n_o], refs[n_o:]
    a_out, o_out = refs[:n_a], refs[n_a : n_a + n_o]
    refs = refs[n_a + n_o :]
    a_bufs, refs = refs[:7], refs[7:]
    act_in, act_t, cot_in, made = refs[:4]
    refs = refs[4:]
    o_bufs, refs = [refs[8 * i : 8 * i + 8] for i in range(n_o)], refs[8 * n_o :]
    a_sems, o_sems = refs[0:2], refs[2:4]
    act_sem, cot_sem, o_load_sem, a_out_sem, o_out_sem = refs[4:]
    core = my_bit("c")
    rows = act_t.shape[1] // 4

    barrier = pltpu.get_barrier_semaphore()
    for name in ("c", "x", "y", "z0", "z1"):
        pl.semaphore_signal(barrier, inc=1, device_id=partner(name), device_id_type=MESH)
    pl.semaphore_wait(barrier, 5)

    def chunk(step, side):
        return Chunk(a_bufs, 2 * step + side, a_sems, 40, CHUNK, ("xy", "yx")[side])

    def act_copy(side, group):
        return pltpu.make_async_copy(acts[sides[side][0][group][1]], act_in.at[side], act_sem.at[side])

    def cot_copy(side, step):
        source, number, _ = sides[side][1][step]
        slot = step % B_SLOTS
        return pltpu.make_async_copy(
            cots[source].at[:, pl.ds(number * CHUNK, CHUNK)], cot_in.at[side, slot], cot_sem.at[side, slot]
        )

    def first_copy(step, side):
        return chunk(step, side).copy(0, made.at[side, step % SLOTS, 1 - core])

    def produce(step):
        for side in range(2):
            groups = sides[side][0]
            for g, (start, _) in enumerate(groups):

                def fresh(g=g, side=side, groups=groups):
                    act_copy(side, g).wait()

                    def turn(i, carry):
                        at = pl.ds(pl.multiple_of(i * 256, 256), 256)
                        act_t[side, at, :] = act_in[side, :, at].T
                        return carry

                    lax.fori_loop(0, act_in.shape[2] // 256, turn, 0)
                    if g + 1 < len(groups):
                        act_copy(side, g + 1).start()

                when(step == start, fresh)
            for later in range(B_SLOTS - 1, steps):
                when(step == later - (B_SLOTS - 1), lambda later=later, side=side: cot_copy(side, later).start())
            slot = step % B_SLOTS
            pltpu.make_async_copy(
                cots[0].at[:, pl.ds(0, CHUNK)], cot_in.at[side, slot], cot_sem.at[side, slot]
            ).wait()
            when(step >= SLOTS, lambda side=side: first_copy(step - SLOTS, side).wait_send())

            def product(i, carry, side=side, slot=slot):
                part = act_t[side, pl.ds(pl.multiple_of(i * rows, rows), rows), :]
                result = jnp.dot(part, cot_in[side, slot], preferred_element_type=F32)
                height = rows // 4
                for x in range(2):
                    for c in range(2):
                        at = (2 * x + c) * height
                        made[side, step % SLOTS, c, i // 2, i % 2, x] = result[at : at + height].astype(BF16)
                return carry

            lax.fori_loop(0, 4, product, 0)
            first_copy(step, side).start()

    small = []
    for i, (r, width, order) in enumerate(others):
        item = Chunk([b.at[0:1] for b in o_bufs[i][:7]], 0, o_sems, r, width, order)
        item.at = i
        small.append(item)
        item.copy(0, o_src[i].at[:, :, :, 1 - core]).start()
        pltpu.make_async_copy(o_src[i].at[:, :, :, core], o_bufs[i][7], o_load_sem.at[i]).start()
    for side in range(2):
        act_copy(side, 0).start()
        for step in range(B_SLOTS - 1):
            cot_copy(side, step).start()

    def begin(step, carry):
        produce(step)
        return carry

    lax.fori_loop(0, AHEAD, begin, 0)
    for i, item in enumerate(small):
        pltpu.make_async_copy(o_src[i].at[:, :, :, core], o_bufs[i][7], o_load_sem.at[i]).wait()
        item.advance(0, o_bufs[i][7])

    def run(step, carry):
        pl.when(step + AHEAD < steps)(lambda: produce(step + AHEAD))

        def enter():
            for side in range(2):
                chunk(step, side).advance(0, made.at[side, step % SLOTS, core])

        pl.when(step < steps)(enter)
        for stage in range(4, 0, -1):
            old = step - stage * LAG

            def act(old=old, stage=stage):
                for side in range(2):
                    chunk(old, side).advance(stage)

            pl.when(jnp.logical_and(old >= 0, old < steps))(act)
        for number in range(4):

            def others_on(number=number):
                for item in small:
                    item.advance(number + 1)

            pl.when(step == 4 + 5 * number)(others_on)
        return carry

    lax.fori_loop(0, steps + 4 * LAG, run, 0)

    outs = []
    for side in range(2):
        for step in range(steps):
            _, number, target = sides[side][1][step]
            at = 2 * step + side
            outs.append(
                pltpu.make_async_copy(
                    a_bufs[6].at[at], a_out[target].at[:, pl.ds(number * CHUNK, CHUNK)], a_out_sem.at[at]
                )
            )
    for i in range(n_o):
        outs.append(pltpu.make_async_copy(o_bufs[i][6].at[0], o_out[i], o_out_sem.at[i]))
    for copy in outs:
        copy.start()
    for step in range(steps - SLOTS, steps):
        for side in range(2):
            first_copy(step, side).wait_send()
    for i, item in enumerate(small):
        item.copy(0, o_src[i].at[:, :, :, 1 - core]).wait_send()
        for stage in range(1, 5):
            item.copy(stage).wait_send()

    def wait_sent(step, carry):
        for side in range(2):
            for stage in range(1, 5):
                chunk(step, side).copy(stage).wait_send()
        return carry

    lax.fori_loop(0, steps, wait_sent, 0)
    for copy in outs:
        copy.wait()


def buffers(count, r, width, kind):
    rp = padded_rows(r)
    return [
        pltpu.VMEM((count, 2, 2, 2, 2 * r, width), kind),
        pltpu.VMEM((count, 2, 2, 2 * r, width), kind),
        pltpu.VMEM((count, 2, 2 * r, width), kind),
        pltpu.VMEM((count, 2 * r, width), kind),
        pltpu.VMEM((count, rp, width), kind),
        pltpu.VMEM((count, rp, width), kind),
        pltpu.VMEM((count, r, width), F32),
    ]


def reduce_all(products, others):
    acts, cots, sides, widths = [], [], [], []
    for side in products:
        groups, sequence = [], []
        for act, own in side:
            groups.append((len(sequence), len(acts)))
            acts.append(act)
            for cot in own:
                for number in range(cot.shape[1] // CHUNK):
                    sequence.append((len(cots), number, len(widths)))
                cots.append(cot)
                widths.append(cot.shape[1])
        sides.append((tuple(groups), tuple(sequence)))
    steps = len(sides[0][1])
    assert steps == len(sides[1][1])

    def view(g):
        return g.reshape(2, 2, 2, 2, g.shape[0] // 16, g.shape[1])

    plan = (
        tuple(sides), steps, len(acts), len(cots), tuple(widths),
        tuple((g.shape[0] // 32, g.shape[1], order) for g, order in others),
    )
    depth, features = acts[0].shape
    scratch = buffers(2 * steps, 40, CHUNK, BF16)
    scratch += [
        pltpu.VMEM((2, depth, features), BF16),
        pltpu.VMEM((2, features, depth), BF16),
        pltpu.VMEM((2, B_SLOTS, depth, CHUNK), BF16),
        pltpu.VMEM((2, SLOTS, 2, 2, 2, 2, 80, CHUNK), BF16),
    ]
    for g, order in others:
        r = g.shape[0] // 32
        scratch += buffers(1, r, g.shape[1], g.dtype)
        scratch.append(pltpu.VMEM((2, 2, 2, 2 * r, g.shape[1]), g.dtype))
    dma = pltpu.SemaphoreType.DMA
    scratch += [dma((2 * steps, 5)), dma((2 * steps, 5)), dma((len(others), 5)), dma((len(others), 5))]
    scratch += [dma((2,)), dma((2, B_SLOTS)), dma((len(others),)), dma((2 * steps,)), dma((len(others),))]
    anywhere = pl.BlockSpec(memory_space=pl.ANY)
    arrays = acts + cots + [view(g) for g, order in others]
    results = pl.pallas_call(
        lambda *refs: reduce_kernel(plan, *refs),
        out_shape=[jax.ShapeDtypeStruct((features // 32, w), F32) for w in widths]
        + [jax.ShapeDtypeStruct((g.shape[0] // 32, g.shape[1]), F32) for g, order in others],
        in_specs=[anywhere] * len(arrays),
        out_specs=[anywhere] * (len(widths) + len(others)),
        scratch_shapes=scratch,
        compiler_params=pltpu.CompilerParams(
            collective_id=0, has_side_effects=True, vmem_limit_bytes=62 * 1024 * 1024
        ),
    )(*arrays)
    return results[: len(widths)], results[len(widths) :]


def finish(plain, table, vectors, vocab, vector_count):
    count = len(plain)
    width = table.shape[0]

    def kernel(*refs):
        sources, refs = refs[:count], refs[count:]
        table_ref, vectors_ref = refs[:2]
        refs = refs[2:]
        targets, refs = refs[:count], refs[count:]
        emb_ref, row_refs, refs = refs[0], refs[1:5], refs[5:]
        gain_refs, refs = refs[:vector_count], refs[vector_count:]
        staged, (in_sem, out_sem) = refs[:count], refs[count:]
        inward = [pltpu.make_async_copy(sources[i], staged[i], in_sem.at[i]) for i in range(count)]
        outward = [pltpu.make_async_copy(staged[i], targets[i], out_sem.at[i]) for i in range(count)]
        for copy in inward:
            copy.start()
        turned = table_ref[...].T
        emb_ref[...] = table_ref[:, :vocab]
        vector_rows = vectors_ref[...].T
        for i, row_ref in enumerate(row_refs):
            row_ref[...] = turned[vocab + i]
        for i, gain_ref in enumerate(gain_refs):
            gain_ref[...] = vector_rows[i]
        for i in range(count):
            inward[i].wait()
            outward[i].start()
        for copy in outward:
            copy.wait()

    anywhere = pl.BlockSpec(memory_space=pl.ANY)
    local_memory = pl.BlockSpec(memory_space=pltpu.VMEM)
    shapes = [jax.ShapeDtypeStruct(p.shape, F32) for p in plain]
    shapes += [jax.ShapeDtypeStruct((width, vocab), F32)] + [jax.ShapeDtypeStruct((width,), F32)] * 4
    shapes += [jax.ShapeDtypeStruct(vectors.shape[:1], F32)] * vector_count
    results = pl.pallas_call(
        kernel,
        out_shape=shapes,
        in_specs=[anywhere] * count + [local_memory] * 2,
        out_specs=[anywhere] * count + [local_memory] * (5 + vector_count),
        scratch_shapes=[pltpu.VMEM(p.shape, F32) for p in plain] + [pltpu.SemaphoreType.DMA((count,))] * 2,
    )(*plain, table, vectors)
    return results[:count], results[count], results[count + 1 : count + 5], results[count + 5 :]


def center(x):
    hat = x - jnp.mean(x, axis=-1, keepdims=True)
    rstd = lax.rsqrt(jnp.mean(hat * hat, axis=-1, keepdims=True) + EPS)
    return hat * rstd, rstd


def center_backward(dhat, hat, rstd):
    first = jnp.mean(dhat, axis=-1, keepdims=True)
    second = jnp.mean(dhat * hat, axis=-1, keepdims=True)
    return rstd * (dhat - first - hat * second)


def lookup_kernel(scale, codes, table, position, gain, qk, nb, rstd_out, soft, p, pn, scores):
    i = pl.program_id(0)
    block = codes.shape[1]
    rows = pl.ds(pl.multiple_of(i * block, block), block)
    entry = lax.broadcasted_iota(jnp.int32, (table.shape[0], block), 0)
    onehot = (entry == codes[...]).astype(BF16)
    hat, rstd = center(nn(onehot.T, table[...]) + position[...].astype(F32))
    normed = (hat * gain[...].astype(F32)).astype(BF16)
    nb[rows, :] = normed
    rstd_out[...] = rstd
    scores[:, rows] = nt(qk[...], normed) * scale

    @pl.when(i == pl.num_programs(0) - 1)
    def _():
        soft[...] = softmax(scores[...])
        p[...] = soft[...].astype(BF16)
        pn[...] = nn(p[...], nb[...]).astype(BF16)


def bytes_forward(codes, table, position, gain, qk, scale):
    rows, width = position.shape
    latents, block = qk.shape[0], 256

    def whole(x):
        return pl.BlockSpec(x.shape, lambda i: (0, 0))

    shapes = [
        jax.ShapeDtypeStruct((rows, width), BF16),
        jax.ShapeDtypeStruct((rows, 1), F32),
        jax.ShapeDtypeStruct((latents, rows), F32),
        jax.ShapeDtypeStruct((latents, rows), BF16),
        jax.ShapeDtypeStruct((latents, width), BF16),
    ]
    specs = [whole(x) for x in shapes]
    specs[1] = pl.BlockSpec((block, 1), lambda i: (i, 0))
    return pl.pallas_call(
        lambda *refs: lookup_kernel(scale, *refs),
        grid=(rows // block,),
        out_shape=shapes,
        in_specs=[
            pl.BlockSpec((1, block), lambda i: (0, i)),
            whole(table),
            pl.BlockSpec((block, width), lambda i: (i, 0)),
            pl.BlockSpec((1, width), lambda i: (0, 0)),
            whole(qk),
        ],
        out_specs=specs,
        scratch_shapes=[pltpu.VMEM((latents, rows), F32)],
        compiler_params=pltpu.CompilerParams(vmem_limit_bytes=48 * 1024 * 1024),
    )(codes[None, :], table, position, gain[None, :], qk)


def bytes_kernel(
    at, scale, p, soft, vd, qk, nb, rstd, gain, codes, emb, sums, wide,
    pn, q, dae, daft, nl, rstd_l, gain_l, w_key, w_query,
    dbytes, table, turned, dq, g_key, g_value, g_latent,
    total, ds,
):
    i = pl.program_id(0)
    block = codes.shape[1]

    @pl.when(i == 0)
    def _():
        total[...] = jnp.zeros_like(total)
        total[: emb.shape[0]] = emb[...]
        total[at + 1 : at + 2] = sums[1:2]
        total[at + 2 : at + 3] = sums[0:1]
        ds[...] = softmax_backward(nt(vd[...], nb[...]), soft[...], scale)
        dn = nn(ds[...], nb[...]).astype(BF16)
        g_key[...] = nn(dn.T, q[...]).astype(BF16)
        g_value[...] = nn(pn[...].T, dae[...]).astype(BF16)
        dq[...] = nn(dn, w_key[...]).astype(BF16)
        dnl = nt(dq[...], w_query[...])
        g = gain_l[...].astype(F32)
        hat = nl[...].astype(F32) / g
        g_latent[...] = (daft[...] + center_backward(dnl * g, hat, rstd_l[...])).astype(BF16)
        first = jnp.sum(dnl * hat, axis=0, keepdims=True)
        own = lax.broadcasted_iota(jnp.int32, wide.shape, 0) == 0
        turned[...] = jnp.zeros_like(turned)
        turned[:, : wide.shape[0]] = jnp.where(own, first, wide[...]).T.astype(BF16)

    rows = pl.ds(pl.multiple_of(i * block, block), block)
    g = gain[...].astype(F32)
    normed = nb[rows, :]
    dnb = nn(p[...].T, vd[...]) + nn(ds[:, rows].T, qk[...])
    hat = normed.astype(F32) / g
    dx = center_backward(dnb * g, hat, rstd[...]).astype(BF16)
    dbytes[...] = dx
    entry = lax.broadcasted_iota(jnp.int32, (total.shape[0], block), 0)
    onehot = (entry == codes[...]).astype(BF16)
    total[...] += nn(onehot, dx)
    total[at : at + 1] += jnp.sum(dnb * hat, axis=0, keepdims=True)

    @pl.when(i == pl.num_programs(0) - 1)
    def _():
        table[...] = total[...].T.astype(BF16)


def bytes_backward(at, scale, p, soft, vd, qk, nb, rstd, gain, codes, emb, sums, wide, rest):
    rows, width = nb.shape
    latents, block, entries = p.shape[0], 256, -(-emb.shape[0] // 128) * 128
    features = wide.shape[1]
    qk_width = rest[1].shape[1]

    def whole(x):
        return pl.BlockSpec(x.shape, lambda i: (0, 0))

    shapes = [
        jax.ShapeDtypeStruct((rows, width), BF16),
        jax.ShapeDtypeStruct((width, entries), BF16),
        jax.ShapeDtypeStruct((features, 128), BF16),
        jax.ShapeDtypeStruct((latents, qk_width), BF16),
        jax.ShapeDtypeStruct((width, qk_width), BF16),
        jax.ShapeDtypeStruct((width, features), BF16),
        jax.ShapeDtypeStruct((latents, features), BF16),
    ]
    arrays = (p, soft, vd, qk, nb, rstd, gain[None, :], codes[None, :], emb, sums, wide) + rest
    specs = [whole(x) for x in arrays]
    specs[0] = pl.BlockSpec((latents, block), lambda i: (0, i))
    specs[5] = pl.BlockSpec((block, 1), lambda i: (i, 0))
    specs[7] = pl.BlockSpec((1, block), lambda i: (0, i))
    return pl.pallas_call(
        lambda *refs: bytes_kernel(at, scale, *refs),
        grid=(rows // block,),
        out_shape=shapes,
        in_specs=specs,
        out_specs=[pl.BlockSpec((block, width), lambda i: (i, 0))] + [whole(x) for x in shapes[1:]],
        scratch_shapes=[pltpu.VMEM((entries, width), F32), pltpu.VMEM((latents, rows), BF16)],
        compiler_params=pltpu.CompilerParams(vmem_limit_bytes=60 * 1024 * 1024),
    )(*arrays)


def head_columns(head, width):
    each = width // HEADS
    low, high = head * each // 128 * 128, -(-(head + 1) * each // 128) * 128
    place = low + lax.broadcasted_iota(jnp.int32, (1, high - low), 1)
    return slice(low, high), jnp.logical_and(place >= head * each, place < (head + 1) * each)


def pick(mask, x):
    return jnp.where(mask, x, jnp.zeros_like(x))


def head_softmax(head, q, k):
    columns, mask = head_columns(head, q.shape[1])
    scale = (q.shape[1] // HEADS) ** (-0.5)
    return softmax(nt(pick(mask, q[:, columns]), k[:, columns]) * scale), scale


def self_forward_heads(q, k, v, total):
    total[...] = jnp.zeros_like(total)
    for head in range(HEADS):
        p = head_softmax(head, q, k)[0].astype(BF16)
        columns, mask = head_columns(head, v.shape[1])
        total[:, columns] += nn(p, pick(mask, v[:, columns]))


def self_backward_heads(q, k, v, da, dq_sum, dk_sum, dv_sum):
    for ref in (dq_sum, dk_sum, dv_sum):
        ref[...] = jnp.zeros_like(ref)
    for head in range(HEADS):
        soft, scale = head_softmax(head, q, k)
        columns, mask = head_columns(head, v.shape[1])
        da_head = pick(mask, da[:, columns])
        ds = softmax_backward(nt(da_head, v[:, columns]), soft, scale)
        dv_sum[:, columns] += nn(soft.astype(BF16).T, da_head)
        columns, mask = head_columns(head, q.shape[1])
        dq_sum[:, columns] += nn(ds, pick(mask, k[:, columns]))
        dk_sum[:, columns] += nn(ds.T, pick(mask, q[:, columns]))


class Stream:
    def __init__(self, sources, targets, sem):
        self.copies = [pltpu.make_async_copy(a, b, sem.at[i]) for i, (a, b) in enumerate(zip(sources, targets))]
        self.targets, self.arrived = targets, set()
        for copy in self.copies:
            copy.start()

    def __getitem__(self, i):
        if i not in self.arrived:
            self.copies[i].wait()
            self.arrived.add(i)
        return self.targets[i][...]


class Results:
    def __init__(self, stage, targets, sem):
        self.stage, self.targets, self.sem, self.copies, self.left = stage, targets, sem, [], set()

    def put(self, value, over=None):
        i = len(self.copies)
        buffer = self.stage[i if over is None else over]
        if over is not None:
            self.copies[over].wait()
            self.left.add(over)
        buffer[...] = value.astype(buffer.dtype)
        copy = pltpu.make_async_copy(buffer, self.targets[i], self.sem.at[i])
        copy.start()
        self.copies.append(copy)
        return buffer

    def send(self, source):
        i = len(self.copies)
        copy = pltpu.make_async_copy(source, self.targets[i], self.sem.at[i])
        copy.start()
        self.copies.append(copy)

    def finish(self):
        for i, copy in enumerate(self.copies):
            if i not in self.left:
                copy.wait()


def streamed(body, small, large, shapes, extra, unstaged):
    n_s, n_l, n_o = len(small), len(large), len(shapes)

    def kernel(*refs):
        ins, refs = refs[: n_s + n_l], refs[n_s + n_l :]
        outs, refs = refs[:n_o], refs[n_o:]
        held, refs = refs[:n_l], refs[n_l:]
        kept, refs = list(refs[: n_o - len(unstaged)]), refs[n_o - len(unstaged) :]
        stage = [None if i in unstaged else kept.pop(0) for i in range(n_o)]
        stream = Stream(ins[n_s:], held, refs[0])
        results = Results(stage, outs, refs[1])
        body(ins[:n_s], stream, results, refs[2:])
        results.finish()

    anywhere = pl.BlockSpec(memory_space=pl.ANY)
    return pl.pallas_call(
        kernel,
        out_shape=shapes,
        in_specs=[pl.BlockSpec(memory_space=pltpu.VMEM)] * n_s + [anywhere] * n_l,
        out_specs=[anywhere] * n_o,
        scratch_shapes=[pltpu.VMEM(x.shape, x.dtype) for x in large]
        + [pltpu.VMEM(x.shape, x.dtype) for i, x in enumerate(shapes) if i not in unstaged]
        + [pltpu.SemaphoreType.DMA((n_l,)), pltpu.SemaphoreType.DMA((n_o,))]
        + extra,
        compiler_params=pltpu.CompilerParams(vmem_limit_bytes=63 * 1024 * 1024),
    )(*small, *large)


def middle_pass(latent, pn, gains, byte_gains, weights, scale):
    rows, width = latent.shape
    emb, queries, cot = weights[14:]
    entries, depth = emb.shape
    block = 256
    qk = weights[4].shape[1]

    def body(small, w, results, extra):
        latent_ref, pn_ref, g1, g2, g3, g4, gain_q, gain_f = small
        total, dq_sum, dk_sum, sums, u1, u2, q, k, v, k_d, v_d, kq, vo, vo_mid, g_pd, g_dn, g_emb, g_byte = extra
        put = results.put

        def norm(x, gain):
            hat, rstd = center(x)
            return put(hat * gain[...].astype(F32)), rstd

        a_e = put(nn(pn_ref[...], w[0]))
        x = latent_ref[...].astype(F32) + nn(a_e[...], w[1])
        n1, r1 = norm(x, g1)
        u1[...] = nn(n1[...], w[2])
        h1 = put(gelu_forward(u1[...]))
        x = x + nn(h1[...], w[3])
        n2, r2 = norm(x, g2)
        q[...] = nn(n2[...], w[4]).astype(BF16)
        k[...] = nn(n2[...], w[5]).astype(BF16)
        v[...] = nn(n2[...], w[6]).astype(BF16)
        self_forward_heads(q, k, v, total)
        a_s = put(total[...])
        x = x + nn(a_s[...], w[7])
        n3, r3 = norm(x, g3)
        u2[...] = nn(n3[...], w[8])
        h2 = put(gelu_forward(u2[...]))
        x = x + nn(h2[...], w[9])
        n4, r4 = norm(x, g4)
        k_d[...] = nn(n4[...], w[10]).astype(BF16)
        v_d[...] = nn(n4[...], w[11]).astype(BF16)

        w_query, w_out = w[12], w[13]
        kq[...] = nt(k_d[...], w_query).astype(BF16)
        out = nn(v_d[...], w_out)
        vo[...] = out.astype(BF16)
        vo_mid[...] = (out - jnp.mean(out, axis=0, keepdims=True)).astype(BF16)
        for ref in (g_pd, g_dn, g_emb, g_byte):
            ref[...] = jnp.zeros_like(ref)
        w[14], w[15], w[16]
        emb_ref, query_ref, cot_ref = w.targets[14:]

        def decode(i, carry):
            at = pl.ds(pl.multiple_of(i * block, block), block)
            x = query_ref[at, :].astype(F32)
            hat_q, rstd_q = center(x)
            gq, gf = gain_q[...].astype(F32), gain_f[...].astype(F32)
            nq = (hat_q * gq).astype(BF16)
            soft = softmax(nt(nq, kq[...]) * scale)
            p = soft.astype(BF16)
            hat_f, rstd_f = center(x + nn(p, vo[...]))
            nf = (hat_f * gf).astype(BF16)
            cot_part = cot_ref[:, at]
            dnf = nn(cot_part.T, emb_ref[...])
            g_emb[...] += nn(cot_part, nf)
            cot_ref[:, at] = nt(emb_ref[...], nf).astype(BF16)
            g_byte[0:1] += jnp.sum(dnf * hat_f, axis=0, keepdims=True)
            ddec = center_backward(dnf * gf, hat_f, rstd_f)
            ddec16 = ddec.astype(BF16)
            g_pd[...] += nn(p.T, ddec16)
            ds = softmax_backward(nt(ddec16, vo_mid[...]), soft, scale)
            g_dn[...] += nn(ds.T, nq)
            dnq = nn(ds, kq[...])
            g_byte[1:2] += jnp.sum(dnq * hat_q, axis=0, keepdims=True)
            query_ref[at, :] = (ddec + center_backward(dnq * gq, hat_q, rstd_q)).astype(BF16)
            return carry

        lax.fori_loop(0, queries.shape[0] // block, decode, 0)
        results.send(query_ref)
        results.send(cot_ref)
        results.send(g_emb)
        results.send(g_byte)
        pd, dn = g_pd[...].astype(BF16), g_dn[...].astype(BF16)
        dk_d = nn(dn, w.targets[12][...]).astype(BF16)
        dv_d = nt(pd, w.targets[13][...]).astype(BF16)
        put(dk_d)
        put(dv_d)
        put(nn(dn.T, k_d[...]))
        put(nn(v_d[...].T, pd))

        sums[...] = jnp.zeros_like(sums)

        def back(dy, normed, rstd, gain, row):
            g = gain[...].astype(F32)
            hat = normed[...].astype(F32) / g
            sums[row : row + 1] = jnp.sum(dy * hat, axis=0, keepdims=True)
            return center_backward(dy * g, hat, rstd)

        dlat = back(nt(dk_d, w[10]) + nt(dv_d, w[11]), n4, r4, g4, 4)
        dlat16 = put(dlat, 0)
        du2 = put(gelu_backward(nt(dlat16[...], w[9]), u2[...]), 2)
        das = dlat + back(nt(du2[...], w[8]), n3, r3, g3, 3)
        das16 = put(das, 4)
        da = nt(das16[...], w[7]).astype(BF16)
        self_backward_heads(q, k, v, da, dq_sum, dk_sum, total)
        dq, dk, dv = put(dq_sum[...]), put(dk_sum[...]), put(total[...], 6)
        dn2 = nt(dq[...], w[4]) + nt(dk[...], w[5]) + nt(dv[...], w[6])
        denc = das + back(dn2, n2, r2, g2, 2)
        denc16 = put(denc, 7)
        du1 = put(gelu_backward(nt(denc16[...], w[3]), u1[...]), 5)
        daft = denc + back(nt(du1[...], w[2]), n1, r1, g1, 1)
        daft16 = put(daft, 3)
        u1[...] = daft
        results.send(u1)
        dae = put(nt(daft16[...], w[1]), 1)
        put(nt(dae[...], w[0]))
        results.send(sums)

    wide = (rows, width)

    def low(*shape):
        return jax.ShapeDtypeStruct(shape, BF16)

    def full(*shape):
        return jax.ShapeDtypeStruct(shape, F32)

    shapes = [low(*wide)] * 8
    shapes += [low(*queries.shape), low(*cot.shape), full(entries, depth), full(8, depth)]
    shapes += [low(rows, qk), low(rows, depth), low(depth, qk), low(depth, depth)]
    shapes += [low(*wide)] * 3 + [low(rows, qk)] * 2 + [low(*wide)] * 4
    shapes += [full(*wide), low(*wide), low(rows, depth), full(8, width)]
    unstaged = {8, 9, 10, 11, 16, 17, 18, 21, 22, 23, 24, 25, 26, 28}
    vmem = pltpu.VMEM
    extra = [vmem(wide, F32), vmem((rows, qk), F32), vmem((rows, qk), F32), vmem((8, width), F32)]
    extra += [vmem(wide, F32)] * 2 + [vmem((rows, qk), BF16)] * 2 + [vmem(wide, BF16)]
    extra += [vmem((rows, qk), BF16)] + [vmem((rows, depth), BF16)] * 4 + [vmem((rows, depth), F32)] * 2
    extra += [vmem((entries, depth), F32), vmem((8, depth), F32)]
    small = [latent, pn] + [g[None, :] for g in gains + byte_gains]
    return streamed(body, small, weights, shapes, extra, unstaged)


def local(
    byte_ids, span_start, span_len, embedding, position, mask_vector, gain_bytes, key_enc,
    value_enc, latent_init, gain_latent, query_enc, out_enc, gain_enc_mlp, up_enc, down_enc,
    gain_self, query_self, key_self, value_self, out_self, gain_self_mlp, up_self, down_self,
    gain_dec_kv, key_dec, value_dec, dec_query, gain_dec_q, query_dec, out_dec, gain_final,
    logit_cot,
):
    me = lax.axis_index("blk")
    half = byte_ids.shape[1]
    total = position.shape[0]
    vocab = embedding.shape[0]
    reducer = Reducer()
    k = reducer.k
    order_yx = [0, "y", 1] + list(range(2, k))
    order_xy = [0, 1, "y"] + list(range(2, k))

    def swap(x):
        return lax.ppermute(x, "blk", [(0, 1), (1, 0)])

    def own_item(first, second, after=()):
        mine = jnp.where(me == 0, first, second)
        send = jnp.where(me == 0, second, first)
        if after:
            (send,) = tie([send], after)
        got = swap(send)
        low_half = jnp.where(me == 0, mine, got)
        high_half = jnp.where(me == 0, got, mine)
        return jnp.concatenate([low_half, high_half], axis=-1)

    ids = own_item(byte_ids[0], byte_ids[1])
    cot_rows = logit_cot.transpose(2, 0, 1)
    cot = own_item(cot_rows[:, 0], cot_rows[:, 1], [ids])
    entries = -(-(vocab + 4) // 16) * 16
    cot = jnp.pad(cot, ((0, entries - vocab), (0, 0)))
    emb_rows = jnp.pad(embedding, ((0, entries - vocab), (0, 0)))
    starts = lax.dynamic_index_in_dim(span_start, me, 0, keepdims=False)
    lengths = lax.dynamic_index_in_dim(span_len, me, 0, keepdims=False)

    places = lax.iota(jnp.int32, total)
    inside = (places[None, :] >= starts[:, None]) & (places[None, :] < (starts + lengths)[:, None])
    codes = jnp.where(jnp.any(inside, axis=0), vocab, ids)
    padded = -(-(vocab + 4) // 128) * 128
    table = jnp.concatenate(
        [embedding, mask_vector[None, :], jnp.zeros((padded - vocab - 1, embedding.shape[1]), BF16)], axis=0
    )

    latent32 = latent_init.astype(F32)
    nl, hat_l, rstd_l = norm_forward(latent32, gain_latent)
    q_e = nn(nl, query_enc).astype(BF16)
    scale_e = q_e.shape[1] ** (-0.5)
    qk_e = nt(q_e, key_enc).astype(BF16)
    nb, rstd_b, soft_e, p_e, pn_e = bytes_forward(codes, table, position, gain_bytes, qk_e, scale_e)

    gains = (gain_enc_mlp, gain_self, gain_self_mlp, gain_dec_kv)
    (
        a_e, n1, h1, n2, a_s, n3, h2, n4,
        g_dec_query, logits, g_emb_out, gain_sums, dk_d, dv_d, g_query_dec, g_out_dec,
        dlat16, du2, das16, dq_s, dk_s, dv_s, denc16, du1, daft16, dafter, dae16, vd_e, wide,
    ) = middle_pass(
        latent_init, pn_e, gains, (gain_dec_q, gain_final),
        [
            value_enc, out_enc, up_enc, down_enc, query_self, key_self, value_self, out_self, up_self,
            down_self, key_dec, value_dec, query_dec, out_dec, emb_rows, dec_query, cot,
        ],
        query_dec.shape[1] ** (-0.5),
    )
    logits = logits[:vocab]
    logits_got = swap(jnp.where(me == 0, logits[:, half:], logits[:, :half]))
    logits_own = jnp.where(me == 0, logits[:, :half], logits[:, half:])
    side = lax.broadcasted_iota(jnp.int32, (1, 2, 1), 1)
    logits_out = jnp.where(side == me, logits_own[:, None, :], logits_got[:, None, :]).transpose(1, 2, 0)

    dbytes, g_table, vectors, dq_e, g_key_enc, g_value_enc, g_latent = bytes_backward(
        vocab + 1, scale_e, p_e, soft_e, vd_e, qk_e, nb, rstd_b, gain_bytes, codes, g_emb_out, gain_sums, wide,
        (pn_e, q_e, dae16, dafter, nl, rstd_l, gain_latent[None, :], key_enc, query_enc),
    )

    def low(g):
        return g.astype(BF16)

    if reducer.n_items == 16:
        first_side = [(n1, [du1]), (a_e, [daft16]), (n3, [du2]), (n2, [dv_s, dk_s])]
        second_side = [
            (h1, [denc16]), (h2, [dlat16]), (a_s, [das16]), (n4, [dv_d, dk_d]), (n2, [dq_s]), (nl, [dq_e]),
        ]
        others = [
            (low(g_dec_query), "xy"), (low(dbytes), "yx"), (low(g_value_enc), "xy"), (low(g_out_dec), "yx"),
            (low(g_table), "yx"), (low(g_key_enc), "xy"), (low(g_query_dec), "yx"), (low(g_latent), "xy"),
            (low(vectors), "yx"),
        ]
        (
            r_up_enc, r_out_enc, r_up_self, r_value_self, r_key_self,
            r_down_enc, r_down_self, r_out_self, r_value_dec, r_key_dec, r_query_self, r_query_enc,
        ), (
            r_dec_query, r_position, r_value_enc, r_out_dec, r_emb, r_key_enc, r_query_dec, r_latent, r_vectors,
        ) = reduce_all((first_side, second_side), others)
    else:
        r_dec_query, r_out_dec, r_value_dec = reducer.reduce([g_dec_query, g_out_dec, tn(n4, dv_d)], order_yx)
        r_down_self, r_up_self, r_out_self = reducer.reduce(
            [tn(h2, dlat16), tn(n3, du2), tn(a_s, das16)], order_xy
        )
        r_value_self, r_down_enc = reducer.reduce([tn(n2, dv_s), tn(h1, denc16)], order_yx)
        r_up_enc, r_out_enc = reducer.reduce([tn(n1, du1), tn(a_e, daft16)], order_xy)
        r_query_dec, r_key_dec, r_query_self, r_key_self = reducer.reduce(
            [g_query_dec, tn(n4, dk_d), tn(n2, dq_s), tn(n2, dk_s)], order_xy
        )
        r_value_enc, r_latent = reducer.reduce([g_value_enc, g_latent], order_xy)
        (r_position,) = reducer.reduce([dbytes], order_yx)
        r_key_enc, r_query_enc = reducer.reduce([g_key_enc, tn(nl, dq_e)], order_yx)
        (r_emb,) = reducer.reduce([g_table], order_yx)
        (r_vectors,) = reducer.reduce([vectors], order_xy)

    plain = [
        r_position, r_key_enc, r_value_enc, r_latent, r_query_enc, r_out_enc, r_up_enc, r_down_enc,
        r_query_self, r_key_self, r_value_self, r_out_self, r_up_self, r_down_self, r_key_dec, r_value_dec,
        r_dec_query, r_query_dec, r_out_dec,
    ]
    plain, r_embedding, (r_mask, r_gain_bytes, r_gain_dec_q, r_gain_final), gains = finish(plain, r_emb, r_vectors, vocab, 1 + len(gains))
    (
        r_position, r_key_enc, r_value_enc, r_latent, r_query_enc, r_out_enc, r_up_enc, r_down_enc,
        r_query_self, r_key_self, r_value_self, r_out_self, r_up_self, r_down_self, r_key_dec, r_value_dec,
        r_dec_query, r_query_dec, r_out_dec,
    ) = plain
    (
        r_gain_latent, r_gain_enc_mlp, r_gain_self, r_gain_self_mlp, r_gain_dec_kv,
    ) = gains
    return (
        logits_out, r_embedding.T, r_position, r_mask, r_gain_bytes, r_key_enc, r_value_enc,
        r_latent, r_gain_latent, r_query_enc, r_out_enc, r_gain_enc_mlp, r_up_enc, r_down_enc, r_gain_self,
        r_query_self, r_key_self, r_value_self, r_out_self, r_gain_self_mlp, r_up_self, r_down_self,
        r_gain_dec_kv, r_key_dec, r_value_dec, r_dec_query, r_gain_dec_q, r_query_dec, r_out_dec, r_gain_final,
    )


def solution(mesh):
    split = P("items", "blk")
    rows = P(("items", "blk"))
    outs = [P("items", "blk", None), P(None, ("items", "blk"))] + [rows] * 28
    return jax.shard_map(
        local,
        mesh=mesh,
        in_specs=(split, P("items", None), P("items", None)) + (P(),) * 29 + (P("items", "blk", None),),
        out_specs=tuple(outs),
        check_vma=False,
    )
```

```python
import jax
import jax.numpy as jnp
from jax import lax
from jax.experimental import pallas as pl
from jax.experimental.pallas import tpu as pltpu
from jax.sharding import PartitionSpec as P

HEADS = 8
EPS = 1e-05
F32 = jnp.float32
BF16 = jnp.bfloat16
GELU_C = 0.7978845608028654
GELU_A = 0.044715


def nn(a, b):
    return lax.dot_general(a, b, (((1,), (0,)), ((), ())), preferred_element_type=F32)


def nt(a, b):
    return lax.dot_general(a, b, (((1,), (1,)), ((), ())), preferred_element_type=F32)


def tn(a, b):
    return lax.dot_general(a, b, (((0,), (0,)), ((), ())), preferred_element_type=F32)


def norm_forward(x, gain):
    centered = x - jnp.mean(x, axis=-1, keepdims=True)
    variance = jnp.mean(centered * centered, axis=-1, keepdims=True)
    rstd = lax.rsqrt(variance + EPS)
    hat = centered * rstd
    return (hat * gain.astype(F32)).astype(BF16), hat, rstd


def norm_backward(dy, hat, rstd, gain):
    dgain = jnp.sum(dy * hat, axis=0, keepdims=True)
    dhat = dy * gain.astype(F32)
    first = jnp.mean(dhat, axis=-1, keepdims=True)
    second = jnp.mean(dhat * hat, axis=-1, keepdims=True)
    return rstd * (dhat - first - hat * second), dgain


def gelu_forward(u):
    t = jnp.tanh(GELU_C * (u + GELU_A * u * u * u))
    return (0.5 * u * (1.0 + t)).astype(BF16)


def gelu_backward(dh, u):
    t = jnp.tanh(GELU_C * (u + GELU_A * u * u * u))
    slope = 0.5 * (1.0 + t) + 0.5 * u * (1.0 - t * t) * GELU_C * (1.0 + 3.0 * GELU_A * u * u)
    return dh * slope


def softmax(s):
    e = jnp.exp(s - jnp.max(s, axis=-1, keepdims=True))
    return e * (1.0 / jnp.sum(e, axis=-1, keepdims=True))


def softmax_backward(dp, soft, scale):
    inner = jnp.sum(dp * soft, axis=-1, keepdims=True)
    return (soft * (dp - inner) * scale).astype(BF16)


class Reducer:
    def __init__(self):
        n_items = lax.axis_size("items")
        self.count = n_items * lax.axis_size("blk")
        self.k = n_items.bit_length() - 1
        self.n_items = n_items

    def bit(self, name):
        if name == "y":
            return lax.axis_index("blk")
        return (lax.axis_index("items") >> name) & 1

    def exchange(self, x, name):
        if name == "y":
            return lax.ppermute(x, "blk", [(0, 1), (1, 0)])
        return lax.ppermute(x, "items", [(i, i ^ (1 << name)) for i in range(self.n_items)])

    def split(self, g):
        rows, width = g.shape
        return g.astype(BF16).reshape((2,) * (self.k + 1) + (rows // self.count, width))

    def reduce(self, grads, order):
        dims = list(range(self.k - 1, -1, -1)) + ["y"]
        parts = [self.split(g) for g in grads]
        heights = [p.shape[-2] for p in parts]
        for number, name in enumerate(order):
            axis = dims.index(name)
            mine = self.bit(name)
            send = [lax.dynamic_index_in_dim(p, 1 - mine, axis, keepdims=False) for p in parts]
            keep = [lax.dynamic_index_in_dim(p, mine, axis, keepdims=False) for p in parts]
            if number == 0:
                send = [jnp.concatenate(send, axis=-2)] if len(send) > 1 else send
                keep = [jnp.concatenate(keep, axis=-2)] if len(keep) > 1 else keep
            got = self.exchange(send[0], name)
            total = keep[0].astype(F32) + got.astype(F32)
            last = number == len(order) - 1
            parts = [total if last else total.astype(BF16)]
            dims.pop(axis)
        out, at = [], 0
        for height in heights:
            out.append(parts[0][at : at + height])
            at += height
        return out


CHUNK = 256
LAG = 2
MESH = pl.DeviceIdType.MESH
STAGES = {
    "xy": ("c", "x", "y", "z0", "z1"),
    "yx": ("c", "y", "x", "z0", "z1"),
}
ITEM_BIT = {"c": 0, "x": 1, "z0": 2, "z1": 3}


def padded_rows(r):
    return -(-r // 16) * 16


def my_bit(name):
    if name == "y":
        return lax.axis_index("blk")
    return (lax.axis_index("items") // 2 ** ITEM_BIT[name]) % 2


def partner(name):
    if name == "y":
        return {"blk": 1 - lax.axis_index("blk")}
    return {"items": lax.axis_index("items") + (1 - 2 * my_bit(name)) * 2 ** ITEM_BIT[name]}


def divide(first, second, mine, r, by_rows):
    if by_rows:
        first, second = (
            jnp.concatenate([first[:r], second[:r]], axis=0),
            jnp.concatenate([first[r:], second[r:]], axis=0),
        )
    return jnp.where(mine == 0, first, second), jnp.where(mine == 0, second, first)


def tie(values, after):
    count = len(values)
    anywhere = pl.BlockSpec(memory_space=pl.ANY)
    return pl.pallas_call(
        lambda *refs: None,
        out_shape=[jax.ShapeDtypeStruct(v.shape, v.dtype) for v in values],
        in_specs=[anywhere] * (count + len(after)),
        out_specs=[anywhere] * count,
        input_output_aliases={i: i for i in range(count)},
    )(*values, *after)


class Chunk:
    def __init__(self, bufs, at, sems, r, width, order):
        self.rc, self.r1, self.r2, self.r3, self.s4, self.r4, self.out = [b.at[at] for b in bufs]
        self.send, self.recv, self.at = sems[0], sems[1], at
        self.r, self.width, self.order = r, width, order
        self.step = 256 if r <= 40 and width % 256 == 0 else 128

    def copy(self, stage, source=None):
        src, dst = (
            (source, self.rc),
            (self.rc.at[:, :, 1], self.r1),
            (self.rc.at[:, 1, 0], self.r2),
            (self.rc.at[1, 0, 0], self.r3),
            (self.s4, self.r4),
        )[stage]
        return pltpu.make_async_remote_copy(
            src_ref=dst if src is None else src,
            dst_ref=dst,
            send_sem=self.send.at[self.at, stage],
            recv_sem=self.recv.at[self.at, stage],
            device_id=partner(STAGES[self.order][stage]),
            device_id_type=MESH,
        )

    def loop(self, pairs, body):
        columns = self.width // self.step

        def run(i, carry):
            body(i // columns, pl.ds(pl.multiple_of((i % columns) * self.step, self.step), self.step))
            return carry

        lax.fori_loop(0, pairs * columns, run, 0)

    def advance(self, stage, loaded=None):
        self.copy(stage).wait_recv()
        names = STAGES[self.order]
        r, kind, rc = self.r, self.rc.dtype, self.rc
        mine = my_bit(names[stage + 1]) if stage < 4 else None

        def total(a, b):
            return a.astype(F32) + b.astype(F32)

        def stage0(p, cols):
            q, z = p // 2, p % 2
            first = total(rc[q, z, 0, :, cols], loaded[q, z, 0, :, cols])
            second = total(rc[q, z, 1, :, cols], loaded[q, z, 1, :, cols])
            keep, send = divide(first, second, mine, r, names[1] == "y")
            rc[q, z, 0, :, cols] = keep.astype(kind)
            rc[q, z, 1, :, cols] = send.astype(kind)

        def stage1(q, cols):
            first = total(rc[q, 0, 0, :, cols], self.r1[q, 0, :, cols])
            second = total(rc[q, 1, 0, :, cols], self.r1[q, 1, :, cols])
            keep, send = divide(first, second, mine, r, True)
            rc[q, 0, 0, :, cols] = keep.astype(kind)
            rc[q, 1, 0, :, cols] = send.astype(kind)

        def stage2(q, cols):
            first = total(rc[0, 0, 0, :, cols], self.r2[0, :, cols])
            second = total(rc[1, 0, 0, :, cols], self.r2[1, :, cols])
            keep, send = divide(first, second, mine, r, True)
            rc[0, 0, 0, :, cols] = keep.astype(kind)
            rc[1, 0, 0, :, cols] = send.astype(kind)

        def stage3(q, cols):
            both = total(rc[0, 0, 0, :, cols], self.r3[:, cols])
            keep = jnp.where(mine == 0, both[:r], both[r:])
            send = jnp.where(mine == 0, both[r:], both[:r])
            extra = padded_rows(r) - r
            if extra:
                send = jnp.concatenate([send, jnp.zeros((extra, send.shape[1]), F32)], axis=0)
            self.s4[:, cols] = send.astype(kind)
            self.out[:, cols] = keep

        def stage4(q, cols):
            self.out[:, cols] = self.out[:, cols] + self.r4[:, cols].astype(F32)[:r]

        self.loop((4, 2, 1, 1, 1)[stage], (stage0, stage1, stage2, stage3, stage4)[stage])
        if stage < 4:
            self.copy(stage + 1).start()


def when(condition, action):
    if isinstance(condition, bool):
        if condition:
            action()
    else:
        pl.when(condition)(action)


SLOTS = 4
AHEAD = 3
B_SLOTS = 3


def reduce_kernel(plan, *refs):
    sides, steps, n_act, n_cot, widths, others = plan
    n_a, n_o = len(widths), len(others)
    acts, refs = refs[:n_act], refs[n_act:]
    cots, refs = refs[:n_cot], refs[n_cot:]
    o_src, refs = refs[:n_o], refs[n_o:]
    a_out, o_out = refs[:n_a], refs[n_a : n_a + n_o]
    refs = refs[n_a + n_o :]
    a_bufs, refs = refs[:7], refs[7:]
    act_in, act_t, cot_in, made = refs[:4]
    refs = refs[4:]
    o_bufs, refs = [refs[8 * i : 8 * i + 8] for i in range(n_o)], refs[8 * n_o :]
    a_sems, o_sems = refs[0:2], refs[2:4]
    act_sem, cot_sem, o_load_sem, a_out_sem, o_out_sem = refs[4:]
    core = my_bit("c")
    rows = act_t.shape[1] // 4

    barrier = pltpu.get_barrier_semaphore()
    for name in ("c", "x", "y", "z0", "z1"):
        pl.semaphore_signal(barrier, inc=1, device_id=partner(name), device_id_type=MESH)
    pl.semaphore_wait(barrier, 5)

    def chunk(step, side):
        return Chunk(a_bufs, 2 * step + side, a_sems, 40, CHUNK, ("xy", "yx")[side])

    def act_copy(side, group):
        return pltpu.make_async_copy(acts[sides[side][0][group][1]], act_in.at[side], act_sem.at[side])

    def cot_copy(side, step):
        source, number, _ = sides[side][1][step]
        slot = step % B_SLOTS
        return pltpu.make_async_copy(
            cots[source].at[:, pl.ds(number * CHUNK, CHUNK)], cot_in.at[side, slot], cot_sem.at[side, slot]
        )

    def first_copy(step, side):
        return chunk(step, side).copy(0, made.at[side, step % SLOTS, 1 - core])

    def produce(step):
        for side in range(2):
            groups = sides[side][0]
            for g, (start, _) in enumerate(groups):

                def fresh(g=g, side=side, groups=groups):
                    act_copy(side, g).wait()

                    def turn(i, carry):
                        at = pl.ds(pl.multiple_of(i * 256, 256), 256)
                        act_t[side, at, :] = act_in[side, :, at].T
                        return carry

                    lax.fori_loop(0, act_in.shape[2] // 256, turn, 0)
                    if g + 1 < len(groups):
                        act_copy(side, g + 1).start()

                when(step == start, fresh)
            for later in range(B_SLOTS - 1, steps):
                when(step == later - (B_SLOTS - 1), lambda later=later, side=side: cot_copy(side, later).start())
            slot = step % B_SLOTS
            pltpu.make_async_copy(
                cots[0].at[:, pl.ds(0, CHUNK)], cot_in.at[side, slot], cot_sem.at[side, slot]
            ).wait()
            when(step >= SLOTS, lambda side=side: first_copy(step - SLOTS, side).wait_send())

            def product(i, carry, side=side, slot=slot):
                part = act_t[side, pl.ds(pl.multiple_of(i * rows, rows), rows), :]
                result = jnp.dot(part, cot_in[side, slot], preferred_element_type=F32)
                height = rows // 4
                for x in range(2):
                    for c in range(2):
                        at = (2 * x + c) * height
                        made[side, step % SLOTS, c, i // 2, i % 2, x] = result[at : at + height].astype(BF16)
                return carry

            lax.fori_loop(0, 4, product, 0)
            first_copy(step, side).start()

    small = []
    for i, (r, width, order) in enumerate(others):
        item = Chunk([b.at[0:1] for b in o_bufs[i][:7]], 0, o_sems, r, width, order)
        item.at = i
        small.append(item)
        item.copy(0, o_src[i].at[:, :, :, 1 - core]).start()
        pltpu.make_async_copy(o_src[i].at[:, :, :, core], o_bufs[i][7], o_load_sem.at[i]).start()
    for side in range(2):
        act_copy(side, 0).start()
        for step in range(B_SLOTS - 1):
            cot_copy(side, step).start()

    def begin(step, carry):
        produce(step)
        return carry

    lax.fori_loop(0, AHEAD, begin, 0)
    for i, item in enumerate(small):
        pltpu.make_async_copy(o_src[i].at[:, :, :, core], o_bufs[i][7], o_load_sem.at[i]).wait()
        item.advance(0, o_bufs[i][7])

    def run(step, carry):
        pl.when(step + AHEAD < steps)(lambda: produce(step + AHEAD))

        def enter():
            for side in range(2):
                chunk(step, side).advance(0, made.at[side, step % SLOTS, core])

        pl.when(step < steps)(enter)
        for stage in range(4, 0, -1):
            old = step - stage * LAG

            def act(old=old, stage=stage):
                for side in range(2):
                    chunk(old, side).advance(stage)

            pl.when(jnp.logical_and(old >= 0, old < steps))(act)
        for number in range(4):

            def others_on(number=number):
                for item in small:
                    item.advance(number + 1)

            pl.when(step == 4 + 5 * number)(others_on)
        return carry

    lax.fori_loop(0, steps + 4 * LAG, run, 0)

    outs = []
    for side in range(2):
        for step in range(steps):
            _, number, target = sides[side][1][step]
            at = 2 * step + side
            outs.append(
                pltpu.make_async_copy(
                    a_bufs[6].at[at], a_out[target].at[:, pl.ds(number * CHUNK, CHUNK)], a_out_sem.at[at]
                )
            )
    for i in range(n_o):
        outs.append(pltpu.make_async_copy(o_bufs[i][6].at[0], o_out[i], o_out_sem.at[i]))
    for copy in outs:
        copy.start()
    for step in range(steps - SLOTS, steps):
        for side in range(2):
            first_copy(step, side).wait_send()
    for i, item in enumerate(small):
        item.copy(0, o_src[i].at[:, :, :, 1 - core]).wait_send()
        for stage in range(1, 5):
            item.copy(stage).wait_send()

    def wait_sent(step, carry):
        for side in range(2):
            for stage in range(1, 5):
                chunk(step, side).copy(stage).wait_send()
        return carry

    lax.fori_loop(0, steps, wait_sent, 0)
    for copy in outs:
        copy.wait()


def buffers(count, r, width, kind):
    rp = padded_rows(r)
    return [
        pltpu.VMEM((count, 2, 2, 2, 2 * r, width), kind),
        pltpu.VMEM((count, 2, 2, 2 * r, width), kind),
        pltpu.VMEM((count, 2, 2 * r, width), kind),
        pltpu.VMEM((count, 2 * r, width), kind),
        pltpu.VMEM((count, rp, width), kind),
        pltpu.VMEM((count, rp, width), kind),
        pltpu.VMEM((count, r, width), F32),
    ]


def reduce_all(products, others):
    acts, cots, sides, widths = [], [], [], []
    for side in products:
        groups, sequence = [], []
        for act, own in side:
            groups.append((len(sequence), len(acts)))
            acts.append(act)
            for cot in own:
                for number in range(cot.shape[1] // CHUNK):
                    sequence.append((len(cots), number, len(widths)))
                cots.append(cot)
                widths.append(cot.shape[1])
        sides.append((tuple(groups), tuple(sequence)))
    steps = len(sides[0][1])
    assert steps == len(sides[1][1])

    def view(g):
        return g.reshape(2, 2, 2, 2, g.shape[0] // 16, g.shape[1])

    plan = (
        tuple(sides), steps, len(acts), len(cots), tuple(widths),
        tuple((g.shape[0] // 32, g.shape[1], order) for g, order in others),
    )
    depth, features = acts[0].shape
    scratch = buffers(2 * steps, 40, CHUNK, BF16)
    scratch += [
        pltpu.VMEM((2, depth, features), BF16),
        pltpu.VMEM((2, features, depth), BF16),
        pltpu.VMEM((2, B_SLOTS, depth, CHUNK), BF16),
        pltpu.VMEM((2, SLOTS, 2, 2, 2, 2, 80, CHUNK), BF16),
    ]
    for g, order in others:
        r = g.shape[0] // 32
        scratch += buffers(1, r, g.shape[1], g.dtype)
        scratch.append(pltpu.VMEM((2, 2, 2, 2 * r, g.shape[1]), g.dtype))
    dma = pltpu.SemaphoreType.DMA
    scratch += [dma((2 * steps, 5)), dma((2 * steps, 5)), dma((len(others), 5)), dma((len(others), 5))]
    scratch += [dma((2,)), dma((2, B_SLOTS)), dma((len(others),)), dma((2 * steps,)), dma((len(others),))]
    anywhere = pl.BlockSpec(memory_space=pl.ANY)
    arrays = acts + cots + [view(g) for g, order in others]
    results = pl.pallas_call(
        lambda *refs: reduce_kernel(plan, *refs),
        out_shape=[jax.ShapeDtypeStruct((features // 32, w), F32) for w in widths]
        + [jax.ShapeDtypeStruct((g.shape[0] // 32, g.shape[1]), F32) for g, order in others],
        in_specs=[anywhere] * len(arrays),
        out_specs=[anywhere] * (len(widths) + len(others)),
        scratch_shapes=scratch,
        compiler_params=pltpu.CompilerParams(
            collective_id=0, has_side_effects=True, vmem_limit_bytes=62 * 1024 * 1024
        ),
    )(*arrays)
    return results[: len(widths)], results[len(widths) :]


def finish(plain, table, vectors, vocab, vector_count):
    count = len(plain)
    width = table.shape[0]

    def kernel(*refs):
        sources, refs = refs[:count], refs[count:]
        table_ref, vectors_ref = refs[:2]
        refs = refs[2:]
        targets, refs = refs[:count], refs[count:]
        emb_ref, row_refs, refs = refs[0], refs[1:5], refs[5:]
        gain_refs, refs = refs[:vector_count], refs[vector_count:]
        staged, (in_sem, out_sem) = refs[:count], refs[count:]
        inward = [pltpu.make_async_copy(sources[i], staged[i], in_sem.at[i]) for i in range(count)]
        outward = [pltpu.make_async_copy(staged[i], targets[i], out_sem.at[i]) for i in range(count)]
        for copy in inward:
            copy.start()
        turned = table_ref[...].T
        emb_ref[...] = table_ref[:, :vocab]
        vector_rows = vectors_ref[...].T
        for i, row_ref in enumerate(row_refs):
            row_ref[...] = turned[vocab + i]
        for i, gain_ref in enumerate(gain_refs):
            gain_ref[...] = vector_rows[i]
        for i in range(count):
            inward[i].wait()
            outward[i].start()
        for copy in outward:
            copy.wait()

    anywhere = pl.BlockSpec(memory_space=pl.ANY)
    local_memory = pl.BlockSpec(memory_space=pltpu.VMEM)
    shapes = [jax.ShapeDtypeStruct(p.shape, F32) for p in plain]
    shapes += [jax.ShapeDtypeStruct((width, vocab), F32)] + [jax.ShapeDtypeStruct((width,), F32)] * 4
    shapes += [jax.ShapeDtypeStruct(vectors.shape[:1], F32)] * vector_count
    results = pl.pallas_call(
        kernel,
        out_shape=shapes,
        in_specs=[anywhere] * count + [local_memory] * 2,
        out_specs=[anywhere] * count + [local_memory] * (5 + vector_count),
        scratch_shapes=[pltpu.VMEM(p.shape, F32) for p in plain] + [pltpu.SemaphoreType.DMA((count,))] * 2,
    )(*plain, table, vectors)
    return results[:count], results[count], results[count + 1 : count + 5], results[count + 5 :]


def center(x):
    hat = x - jnp.mean(x, axis=-1, keepdims=True)
    rstd = lax.rsqrt(jnp.mean(hat * hat, axis=-1, keepdims=True) + EPS)
    return hat * rstd, rstd


def center_backward(dhat, hat, rstd):
    first = jnp.mean(dhat, axis=-1, keepdims=True)
    second = jnp.mean(dhat * hat, axis=-1, keepdims=True)
    return rstd * (dhat - first - hat * second)


def lookup_kernel(scale, codes, table, position, gain, qk, nb, rstd_out, soft, p, pn, scores):
    i = pl.program_id(0)
    block = codes.shape[1]
    rows = pl.ds(pl.multiple_of(i * block, block), block)
    entry = lax.broadcasted_iota(jnp.int32, (table.shape[0], block), 0)
    onehot = (entry == codes[...]).astype(BF16)
    hat, rstd = center(nn(onehot.T, table[...]) + position[...].astype(F32))
    normed = (hat * gain[...].astype(F32)).astype(BF16)
    nb[rows, :] = normed
    rstd_out[...] = jnp.broadcast_to(rstd, (block, 128)).T[:1]
    scores[:, rows] = nt(qk[...], normed) * scale

    @pl.when(i == pl.num_programs(0) - 1)
    def _():
        soft[...] = softmax(scores[...])
        p[...] = soft[...].astype(BF16)
        pn[...] = nn(p[...], nb[...]).astype(BF16)


def bytes_forward(codes, table, position, gain, qk, scale):
    rows, width = position.shape
    latents, block = qk.shape[0], 256

    def whole(x):
        return pl.BlockSpec(x.shape, lambda i: (0, 0))

    shapes = [
        jax.ShapeDtypeStruct((rows, width), BF16),
        jax.ShapeDtypeStruct((1, rows), F32),
        jax.ShapeDtypeStruct((latents, rows), F32),
        jax.ShapeDtypeStruct((latents, rows), BF16),
        jax.ShapeDtypeStruct((latents, width), BF16),
    ]
    specs = [whole(x) for x in shapes]
    specs[1] = pl.BlockSpec((1, block), lambda i: (0, i))
    return pl.pallas_call(
        lambda *refs: lookup_kernel(scale, *refs),
        grid=(rows // block,),
        out_shape=shapes,
        in_specs=[
            pl.BlockSpec((1, block), lambda i: (0, i)),
            whole(table),
            pl.BlockSpec((block, width), lambda i: (i, 0)),
            pl.BlockSpec((1, width), lambda i: (0, 0)),
            whole(qk),
        ],
        out_specs=specs,
        scratch_shapes=[pltpu.VMEM((latents, rows), F32)],
        compiler_params=pltpu.CompilerParams(vmem_limit_bytes=48 * 1024 * 1024),
    )(codes[None, :], table, position, gain[None, :], qk)


def head_columns(head, width):
    each = width // HEADS
    low, high = head * each // 128 * 128, -(-(head + 1) * each // 128) * 128
    place = low + lax.broadcasted_iota(jnp.int32, (1, high - low), 1)
    return slice(low, high), jnp.logical_and(place >= head * each, place < (head + 1) * each)


def pick(mask, x):
    return jnp.where(mask, x, jnp.zeros_like(x))


def head_softmax(head, q, k):
    columns, mask = head_columns(head, q.shape[1])
    scale = (q.shape[1] // HEADS) ** (-0.5)
    return softmax(nt(pick(mask, q[:, columns]), k[:, columns]) * scale), scale


def self_forward_heads(q, k, v, total):
    total[...] = jnp.zeros_like(total)
    for head in range(HEADS):
        p = head_softmax(head, q, k)[0].astype(BF16)
        columns, mask = head_columns(head, v.shape[1])
        total[:, columns] += nn(p, pick(mask, v[:, columns]))


def self_backward_heads(q, k, v, da, dq_sum, dk_sum, dv_sum):
    for ref in (dq_sum, dk_sum, dv_sum):
        ref[...] = jnp.zeros_like(ref)
    for head in range(HEADS):
        soft, scale = head_softmax(head, q, k)
        columns, mask = head_columns(head, v.shape[1])
        da_head = pick(mask, da[:, columns])
        ds = softmax_backward(nt(da_head, v[:, columns]), soft, scale)
        dv_sum[:, columns] += nn(soft.astype(BF16).T, da_head)
        columns, mask = head_columns(head, q.shape[1])
        dq_sum[:, columns] += nn(ds, pick(mask, k[:, columns]))
        dk_sum[:, columns] += nn(ds.T, pick(mask, q[:, columns]))


class Stream:
    def __init__(self, sources, targets, sem):
        self.copies = [pltpu.make_async_copy(a, b, sem.at[i]) for i, (a, b) in enumerate(zip(sources, targets))]
        self.targets, self.arrived = targets, set()
        for copy in self.copies:
            copy.start()

    def __getitem__(self, i):
        if i not in self.arrived:
            self.copies[i].wait()
            self.arrived.add(i)
        return self.targets[i][...]


class Results:
    def __init__(self, stage, targets, sem):
        self.stage, self.targets, self.sem, self.copies, self.left = stage, targets, sem, [], set()

    def put(self, value, over=None):
        i = len(self.copies)
        buffer = self.stage[i if over is None else over]
        if over is not None:
            self.copies[over].wait()
            self.left.add(over)
        buffer[...] = value.astype(buffer.dtype)
        copy = pltpu.make_async_copy(buffer, self.targets[i], self.sem.at[i])
        copy.start()
        self.copies.append(copy)
        return buffer

    def send(self, source):
        i = len(self.copies)
        copy = pltpu.make_async_copy(source, self.targets[i], self.sem.at[i])
        copy.start()
        self.copies.append(copy)

    def finish(self):
        for i, copy in enumerate(self.copies):
            if i not in self.left:
                copy.wait()


def streamed(body, small, large, shapes, extra, unstaged):
    n_s, n_l, n_o = len(small), len(large), len(shapes)

    def kernel(*refs):
        ins, refs = refs[: n_s + n_l], refs[n_s + n_l :]
        outs, refs = refs[:n_o], refs[n_o:]
        held, refs = refs[:n_l], refs[n_l:]
        kept, refs = list(refs[: n_o - len(unstaged)]), refs[n_o - len(unstaged) :]
        stage = [None if i in unstaged else kept.pop(0) for i in range(n_o)]
        stream = Stream(ins[n_s:], held, refs[0])
        results = Results(stage, outs, refs[1])
        body(ins[:n_s], stream, results, refs[2:])
        results.finish()

    anywhere = pl.BlockSpec(memory_space=pl.ANY)
    return pl.pallas_call(
        kernel,
        out_shape=shapes,
        in_specs=[pl.BlockSpec(memory_space=pltpu.VMEM)] * n_s + [anywhere] * n_l,
        out_specs=[anywhere] * n_o,
        scratch_shapes=[pltpu.VMEM(x.shape, x.dtype) for x in large]
        + [pltpu.VMEM(x.shape, x.dtype) for i, x in enumerate(shapes) if i not in unstaged]
        + [pltpu.SemaphoreType.DMA((n_l,)), pltpu.SemaphoreType.DMA((n_o,))]
        + extra,
        compiler_params=pltpu.CompilerParams(vmem_limit_bytes=63 * 1024 * 1024),
    )(*small, *large)


def bytes_backward(at, scale, arrays):
    vd, nb, soft, q, w_key, w_query, latent = arrays[:7]
    rows, width = nb.shape
    latents, features = latent.shape
    entries, block = -(-arrays[12].shape[0] // 128) * 128, 256
    steps = rows // block

    def body(small, w, results, extra):
        ds, turned, total, table, dq, g_key, g_value, g_latent, row_sem = extra
        vd, nb = w[0], w[1]
        ds[...] = softmax_backward(nt(vd, nb), w[2], scale)
        dn = nn(ds[...], nb).astype(BF16)
        g_key[...] = nn(dn.T, w[3]).astype(BF16)
        results.send(g_key)
        dq[...] = nn(dn, w[4]).astype(BF16)
        results.send(dq)
        dnl = nt(dq[...], w[5])
        hat, rstd = center(w[6].astype(F32))
        g = w[10].astype(F32)
        g_latent[...] = (w[7] + center_backward(dnl * g, hat, rstd)).astype(BF16)
        results.send(g_latent)
        g_value[...] = nn(w[8].T, w[9]).astype(BF16)
        results.send(g_value)
        first = jnp.sum(dnl * hat, axis=0, keepdims=True)
        own = lax.broadcasted_iota(jnp.int32, (8, features), 0) == 0
        turned[...] = jnp.zeros_like(turned)
        turned[:, :8] = jnp.where(own, first, w[11]).T.astype(BF16)
        results.send(turned)
        emb, sums = w[12], w[13]
        total[...] = jnp.zeros_like(total)
        total[: emb.shape[0]] = emb
        total[at + 1 : at + 2] = sums[1:2]
        total[at + 2 : at + 3] = sums[0:1]
        qk, g = w[15], w[18].astype(F32)
        inverse = 1.0 / g
        w[14], w[16], w[17]
        p_ref, scale_ref, codes_ref, nb_ref = w.targets[14], w.targets[16], w.targets[17], w.targets[1]
        target = results.targets[6]

        def out_copy(i):
            here = pl.ds(pl.multiple_of(i * block, block), block)
            return pltpu.make_async_copy(nb_ref.at[here], target.at[here], row_sem.at[i])

        def step(i, carry):
            here = pl.ds(pl.multiple_of(i * block, block), block)
            rstd = jnp.broadcast_to(scale_ref[:, here], (128, block)).T[:, :1]
            normed = nb_ref[here, :]
            dnb = nn(p_ref[:, here].T, vd) + nn(ds[:, here].T, qk)
            hat = normed.astype(F32) * inverse
            dx = center_backward(dnb * g, hat, rstd).astype(BF16)
            nb_ref[here, :] = dx
            out_copy(i).start()
            entry = lax.broadcasted_iota(jnp.int32, (entries, block), 0)
            onehot = (entry == codes_ref[:, here]).astype(BF16)
            total[...] += nn(onehot, dx)
            total[at : at + 1] += jnp.sum(dnb * hat, axis=0, keepdims=True)
            return carry

        lax.fori_loop(0, steps, step, 0)
        table[...] = total[...].T.astype(BF16)
        results.send(table)

        def wait(i, carry):
            out_copy(i).wait()
            return carry

        lax.fori_loop(0, steps, wait, 0)

    qk_width = q.shape[1]

    def low(*shape):
        return jax.ShapeDtypeStruct(shape, BF16)

    shapes = [
        low(width, qk_width), low(latents, qk_width), low(latents, features), low(width, features),
        low(features, 128), low(width, entries), low(rows, width),
    ]
    vmem = pltpu.VMEM
    extra = [vmem((latents, rows), BF16), vmem((features, 128), BF16), vmem((entries, width), F32)]
    extra += [vmem((width, entries), BF16), vmem((latents, qk_width), BF16), vmem((width, qk_width), BF16)]
    extra += [vmem((width, features), BF16), vmem((latents, features), BF16), pltpu.SemaphoreType.DMA((steps,))]
    return streamed(body, [], arrays, shapes, extra, set(range(len(shapes))))


def middle_pass(latent, pn, gains, byte_gains, weights, scale):
    rows, width = latent.shape
    emb, queries, cot = weights[14:]
    entries, depth = emb.shape
    block = 256
    qk = weights[4].shape[1]

    def body(small, w, results, extra):
        latent_ref, pn_ref, g1, g2, g3, g4, gain_q, gain_f = small
        total, dq_sum, dk_sum, sums, u1, u2, q, k, v, k_d, v_d, kq, vo, vo_mid, g_pd, g_dn, g_emb, g_byte = extra
        put = results.put

        def norm(x, gain):
            hat, rstd = center(x)
            return put(hat * gain[...].astype(F32)), rstd

        a_e = put(nn(pn_ref[...], w[0]))
        x = latent_ref[...].astype(F32) + nn(a_e[...], w[1])
        n1, r1 = norm(x, g1)
        u1[...] = nn(n1[...], w[2])
        h1 = put(gelu_forward(u1[...]))
        x = x + nn(h1[...], w[3])
        n2, r2 = norm(x, g2)
        q[...] = nn(n2[...], w[4]).astype(BF16)
        k[...] = nn(n2[...], w[5]).astype(BF16)
        v[...] = nn(n2[...], w[6]).astype(BF16)
        self_forward_heads(q, k, v, total)
        a_s = put(total[...])
        x = x + nn(a_s[...], w[7])
        n3, r3 = norm(x, g3)
        u2[...] = nn(n3[...], w[8])
        h2 = put(gelu_forward(u2[...]))
        x = x + nn(h2[...], w[9])
        n4, r4 = norm(x, g4)
        k_d[...] = nn(n4[...], w[10]).astype(BF16)
        v_d[...] = nn(n4[...], w[11]).astype(BF16)

        w_query, w_out = w[12], w[13]
        kq[...] = nt(k_d[...], w_query).astype(BF16)
        out = nn(v_d[...], w_out)
        vo[...] = out.astype(BF16)
        vo_mid[...] = (out - jnp.mean(out, axis=0, keepdims=True)).astype(BF16)
        for ref in (g_pd, g_dn, g_emb, g_byte):
            ref[...] = jnp.zeros_like(ref)
        w[14], w[15], w[16]
        emb_ref, query_ref, cot_ref = w.targets[14:]

        def decode(i, carry):
            at = pl.ds(pl.multiple_of(i * block, block), block)
            x = query_ref[at, :].astype(F32)
            hat_q, rstd_q = center(x)
            gq, gf = gain_q[...].astype(F32), gain_f[...].astype(F32)
            nq = (hat_q * gq).astype(BF16)
            soft = softmax(nt(nq, kq[...]) * scale)
            p = soft.astype(BF16)
            hat_f, rstd_f = center(x + nn(p, vo[...]))
            nf = (hat_f * gf).astype(BF16)
            cot_part = cot_ref[:, at]
            dnf = nn(cot_part.T, emb_ref[...])
            g_emb[...] += nn(cot_part, nf)
            cot_ref[:, at] = nt(emb_ref[...], nf).astype(BF16)
            g_byte[0:1] += jnp.sum(dnf * hat_f, axis=0, keepdims=True)
            ddec = center_backward(dnf * gf, hat_f, rstd_f)
            ddec16 = ddec.astype(BF16)
            g_pd[...] += nn(p.T, ddec16)
            ds = softmax_backward(nt(ddec16, vo_mid[...]), soft, scale)
            g_dn[...] += nn(ds.T, nq)
            dnq = nn(ds, kq[...])
            g_byte[1:2] += jnp.sum(dnq * hat_q, axis=0, keepdims=True)
            query_ref[at, :] = (ddec + center_backward(dnq * gq, hat_q, rstd_q)).astype(BF16)
            return carry

        lax.fori_loop(0, queries.shape[0] // block, decode, 0)
        results.send(query_ref)
        half = queries.shape[0] // 2
        mine = lax.axis_index("blk")
        for part in (mine, 1 - mine):
            results.send(cot_ref.at[:, pl.ds(pl.multiple_of(part * half, half), half)])
        results.send(g_emb)
        results.send(g_byte)
        pd, dn = g_pd[...].astype(BF16), g_dn[...].astype(BF16)
        dk_d = nn(dn, w.targets[12][...]).astype(BF16)
        dv_d = nt(pd, w.targets[13][...]).astype(BF16)
        put(dk_d)
        put(dv_d)
        put(nn(dn.T, k_d[...]))
        put(nn(v_d[...].T, pd))

        sums[...] = jnp.zeros_like(sums)

        def back(dy, normed, rstd, gain, row):
            g = gain[...].astype(F32)
            hat = normed[...].astype(F32) * (1.0 / g)
            sums[row : row + 1] = jnp.sum(dy * hat, axis=0, keepdims=True)
            return center_backward(dy * g, hat, rstd)

        dlat = back(nt(dk_d, w[10]) + nt(dv_d, w[11]), n4, r4, g4, 4)
        dlat16 = put(dlat, 0)
        du2 = put(gelu_backward(nt(dlat16[...], w[9]), u2[...]), 2)
        das = dlat + back(nt(du2[...], w[8]), n3, r3, g3, 3)
        das16 = put(das, 4)
        da = nt(das16[...], w[7]).astype(BF16)
        self_backward_heads(q, k, v, da, dq_sum, dk_sum, total)
        dq, dk, dv = put(dq_sum[...]), put(dk_sum[...]), put(total[...], 6)
        dn2 = nt(dq[...], w[4]) + nt(dk[...], w[5]) + nt(dv[...], w[6])
        denc = das + back(dn2, n2, r2, g2, 2)
        denc16 = put(denc, 7)
        du1 = put(gelu_backward(nt(denc16[...], w[3]), u1[...]), 5)
        daft = denc + back(nt(du1[...], w[2]), n1, r1, g1, 1)
        daft16 = put(daft, 3)
        u1[...] = daft
        results.send(u1)
        dae = put(nt(daft16[...], w[1]), 1)
        put(nt(dae[...], w[0]))
        results.send(sums)

    wide = (rows, width)

    def low(*shape):
        return jax.ShapeDtypeStruct(shape, BF16)

    def full(*shape):
        return jax.ShapeDtypeStruct(shape, F32)

    shapes = [low(*wide)] * 8
    shapes += [low(*queries.shape)] + [low(entries, queries.shape[0] // 2)] * 2
    shapes += [full(entries, depth), full(8, depth)]
    shapes += [low(rows, qk), low(rows, depth), low(depth, qk), low(depth, depth)]
    shapes += [low(*wide)] * 3 + [low(rows, qk)] * 2 + [low(*wide)] * 4
    shapes += [full(*wide), low(*wide), low(rows, depth), full(8, width)]
    unstaged = {8, 9, 10, 11, 12, 17, 18, 19, 22, 23, 24, 25, 26, 27, 29}
    vmem = pltpu.VMEM
    extra = [vmem(wide, F32), vmem((rows, qk), F32), vmem((rows, qk), F32), vmem((8, width), F32)]
    extra += [vmem(wide, F32)] * 2 + [vmem((rows, qk), BF16)] * 2 + [vmem(wide, BF16)]
    extra += [vmem((rows, qk), BF16)] + [vmem((rows, depth), BF16)] * 4 + [vmem((rows, depth), F32)] * 2
    extra += [vmem((entries, depth), F32), vmem((8, depth), F32)]
    small = [latent, pn] + [g[None, :] for g in gains + byte_gains]
    return streamed(body, small, weights, shapes, extra, unstaged)


def local(
    byte_ids, span_start, span_len, embedding, position, mask_vector, gain_bytes, key_enc,
    value_enc, latent_init, gain_latent, query_enc, out_enc, gain_enc_mlp, up_enc, down_enc,
    gain_self, query_self, key_self, value_self, out_self, gain_self_mlp, up_self, down_self,
    gain_dec_kv, key_dec, value_dec, dec_query, gain_dec_q, query_dec, out_dec, gain_final,
    logit_cot,
):
    me = lax.axis_index("blk")
    half = byte_ids.shape[1]
    total = position.shape[0]
    vocab = embedding.shape[0]
    reducer = Reducer()
    k = reducer.k
    order_yx = [0, "y", 1] + list(range(2, k))
    order_xy = [0, 1, "y"] + list(range(2, k))

    def swap(x):
        return lax.ppermute(x, "blk", [(0, 1), (1, 0)])

    def own_item(first, second, after=()):
        mine = jnp.where(me == 0, first, second)
        send = jnp.where(me == 0, second, first)
        if after:
            (send,) = tie([send], after)
        got = swap(send)
        low_half = jnp.where(me == 0, mine, got)
        high_half = jnp.where(me == 0, got, mine)
        return jnp.concatenate([low_half, high_half], axis=-1)

    ids = own_item(byte_ids[0], byte_ids[1])
    cot_rows = logit_cot.transpose(2, 0, 1)
    cot = own_item(cot_rows[:, 0], cot_rows[:, 1], [ids])
    entries = -(-(vocab + 4) // 16) * 16
    cot = jnp.pad(cot, ((0, entries - vocab), (0, 0)))
    emb_rows = jnp.pad(embedding, ((0, entries - vocab), (0, 0)))
    starts = lax.dynamic_index_in_dim(span_start, me, 0, keepdims=False)
    lengths = lax.dynamic_index_in_dim(span_len, me, 0, keepdims=False)

    places = lax.iota(jnp.int32, total)
    inside = (places[None, :] >= starts[:, None]) & (places[None, :] < (starts + lengths)[:, None])
    codes = jnp.where(jnp.any(inside, axis=0), vocab, ids)
    padded = -(-(vocab + 4) // 128) * 128
    table = jnp.concatenate(
        [embedding, mask_vector[None, :], jnp.zeros((padded - vocab - 1, embedding.shape[1]), BF16)], axis=0
    )

    latent32 = latent_init.astype(F32)
    nl = norm_forward(latent32, gain_latent)[0]
    q_e = nn(nl, query_enc).astype(BF16)
    scale_e = q_e.shape[1] ** (-0.5)
    qk_e = nt(q_e, key_enc).astype(BF16)
    nb, rstd_b, soft_e, p_e, pn_e = bytes_forward(codes, table, position, gain_bytes, qk_e, scale_e)

    gains = (gain_enc_mlp, gain_self, gain_self_mlp, gain_dec_kv)
    (
        a_e, n1, h1, n2, a_s, n3, h2, n4,
        g_dec_query, logits_own, logits_other, g_emb_out, gain_sums, dk_d, dv_d, g_query_dec, g_out_dec,
        dlat16, du2, das16, dq_s, dk_s, dv_s, denc16, du1, daft16, dafter, dae16, vd_e, wide,
    ) = middle_pass(
        latent_init, pn_e, gains, (gain_dec_q, gain_final),
        [
            value_enc, out_enc, up_enc, down_enc, query_self, key_self, value_self, out_self, up_self,
            down_self, key_dec, value_dec, query_dec, out_dec, emb_rows, dec_query, cot,
        ],
        query_dec.shape[1] ** (-0.5),
    )
    logits_own, logits_got = logits_own[:vocab], swap(logits_other)[:vocab]
    side = lax.broadcasted_iota(jnp.int32, (1, 2, 1), 1)
    logits_out = jnp.where(side == me, logits_own[:, None, :], logits_got[:, None, :]).transpose(1, 2, 0)

    g_key_enc, dq_e, g_latent, g_value_enc, vectors, g_table, dbytes = bytes_backward(
        vocab + 1, scale_e,
        [
            vd_e, nb, soft_e, q_e, key_enc, query_enc, latent_init, dafter, pn_e, dae16, gain_latent[None, :], wide,
            g_emb_out, gain_sums, p_e, qk_e, rstd_b, codes[None, :], gain_bytes[None, :],
        ],
    )

    def low(g):
        return g.astype(BF16)

    if reducer.n_items == 16:
        first_side = [(n1, [du1]), (a_e, [daft16]), (n3, [du2]), (n2, [dv_s, dk_s])]
        second_side = [
            (h1, [denc16]), (h2, [dlat16]), (a_s, [das16]), (n4, [dv_d, dk_d]), (n2, [dq_s]), (nl, [dq_e]),
        ]
        others = [
            (low(g_dec_query), "xy"), (low(dbytes), "yx"), (low(g_value_enc), "xy"), (low(g_out_dec), "yx"),
            (low(g_table), "yx"), (low(g_key_enc), "xy"), (low(g_query_dec), "yx"), (low(g_latent), "xy"),
            (low(vectors), "yx"),
        ]
        (
            r_up_enc, r_out_enc, r_up_self, r_value_self, r_key_self,
            r_down_enc, r_down_self, r_out_self, r_value_dec, r_key_dec, r_query_self, r_query_enc,
        ), (
            r_dec_query, r_position, r_value_enc, r_out_dec, r_emb, r_key_enc, r_query_dec, r_latent, r_vectors,
        ) = reduce_all((first_side, second_side), others)
    else:
        r_dec_query, r_out_dec, r_value_dec = reducer.reduce([g_dec_query, g_out_dec, tn(n4, dv_d)], order_yx)
        r_down_self, r_up_self, r_out_self = reducer.reduce(
            [tn(h2, dlat16), tn(n3, du2), tn(a_s, das16)], order_xy
        )
        r_value_self, r_down_enc = reducer.reduce([tn(n2, dv_s), tn(h1, denc16)], order_yx)
        r_up_enc, r_out_enc = reducer.reduce([tn(n1, du1), tn(a_e, daft16)], order_xy)
        r_query_dec, r_key_dec, r_query_self, r_key_self = reducer.reduce(
            [g_query_dec, tn(n4, dk_d), tn(n2, dq_s), tn(n2, dk_s)], order_xy
        )
        r_value_enc, r_latent = reducer.reduce([g_value_enc, g_latent], order_xy)
        (r_position,) = reducer.reduce([dbytes], order_yx)
        r_key_enc, r_query_enc = reducer.reduce([g_key_enc, tn(nl, dq_e)], order_yx)
        (r_emb,) = reducer.reduce([g_table], order_yx)
        (r_vectors,) = reducer.reduce([vectors], order_xy)

    plain = [
        r_position, r_key_enc, r_value_enc, r_latent, r_query_enc, r_out_enc, r_up_enc, r_down_enc,
        r_query_self, r_key_self, r_value_self, r_out_self, r_up_self, r_down_self, r_key_dec, r_value_dec,
        r_dec_query, r_query_dec, r_out_dec,
    ]
    plain, r_embedding, (r_mask, r_gain_bytes, r_gain_dec_q, r_gain_final), gains = finish(plain, r_emb, r_vectors, vocab, 1 + len(gains))
    (
        r_position, r_key_enc, r_value_enc, r_latent, r_query_enc, r_out_enc, r_up_enc, r_down_enc,
        r_query_self, r_key_self, r_value_self, r_out_self, r_up_self, r_down_self, r_key_dec, r_value_dec,
        r_dec_query, r_query_dec, r_out_dec,
    ) = plain
    (
        r_gain_latent, r_gain_enc_mlp, r_gain_self, r_gain_self_mlp, r_gain_dec_kv,
    ) = gains
    return (
        logits_out, r_embedding.T, r_position, r_mask, r_gain_bytes, r_key_enc, r_value_enc,
        r_latent, r_gain_latent, r_query_enc, r_out_enc, r_gain_enc_mlp, r_up_enc, r_down_enc, r_gain_self,
        r_query_self, r_key_self, r_value_self, r_out_self, r_gain_self_mlp, r_up_self, r_down_self,
        r_gain_dec_kv, r_key_dec, r_value_dec, r_dec_query, r_gain_dec_q, r_query_dec, r_out_dec, r_gain_final,
    )


def solution(mesh):
    split = P("items", "blk")
    rows = P(("items", "blk"))
    outs = [P("items", "blk", None), P(None, ("items", "blk"))] + [rows] * 28
    return jax.shard_map(
        local,
        mesh=mesh,
        in_specs=(split, P("items", None), P("items", None)) + (P(),) * 29 + (P("items", "blk", None),),
        out_specs=tuple(outs),
        check_vma=False,
    )
```

```python
import jax
import jax.numpy as jnp
from jax import lax
from jax.experimental import pallas as pl
from jax.experimental.pallas import tpu as pltpu
from jax.sharding import PartitionSpec as P

HEADS = 8
EPS = 1e-05
F32 = jnp.float32
BF16 = jnp.bfloat16
GELU_C = 0.7978845608028654
GELU_A = 0.044715


def nn(a, b):
    return lax.dot_general(a, b, (((1,), (0,)), ((), ())), preferred_element_type=F32)


def nt(a, b):
    return lax.dot_general(a, b, (((1,), (1,)), ((), ())), preferred_element_type=F32)


def tn(a, b):
    return lax.dot_general(a, b, (((0,), (0,)), ((), ())), preferred_element_type=F32)


def norm_forward(x, gain):
    centered = x - jnp.mean(x, axis=-1, keepdims=True)
    variance = jnp.mean(centered * centered, axis=-1, keepdims=True)
    rstd = lax.rsqrt(variance + EPS)
    hat = centered * rstd
    return (hat * gain.astype(F32)).astype(BF16), hat, rstd


def norm_backward(dy, hat, rstd, gain):
    dgain = jnp.sum(dy * hat, axis=0, keepdims=True)
    dhat = dy * gain.astype(F32)
    first = jnp.mean(dhat, axis=-1, keepdims=True)
    second = jnp.mean(dhat * hat, axis=-1, keepdims=True)
    return rstd * (dhat - first - hat * second), dgain


def gelu_forward(u):
    t = jnp.tanh(GELU_C * (u + GELU_A * u * u * u))
    return (0.5 * u * (1.0 + t)).astype(BF16)


def gelu_backward(dh, u):
    t = jnp.tanh(GELU_C * (u + GELU_A * u * u * u))
    slope = 0.5 * (1.0 + t) + 0.5 * u * (1.0 - t * t) * GELU_C * (1.0 + 3.0 * GELU_A * u * u)
    return dh * slope


def softmax(s):
    e = jnp.exp(s - jnp.max(s, axis=-1, keepdims=True))
    return e * (1.0 / jnp.sum(e, axis=-1, keepdims=True))


def softmax_backward(dp, soft, scale):
    inner = jnp.sum(dp * soft, axis=-1, keepdims=True)
    return (soft * (dp - inner) * scale).astype(BF16)


class Reducer:
    def __init__(self):
        n_items = lax.axis_size("items")
        self.count = n_items * lax.axis_size("blk")
        self.k = n_items.bit_length() - 1
        self.n_items = n_items

    def bit(self, name):
        if name == "y":
            return lax.axis_index("blk")
        return (lax.axis_index("items") >> name) & 1

    def exchange(self, x, name):
        if name == "y":
            return lax.ppermute(x, "blk", [(0, 1), (1, 0)])
        return lax.ppermute(x, "items", [(i, i ^ (1 << name)) for i in range(self.n_items)])

    def split(self, g):
        rows, width = g.shape
        return g.astype(BF16).reshape((2,) * (self.k + 1) + (rows // self.count, width))

    def reduce(self, grads, order):
        dims = list(range(self.k - 1, -1, -1)) + ["y"]
        parts = [self.split(g) for g in grads]
        heights = [p.shape[-2] for p in parts]
        for number, name in enumerate(order):
            axis = dims.index(name)
            mine = self.bit(name)
            send = [lax.dynamic_index_in_dim(p, 1 - mine, axis, keepdims=False) for p in parts]
            keep = [lax.dynamic_index_in_dim(p, mine, axis, keepdims=False) for p in parts]
            if number == 0:
                send = [jnp.concatenate(send, axis=-2)] if len(send) > 1 else send
                keep = [jnp.concatenate(keep, axis=-2)] if len(keep) > 1 else keep
            got = self.exchange(send[0], name)
            total = keep[0].astype(F32) + got.astype(F32)
            last = number == len(order) - 1
            parts = [total if last else total.astype(BF16)]
            dims.pop(axis)
        out, at = [], 0
        for height in heights:
            out.append(parts[0][at : at + height])
            at += height
        return out


CHUNK = 256
LAG = 2
MESH = pl.DeviceIdType.MESH
STAGES = {
    "xy": ("c", "x", "y", "z0", "z1"),
    "yx": ("c", "y", "x", "z0", "z1"),
}
ITEM_BIT = {"c": 0, "x": 1, "z0": 2, "z1": 3}


def padded_rows(r):
    return -(-r // 16) * 16


def my_bit(name):
    if name == "y":
        return lax.axis_index("blk")
    return (lax.axis_index("items") // 2 ** ITEM_BIT[name]) % 2


def partner(name):
    if name == "y":
        return {"blk": 1 - lax.axis_index("blk")}
    return {"items": lax.axis_index("items") + (1 - 2 * my_bit(name)) * 2 ** ITEM_BIT[name]}


def divide(first, second, mine, r, by_rows):
    if by_rows:
        first, second = (
            jnp.concatenate([first[:r], second[:r]], axis=0),
            jnp.concatenate([first[r:], second[r:]], axis=0),
        )
    return jnp.where(mine == 0, first, second), jnp.where(mine == 0, second, first)


def tie(values, after):
    count = len(values)
    anywhere = pl.BlockSpec(memory_space=pl.ANY)
    return pl.pallas_call(
        lambda *refs: None,
        out_shape=[jax.ShapeDtypeStruct(v.shape, v.dtype) for v in values],
        in_specs=[anywhere] * (count + len(after)),
        out_specs=[anywhere] * count,
        input_output_aliases={i: i for i in range(count)},
    )(*values, *after)


class Chunk:
    def __init__(self, bufs, at, sems, r, width, order):
        self.rc, self.r1, self.r2, self.r3, self.s4, self.r4, self.out = [b.at[at] for b in bufs]
        self.send, self.recv, self.at = sems[0], sems[1], at
        self.r, self.width, self.order = r, width, order
        self.step = 256 if r <= 40 and width % 256 == 0 else 128

    def copy(self, stage, source=None):
        src, dst = (
            (source, self.rc),
            (self.rc.at[:, :, 1], self.r1),
            (self.rc.at[:, 1, 0], self.r2),
            (self.rc.at[1, 0, 0], self.r3),
            (self.s4, self.r4),
        )[stage]
        return pltpu.make_async_remote_copy(
            src_ref=dst if src is None else src,
            dst_ref=dst,
            send_sem=self.send.at[self.at, stage],
            recv_sem=self.recv.at[self.at, stage],
            device_id=partner(STAGES[self.order][stage]),
            device_id_type=MESH,
        )

    def loop(self, pairs, body):
        columns = self.width // self.step

        def run(i, carry):
            body(i // columns, pl.ds(pl.multiple_of((i % columns) * self.step, self.step), self.step))
            return carry

        lax.fori_loop(0, pairs * columns, run, 0)

    def advance(self, stage, loaded=None):
        self.copy(stage).wait_recv()
        names = STAGES[self.order]
        r, kind, rc = self.r, self.rc.dtype, self.rc
        mine = my_bit(names[stage + 1]) if stage < 4 else None

        def total(a, b):
            return a.astype(F32) + b.astype(F32)

        def stage0(p, cols):
            q, z = p // 2, p % 2
            first = total(rc[q, z, 0, :, cols], loaded[q, z, 0, :, cols])
            second = total(rc[q, z, 1, :, cols], loaded[q, z, 1, :, cols])
            keep, send = divide(first, second, mine, r, names[1] == "y")
            rc[q, z, 0, :, cols] = keep.astype(kind)
            rc[q, z, 1, :, cols] = send.astype(kind)

        def stage1(q, cols):
            first = total(rc[q, 0, 0, :, cols], self.r1[q, 0, :, cols])
            second = total(rc[q, 1, 0, :, cols], self.r1[q, 1, :, cols])
            keep, send = divide(first, second, mine, r, True)
            rc[q, 0, 0, :, cols] = keep.astype(kind)
            rc[q, 1, 0, :, cols] = send.astype(kind)

        def stage2(q, cols):
            first = total(rc[0, 0, 0, :, cols], self.r2[0, :, cols])
            second = total(rc[1, 0, 0, :, cols], self.r2[1, :, cols])
            keep, send = divide(first, second, mine, r, True)
            rc[0, 0, 0, :, cols] = keep.astype(kind)
            rc[1, 0, 0, :, cols] = send.astype(kind)

        def stage3(q, cols):
            both = total(rc[0, 0, 0, :, cols], self.r3[:, cols])
            keep = jnp.where(mine == 0, both[:r], both[r:])
            send = jnp.where(mine == 0, both[r:], both[:r])
            extra = padded_rows(r) - r
            if extra:
                send = jnp.concatenate([send, jnp.zeros((extra, send.shape[1]), F32)], axis=0)
            self.s4[:, cols] = send.astype(kind)
            self.out[:, cols] = keep

        def stage4(q, cols):
            self.out[:, cols] = self.out[:, cols] + self.r4[:, cols].astype(F32)[:r]

        self.loop((4, 2, 1, 1, 1)[stage], (stage0, stage1, stage2, stage3, stage4)[stage])
        if stage < 4:
            self.copy(stage + 1).start()


def when(condition, action):
    if isinstance(condition, bool):
        if condition:
            action()
    else:
        pl.when(condition)(action)


SLOTS = 4
AHEAD = 3
B_SLOTS = 3


def reduce_kernel(plan, *refs):
    sides, steps, n_act, n_cot, widths, others = plan
    n_a, n_o = len(widths), len(others)
    acts, refs = refs[:n_act], refs[n_act:]
    cots, refs = refs[:n_cot], refs[n_cot:]
    o_src, refs = refs[:n_o], refs[n_o:]
    a_out, o_out = refs[:n_a], refs[n_a : n_a + n_o]
    refs = refs[n_a + n_o :]
    a_bufs, refs = refs[:7], refs[7:]
    act_in, act_t, cot_in, made = refs[:4]
    refs = refs[4:]
    o_bufs, refs = [refs[8 * i : 8 * i + 8] for i in range(n_o)], refs[8 * n_o :]
    a_sems, o_sems = refs[0:2], refs[2:4]
    act_sem, cot_sem, o_load_sem, a_out_sem, o_out_sem = refs[4:]
    core = my_bit("c")
    rows = act_t.shape[1] // 4

    barrier = pltpu.get_barrier_semaphore()
    for name in ("c", "x", "y", "z0", "z1"):
        pl.semaphore_signal(barrier, inc=1, device_id=partner(name), device_id_type=MESH)
    pl.semaphore_wait(barrier, 5)

    def chunk(step, side):
        return Chunk(a_bufs, 2 * step + side, a_sems, 40, CHUNK, ("xy", "yx")[side])

    def act_copy(side, group):
        return pltpu.make_async_copy(acts[sides[side][0][group][1]], act_in.at[side], act_sem.at[side])

    def cot_copy(side, step):
        source, number, _ = sides[side][1][step]
        slot = step % B_SLOTS
        return pltpu.make_async_copy(
            cots[source].at[:, pl.ds(number * CHUNK, CHUNK)], cot_in.at[side, slot], cot_sem.at[side, slot]
        )

    def first_copy(step, side):
        return chunk(step, side).copy(0, made.at[side, step % SLOTS, 1 - core])

    def produce(step):
        for side in range(2):
            groups = sides[side][0]
            for g, (start, _) in enumerate(groups):

                def fresh(g=g, side=side, groups=groups):
                    act_copy(side, g).wait()

                    def turn(i, carry):
                        at = pl.ds(pl.multiple_of(i * 256, 256), 256)
                        act_t[side, at, :] = act_in[side, :, at].T
                        return carry

                    lax.fori_loop(0, act_in.shape[2] // 256, turn, 0)
                    if g + 1 < len(groups):
                        act_copy(side, g + 1).start()

                when(step == start, fresh)
            for later in range(B_SLOTS - 1, steps):
                when(step == later - (B_SLOTS - 1), lambda later=later, side=side: cot_copy(side, later).start())
            slot = step % B_SLOTS
            pltpu.make_async_copy(
                cots[0].at[:, pl.ds(0, CHUNK)], cot_in.at[side, slot], cot_sem.at[side, slot]
            ).wait()
            when(step >= SLOTS, lambda side=side: first_copy(step - SLOTS, side).wait_send())

            def product(i, carry, side=side, slot=slot):
                part = act_t[side, pl.ds(pl.multiple_of(i * rows, rows), rows), :]
                result = jnp.dot(part, cot_in[side, slot], preferred_element_type=F32)
                height = rows // 4
                for x in range(2):
                    for c in range(2):
                        at = (2 * x + c) * height
                        made[side, step % SLOTS, c, i // 2, i % 2, x] = result[at : at + height].astype(BF16)
                return carry

            lax.fori_loop(0, 4, product, 0)
            first_copy(step, side).start()

    small = []
    for i, (r, width, order) in enumerate(others):
        item = Chunk([b.at[0:1] for b in o_bufs[i][:7]], 0, o_sems, r, width, order)
        item.at = i
        small.append(item)
        item.copy(0, o_src[i].at[:, :, :, 1 - core]).start()
        pltpu.make_async_copy(o_src[i].at[:, :, :, core], o_bufs[i][7], o_load_sem.at[i]).start()
    for side in range(2):
        act_copy(side, 0).start()
        for step in range(B_SLOTS - 1):
            cot_copy(side, step).start()

    def begin(step, carry):
        produce(step)
        return carry

    lax.fori_loop(0, AHEAD, begin, 0)
    for i, item in enumerate(small):
        pltpu.make_async_copy(o_src[i].at[:, :, :, core], o_bufs[i][7], o_load_sem.at[i]).wait()
        item.advance(0, o_bufs[i][7])

    def run(step, carry):
        pl.when(step + AHEAD < steps)(lambda: produce(step + AHEAD))

        def enter():
            for side in range(2):
                chunk(step, side).advance(0, made.at[side, step % SLOTS, core])

        pl.when(step < steps)(enter)
        for stage in range(4, 0, -1):
            old = step - stage * LAG

            def act(old=old, stage=stage):
                for side in range(2):
                    chunk(old, side).advance(stage)

            pl.when(jnp.logical_and(old >= 0, old < steps))(act)
        for number in range(4):

            def others_on(number=number):
                for item in small:
                    item.advance(number + 1)

            pl.when(step == 4 + 5 * number)(others_on)
        return carry

    lax.fori_loop(0, steps + 4 * LAG, run, 0)

    outs = []
    for side in range(2):
        for step in range(steps):
            _, number, target = sides[side][1][step]
            at = 2 * step + side
            outs.append(
                pltpu.make_async_copy(
                    a_bufs[6].at[at], a_out[target].at[:, pl.ds(number * CHUNK, CHUNK)], a_out_sem.at[at]
                )
            )
    for i in range(n_o):
        outs.append(pltpu.make_async_copy(o_bufs[i][6].at[0], o_out[i], o_out_sem.at[i]))
    for copy in outs:
        copy.start()
    for step in range(steps - SLOTS, steps):
        for side in range(2):
            first_copy(step, side).wait_send()
    for i, item in enumerate(small):
        item.copy(0, o_src[i].at[:, :, :, 1 - core]).wait_send()
        for stage in range(1, 5):
            item.copy(stage).wait_send()

    def wait_sent(step, carry):
        for side in range(2):
            for stage in range(1, 5):
                chunk(step, side).copy(stage).wait_send()
        return carry

    lax.fori_loop(0, steps, wait_sent, 0)
    for copy in outs:
        copy.wait()


def buffers(count, r, width, kind):
    rp = padded_rows(r)
    return [
        pltpu.VMEM((count, 2, 2, 2, 2 * r, width), kind),
        pltpu.VMEM((count, 2, 2, 2 * r, width), kind),
        pltpu.VMEM((count, 2, 2 * r, width), kind),
        pltpu.VMEM((count, 2 * r, width), kind),
        pltpu.VMEM((count, rp, width), kind),
        pltpu.VMEM((count, rp, width), kind),
        pltpu.VMEM((count, r, width), F32),
    ]


def reduce_all(products, others):
    acts, cots, sides, widths = [], [], [], []
    for side in products:
        groups, sequence = [], []
        for act, own in side:
            groups.append((len(sequence), len(acts)))
            acts.append(act)
            for cot in own:
                for number in range(cot.shape[1] // CHUNK):
                    sequence.append((len(cots), number, len(widths)))
                cots.append(cot)
                widths.append(cot.shape[1])
        sides.append((tuple(groups), tuple(sequence)))
    steps = len(sides[0][1])
    assert steps == len(sides[1][1])

    def view(g):
        return g.reshape(2, 2, 2, 2, g.shape[0] // 16, g.shape[1])

    plan = (
        tuple(sides), steps, len(acts), len(cots), tuple(widths),
        tuple((g.shape[0] // 32, g.shape[1], order) for g, order in others),
    )
    depth, features = acts[0].shape
    scratch = buffers(2 * steps, 40, CHUNK, BF16)
    scratch += [
        pltpu.VMEM((2, depth, features), BF16),
        pltpu.VMEM((2, features, depth), BF16),
        pltpu.VMEM((2, B_SLOTS, depth, CHUNK), BF16),
        pltpu.VMEM((2, SLOTS, 2, 2, 2, 2, 80, CHUNK), BF16),
    ]
    for g, order in others:
        r = g.shape[0] // 32
        scratch += buffers(1, r, g.shape[1], g.dtype)
        scratch.append(pltpu.VMEM((2, 2, 2, 2 * r, g.shape[1]), g.dtype))
    dma = pltpu.SemaphoreType.DMA
    scratch += [dma((2 * steps, 5)), dma((2 * steps, 5)), dma((len(others), 5)), dma((len(others), 5))]
    scratch += [dma((2,)), dma((2, B_SLOTS)), dma((len(others),)), dma((2 * steps,)), dma((len(others),))]
    anywhere = pl.BlockSpec(memory_space=pl.ANY)
    arrays = acts + cots + [view(g) for g, order in others]
    results = pl.pallas_call(
        lambda *refs: reduce_kernel(plan, *refs),
        out_shape=[jax.ShapeDtypeStruct((features // 32, w), F32) for w in widths]
        + [jax.ShapeDtypeStruct((g.shape[0] // 32, g.shape[1]), F32) for g, order in others],
        in_specs=[anywhere] * len(arrays),
        out_specs=[anywhere] * (len(widths) + len(others)),
        scratch_shapes=scratch,
        compiler_params=pltpu.CompilerParams(
            collective_id=0, has_side_effects=True, vmem_limit_bytes=62 * 1024 * 1024
        ),
    )(*arrays)
    return results[: len(widths)], results[len(widths) :]


def finish(plain, table, vectors, vocab, vector_count):
    count = len(plain)
    width = table.shape[0]

    def kernel(*refs):
        sources, refs = refs[:count], refs[count:]
        table_ref, vectors_ref = refs[:2]
        refs = refs[2:]
        targets, refs = refs[:count], refs[count:]
        emb_ref, row_refs, refs = refs[0], refs[1:5], refs[5:]
        gain_refs, refs = refs[:vector_count], refs[vector_count:]
        staged, (in_sem, out_sem) = refs[:count], refs[count:]
        inward = [pltpu.make_async_copy(sources[i], staged[i], in_sem.at[i]) for i in range(count)]
        outward = [pltpu.make_async_copy(staged[i], targets[i], out_sem.at[i]) for i in range(count)]
        for copy in inward:
            copy.start()
        turned = table_ref[...].T
        emb_ref[...] = table_ref[:, :vocab]
        vector_rows = vectors_ref[...].T
        for i, row_ref in enumerate(row_refs):
            row_ref[...] = turned[vocab + i]
        for i, gain_ref in enumerate(gain_refs):
            gain_ref[...] = vector_rows[i]
        for i in range(count):
            inward[i].wait()
            outward[i].start()
        for copy in outward:
            copy.wait()

    anywhere = pl.BlockSpec(memory_space=pl.ANY)
    local_memory = pl.BlockSpec(memory_space=pltpu.VMEM)
    shapes = [jax.ShapeDtypeStruct(p.shape, F32) for p in plain]
    shapes += [jax.ShapeDtypeStruct((width, vocab), F32)] + [jax.ShapeDtypeStruct((width,), F32)] * 4
    shapes += [jax.ShapeDtypeStruct(vectors.shape[:1], F32)] * vector_count
    results = pl.pallas_call(
        kernel,
        out_shape=shapes,
        in_specs=[anywhere] * count + [local_memory] * 2,
        out_specs=[anywhere] * count + [local_memory] * (5 + vector_count),
        scratch_shapes=[pltpu.VMEM(p.shape, F32) for p in plain] + [pltpu.SemaphoreType.DMA((count,))] * 2,
    )(*plain, table, vectors)
    return results[:count], results[count], results[count + 1 : count + 5], results[count + 5 :]


def center(x):
    hat = x - jnp.mean(x, axis=-1, keepdims=True)
    rstd = lax.rsqrt(jnp.mean(hat * hat, axis=-1, keepdims=True) + EPS)
    return hat * rstd, rstd


def center_backward(dhat, hat, rstd):
    first = jnp.mean(dhat, axis=-1, keepdims=True)
    second = jnp.mean(dhat * hat, axis=-1, keepdims=True)
    return rstd * (dhat - first - hat * second)


def lookup_kernel(scale, codes, table, position, gain, qk, nb, rstd_out, soft, p, pn, scores):
    i = pl.program_id(0)
    block = codes.shape[1]
    rows = pl.ds(pl.multiple_of(i * block, block), block)
    entry = lax.broadcasted_iota(jnp.int32, (table.shape[0], block), 0)
    onehot = (entry == codes[...]).astype(BF16)
    hat, rstd = center(nn(onehot.T, table[...]) + position[...].astype(F32))
    normed = (hat * gain[...].astype(F32)).astype(BF16)
    nb[rows, :] = normed
    rstd_out[...] = jnp.broadcast_to(rstd, (block, 128)).T[:1]
    scores[:, rows] = nt(qk[...], normed) * scale

    @pl.when(i == pl.num_programs(0) - 1)
    def _():
        soft[...] = softmax(scores[...])
        p[...] = soft[...].astype(BF16)
        pn[...] = nn(p[...], nb[...]).astype(BF16)


def bytes_forward(codes, table, position, gain, qk, scale):
    rows, width = position.shape
    latents, block = qk.shape[0], 512

    def whole(x):
        return pl.BlockSpec(x.shape, lambda i: (0, 0))

    shapes = [
        jax.ShapeDtypeStruct((rows, width), BF16),
        jax.ShapeDtypeStruct((1, rows), F32),
        jax.ShapeDtypeStruct((latents, rows), F32),
        jax.ShapeDtypeStruct((latents, rows), BF16),
        jax.ShapeDtypeStruct((latents, width), BF16),
    ]
    specs = [whole(x) for x in shapes]
    specs[1] = pl.BlockSpec((1, block), lambda i: (0, i))
    return pl.pallas_call(
        lambda *refs: lookup_kernel(scale, *refs),
        grid=(rows // block,),
        out_shape=shapes,
        in_specs=[
            pl.BlockSpec((1, block), lambda i: (0, i)),
            whole(table),
            pl.BlockSpec((block, width), lambda i: (i, 0)),
            pl.BlockSpec((1, width), lambda i: (0, 0)),
            whole(qk),
        ],
        out_specs=specs,
        scratch_shapes=[pltpu.VMEM((latents, rows), F32)],
        compiler_params=pltpu.CompilerParams(vmem_limit_bytes=48 * 1024 * 1024),
    )(codes[None, :], table, position, gain[None, :], qk)


def head_columns(head, width):
    each = width // HEADS
    low, high = head * each // 128 * 128, -(-(head + 1) * each // 128) * 128
    place = low + lax.broadcasted_iota(jnp.int32, (1, high - low), 1)
    return slice(low, high), jnp.logical_and(place >= head * each, place < (head + 1) * each)


def pick(mask, x):
    return jnp.where(mask, x, jnp.zeros_like(x))


def head_softmax(head, q, k):
    columns, mask = head_columns(head, q.shape[1])
    scale = (q.shape[1] // HEADS) ** (-0.5)
    return softmax(nt(pick(mask, q[:, columns]), k[:, columns]) * scale), scale


def self_forward_heads(q, k, v, total):
    total[...] = jnp.zeros_like(total)
    for head in range(HEADS):
        p = head_softmax(head, q, k)[0].astype(BF16)
        columns, mask = head_columns(head, v.shape[1])
        total[:, columns] += nn(p, pick(mask, v[:, columns]))


def self_backward_heads(q, k, v, da, dq_sum, dk_sum, dv_sum):
    for ref in (dq_sum, dk_sum, dv_sum):
        ref[...] = jnp.zeros_like(ref)
    for head in range(HEADS):
        soft, scale = head_softmax(head, q, k)
        columns, mask = head_columns(head, v.shape[1])
        da_head = pick(mask, da[:, columns])
        ds = softmax_backward(nt(da_head, v[:, columns]), soft, scale)
        dv_sum[:, columns] += nn(soft.astype(BF16).T, da_head)
        columns, mask = head_columns(head, q.shape[1])
        dq_sum[:, columns] += nn(ds, pick(mask, k[:, columns]))
        dk_sum[:, columns] += nn(ds.T, pick(mask, q[:, columns]))


class Stream:
    def __init__(self, sources, targets, sem):
        self.copies = [pltpu.make_async_copy(a, b, sem.at[i]) for i, (a, b) in enumerate(zip(sources, targets))]
        self.targets, self.arrived = targets, set()
        for copy in self.copies:
            copy.start()

    def __getitem__(self, i):
        if i not in self.arrived:
            self.copies[i].wait()
            self.arrived.add(i)
        return self.targets[i][...]


class Results:
    def __init__(self, stage, targets, sem):
        self.stage, self.targets, self.sem, self.copies, self.left = stage, targets, sem, [], set()

    def put(self, value, over=None):
        i = len(self.copies)
        buffer = self.stage[i if over is None else over]
        if over is not None:
            self.copies[over].wait()
            self.left.add(over)
        buffer[...] = value.astype(buffer.dtype)
        copy = pltpu.make_async_copy(buffer, self.targets[i], self.sem.at[i])
        copy.start()
        self.copies.append(copy)
        return buffer

    def send(self, source):
        i = len(self.copies)
        copy = pltpu.make_async_copy(source, self.targets[i], self.sem.at[i])
        copy.start()
        self.copies.append(copy)

    def finish(self):
        for i, copy in enumerate(self.copies):
            if i not in self.left:
                copy.wait()


def streamed(body, small, large, shapes, extra, unstaged):
    n_s, n_l, n_o = len(small), len(large), len(shapes)

    def kernel(*refs):
        ins, refs = refs[: n_s + n_l], refs[n_s + n_l :]
        outs, refs = refs[:n_o], refs[n_o:]
        held, refs = refs[:n_l], refs[n_l:]
        kept, refs = list(refs[: n_o - len(unstaged)]), refs[n_o - len(unstaged) :]
        stage = [None if i in unstaged else kept.pop(0) for i in range(n_o)]
        stream = Stream(ins[n_s:], held, refs[0])
        results = Results(stage, outs, refs[1])
        body(ins[:n_s], stream, results, refs[2:])
        results.finish()

    anywhere = pl.BlockSpec(memory_space=pl.ANY)
    return pl.pallas_call(
        kernel,
        out_shape=shapes,
        in_specs=[pl.BlockSpec(memory_space=pltpu.VMEM)] * n_s + [anywhere] * n_l,
        out_specs=[anywhere] * n_o,
        scratch_shapes=[pltpu.VMEM(x.shape, x.dtype) for x in large]
        + [pltpu.VMEM(x.shape, x.dtype) for i, x in enumerate(shapes) if i not in unstaged]
        + [pltpu.SemaphoreType.DMA((n_l,)), pltpu.SemaphoreType.DMA((n_o,))]
        + extra,
        compiler_params=pltpu.CompilerParams(vmem_limit_bytes=63 * 1024 * 1024),
    )(*small, *large)


def bytes_backward(at, scale, arrays):
    vd, nb, soft, q, w_key, w_query, latent = arrays[:7]
    rows, width = nb.shape
    latents, features = latent.shape
    entries, block = -(-arrays[12].shape[0] // 128) * 128, 512
    steps = rows // block

    def body(small, w, results, extra):
        ds, turned, total, table, dq, g_key, g_value, g_latent, row_sem = extra
        vd, nb = w[0], w[1]
        ds[...] = softmax_backward(nt(vd, nb), w[2], scale)
        dn = nn(ds[...], nb).astype(BF16)
        g_key[...] = nn(dn.T, w[3]).astype(BF16)
        results.send(g_key)
        dq[...] = nn(dn, w[4]).astype(BF16)
        results.send(dq)
        dnl = nt(dq[...], w[5])
        hat, rstd = center(w[6].astype(F32))
        g = w[10].astype(F32)
        g_latent[...] = (w[7] + center_backward(dnl * g, hat, rstd)).astype(BF16)
        results.send(g_latent)
        g_value[...] = nn(w[8].T, w[9]).astype(BF16)
        results.send(g_value)
        first = jnp.sum(dnl * hat, axis=0, keepdims=True)
        own = lax.broadcasted_iota(jnp.int32, (8, features), 0) == 0
        turned[...] = jnp.zeros_like(turned)
        turned[:, :8] = jnp.where(own, first, w[11]).T.astype(BF16)
        results.send(turned)
        emb, sums = w[12], w[13]
        total[...] = jnp.zeros_like(total)
        total[: emb.shape[0]] = emb
        total[at + 1 : at + 2] = sums[1:2]
        total[at + 2 : at + 3] = sums[0:1]
        qk, g = w[15], w[18].astype(F32)
        inverse = 1.0 / g
        w[14], w[16], w[17]
        p_ref, scale_ref, codes_ref, nb_ref = w.targets[14], w.targets[16], w.targets[17], w.targets[1]
        target = results.targets[6]

        def out_copy(i):
            here = pl.ds(pl.multiple_of(i * block, block), block)
            return pltpu.make_async_copy(nb_ref.at[here], target.at[here], row_sem.at[i])

        def step(i, carry):
            here = pl.ds(pl.multiple_of(i * block, block), block)
            rstd = jnp.broadcast_to(scale_ref[:, here], (128, block)).T[:, :1]
            normed = nb_ref[here, :]
            dnb = nn(p_ref[:, here].T, vd) + nn(ds[:, here].T, qk)
            hat = normed.astype(F32) * inverse
            dx = center_backward(dnb * g, hat, rstd).astype(BF16)
            nb_ref[here, :] = dx
            out_copy(i).start()
            entry = lax.broadcasted_iota(jnp.int32, (entries, block), 0)
            onehot = (entry == codes_ref[:, here]).astype(BF16)
            total[...] += nn(onehot, dx)
            total[at : at + 1] += jnp.sum(dnb * hat, axis=0, keepdims=True)
            return carry

        lax.fori_loop(0, steps, step, 0)
        table[...] = total[...].T.astype(BF16)
        results.send(table)

        def wait(i, carry):
            out_copy(i).wait()
            return carry

        lax.fori_loop(0, steps, wait, 0)

    qk_width = q.shape[1]

    def low(*shape):
        return jax.ShapeDtypeStruct(shape, BF16)

    shapes = [
        low(width, qk_width), low(latents, qk_width), low(latents, features), low(width, features),
        low(features, 128), low(width, entries), low(rows, width),
    ]
    vmem = pltpu.VMEM
    extra = [vmem((latents, rows), BF16), vmem((features, 128), BF16), vmem((entries, width), F32)]
    extra += [vmem((width, entries), BF16), vmem((latents, qk_width), BF16), vmem((width, qk_width), BF16)]
    extra += [vmem((width, features), BF16), vmem((latents, features), BF16), pltpu.SemaphoreType.DMA((steps,))]
    return streamed(body, [], arrays, shapes, extra, set(range(len(shapes))))


def middle_pass(latent, pn, gains, byte_gains, weights, scale):
    rows, width = latent.shape
    emb, queries, cot = weights[14:]
    entries, depth = emb.shape
    block = 256
    qk = weights[4].shape[1]

    def body(small, w, results, extra):
        latent_ref, pn_ref, g1, g2, g3, g4, gain_q, gain_f = small
        total, dq_sum, dk_sum, sums, u1, u2, q, k, v, k_d, v_d, kq, vo, vo_mid, g_pd, g_dn, g_emb, g_byte = extra
        put = results.put

        def norm(x, gain):
            hat, rstd = center(x)
            return put(hat * gain[...].astype(F32)), rstd

        a_e = put(nn(pn_ref[...], w[0]))
        x = latent_ref[...].astype(F32) + nn(a_e[...], w[1])
        n1, r1 = norm(x, g1)
        u1[...] = nn(n1[...], w[2])
        h1 = put(gelu_forward(u1[...]))
        x = x + nn(h1[...], w[3])
        n2, r2 = norm(x, g2)
        q[...] = nn(n2[...], w[4]).astype(BF16)
        k[...] = nn(n2[...], w[5]).astype(BF16)
        v[...] = nn(n2[...], w[6]).astype(BF16)
        self_forward_heads(q, k, v, total)
        a_s = put(total[...])
        x = x + nn(a_s[...], w[7])
        n3, r3 = norm(x, g3)
        u2[...] = nn(n3[...], w[8])
        h2 = put(gelu_forward(u2[...]))
        x = x + nn(h2[...], w[9])
        n4, r4 = norm(x, g4)
        k_d[...] = nn(n4[...], w[10]).astype(BF16)
        v_d[...] = nn(n4[...], w[11]).astype(BF16)

        w_query, w_out = w[12], w[13]
        kq[...] = nt(k_d[...], w_query).astype(BF16)
        out = nn(v_d[...], w_out)
        vo[...] = out.astype(BF16)
        vo_mid[...] = (out - jnp.mean(out, axis=0, keepdims=True)).astype(BF16)
        for ref in (g_pd, g_dn, g_emb, g_byte):
            ref[...] = jnp.zeros_like(ref)
        w[14], w[15], w[16]
        emb_ref, query_ref, cot_ref = w.targets[14:]

        def decode(i, carry):
            at = pl.ds(pl.multiple_of(i * block, block), block)
            x = query_ref[at, :].astype(F32)
            hat_q, rstd_q = center(x)
            gq, gf = gain_q[...].astype(F32), gain_f[...].astype(F32)
            nq = (hat_q * gq).astype(BF16)
            soft = softmax(nt(nq, kq[...]) * scale)
            p = soft.astype(BF16)
            hat_f, rstd_f = center(x + nn(p, vo[...]))
            nf = (hat_f * gf).astype(BF16)
            cot_part = cot_ref[:, at]
            dnf = nn(cot_part.T, emb_ref[...])
            g_emb[...] += nn(cot_part, nf)
            cot_ref[:, at] = nt(emb_ref[...], nf).astype(BF16)
            g_byte[0:1] += jnp.sum(dnf * hat_f, axis=0, keepdims=True)
            ddec = center_backward(dnf * gf, hat_f, rstd_f)
            ddec16 = ddec.astype(BF16)
            g_pd[...] += nn(p.T, ddec16)
            ds = softmax_backward(nt(ddec16, vo_mid[...]), soft, scale)
            g_dn[...] += nn(ds.T, nq)
            dnq = nn(ds, kq[...])
            g_byte[1:2] += jnp.sum(dnq * hat_q, axis=0, keepdims=True)
            query_ref[at, :] = (ddec + center_backward(dnq * gq, hat_q, rstd_q)).astype(BF16)
            return carry

        lax.fori_loop(0, queries.shape[0] // block, decode, 0)
        results.send(query_ref)
        half = queries.shape[0] // 2
        mine = lax.axis_index("blk")
        for part in (mine, 1 - mine):
            results.send(cot_ref.at[:, pl.ds(pl.multiple_of(part * half, half), half)])
        results.send(g_emb)
        results.send(g_byte)
        pd, dn = g_pd[...].astype(BF16), g_dn[...].astype(BF16)
        dk_d = nn(dn, w.targets[12][...]).astype(BF16)
        dv_d = nt(pd, w.targets[13][...]).astype(BF16)
        put(dk_d)
        put(dv_d)
        put(nn(dn.T, k_d[...]))
        put(nn(v_d[...].T, pd))

        sums[...] = jnp.zeros_like(sums)

        def back(dy, normed, rstd, gain, row):
            g = gain[...].astype(F32)
            hat = normed[...].astype(F32) * (1.0 / g)
            sums[row : row + 1] = jnp.sum(dy * hat, axis=0, keepdims=True)
            return center_backward(dy * g, hat, rstd)

        dlat = back(nt(dk_d, w[10]) + nt(dv_d, w[11]), n4, r4, g4, 4)
        dlat16 = put(dlat, 0)
        du2 = put(gelu_backward(nt(dlat16[...], w[9]), u2[...]), 2)
        das = dlat + back(nt(du2[...], w[8]), n3, r3, g3, 3)
        das16 = put(das, 4)
        da = nt(das16[...], w[7]).astype(BF16)
        self_backward_heads(q, k, v, da, dq_sum, dk_sum, total)
        dq, dk, dv = put(dq_sum[...]), put(dk_sum[...]), put(total[...], 6)
        dn2 = nt(dq[...], w[4]) + nt(dk[...], w[5]) + nt(dv[...], w[6])
        denc = das + back(dn2, n2, r2, g2, 2)
        denc16 = put(denc, 7)
        du1 = put(gelu_backward(nt(denc16[...], w[3]), u1[...]), 5)
        daft = denc + back(nt(du1[...], w[2]), n1, r1, g1, 1)
        daft16 = put(daft, 3)
        u1[...] = daft
        results.send(u1)
        dae = put(nt(daft16[...], w[1]), 1)
        put(nt(dae[...], w[0]))
        results.send(sums)

    wide = (rows, width)

    def low(*shape):
        return jax.ShapeDtypeStruct(shape, BF16)

    def full(*shape):
        return jax.ShapeDtypeStruct(shape, F32)

    shapes = [low(*wide)] * 8
    shapes += [low(*queries.shape)] + [low(entries, queries.shape[0] // 2)] * 2
    shapes += [full(entries, depth), full(8, depth)]
    shapes += [low(rows, qk), low(rows, depth), low(depth, qk), low(depth, depth)]
    shapes += [low(*wide)] * 3 + [low(rows, qk)] * 2 + [low(*wide)] * 4
    shapes += [full(*wide), low(*wide), low(rows, depth), full(8, width)]
    unstaged = {8, 9, 10, 11, 12, 17, 18, 19, 22, 23, 24, 25, 26, 27, 29}
    vmem = pltpu.VMEM
    extra = [vmem(wide, F32), vmem((rows, qk), F32), vmem((rows, qk), F32), vmem((8, width), F32)]
    extra += [vmem(wide, F32)] * 2 + [vmem((rows, qk), BF16)] * 2 + [vmem(wide, BF16)]
    extra += [vmem((rows, qk), BF16)] + [vmem((rows, depth), BF16)] * 4 + [vmem((rows, depth), F32)] * 2
    extra += [vmem((entries, depth), F32), vmem((8, depth), F32)]
    small = [latent, pn] + [g[None, :] for g in gains + byte_gains]
    return streamed(body, small, weights, shapes, extra, unstaged)


def local(
    byte_ids, span_start, span_len, embedding, position, mask_vector, gain_bytes, key_enc,
    value_enc, latent_init, gain_latent, query_enc, out_enc, gain_enc_mlp, up_enc, down_enc,
    gain_self, query_self, key_self, value_self, out_self, gain_self_mlp, up_self, down_self,
    gain_dec_kv, key_dec, value_dec, dec_query, gain_dec_q, query_dec, out_dec, gain_final,
    logit_cot,
):
    me = lax.axis_index("blk")
    half = byte_ids.shape[1]
    total = position.shape[0]
    vocab = embedding.shape[0]
    reducer = Reducer()
    k = reducer.k
    order_yx = [0, "y", 1] + list(range(2, k))
    order_xy = [0, 1, "y"] + list(range(2, k))

    def swap(x):
        return lax.ppermute(x, "blk", [(0, 1), (1, 0)])

    def own_item(first, second, after=()):
        mine = jnp.where(me == 0, first, second)
        send = jnp.where(me == 0, second, first)
        if after:
            (send,) = tie([send], after)
        got = swap(send)
        low_half = jnp.where(me == 0, mine, got)
        high_half = jnp.where(me == 0, got, mine)
        return jnp.concatenate([low_half, high_half], axis=-1)

    ids = own_item(byte_ids[0], byte_ids[1])
    cot_rows = logit_cot.transpose(2, 0, 1)
    cot = own_item(cot_rows[:, 0], cot_rows[:, 1], [ids])
    entries = -(-(vocab + 4) // 16) * 16
    cot = jnp.pad(cot, ((0, entries - vocab), (0, 0)))
    emb_rows = jnp.pad(embedding, ((0, entries - vocab), (0, 0)))
    starts = lax.dynamic_index_in_dim(span_start, me, 0, keepdims=False)
    lengths = lax.dynamic_index_in_dim(span_len, me, 0, keepdims=False)

    places = lax.iota(jnp.int32, total)
    inside = (places[None, :] >= starts[:, None]) & (places[None, :] < (starts + lengths)[:, None])
    codes = jnp.where(jnp.any(inside, axis=0), vocab, ids)
    padded = -(-(vocab + 4) // 128) * 128
    table = jnp.concatenate(
        [embedding, mask_vector[None, :], jnp.zeros((padded - vocab - 1, embedding.shape[1]), BF16)], axis=0
    )

    latent32 = latent_init.astype(F32)
    nl = norm_forward(latent32, gain_latent)[0]
    q_e = nn(nl, query_enc).astype(BF16)
    scale_e = q_e.shape[1] ** (-0.5)
    qk_e = nt(q_e, key_enc).astype(BF16)
    nb, rstd_b, soft_e, p_e, pn_e = bytes_forward(codes, table, position, gain_bytes, qk_e, scale_e)

    gains = (gain_enc_mlp, gain_self, gain_self_mlp, gain_dec_kv)
    (
        a_e, n1, h1, n2, a_s, n3, h2, n4,
        g_dec_query, logits_own, logits_other, g_emb_out, gain_sums, dk_d, dv_d, g_query_dec, g_out_dec,
        dlat16, du2, das16, dq_s, dk_s, dv_s, denc16, du1, daft16, dafter, dae16, vd_e, wide,
    ) = middle_pass(
        latent_init, pn_e, gains, (gain_dec_q, gain_final),
        [
            value_enc, out_enc, up_enc, down_enc, query_self, key_self, value_self, out_self, up_self,
            down_self, key_dec, value_dec, query_dec, out_dec, emb_rows, dec_query, cot,
        ],
        query_dec.shape[1] ** (-0.5),
    )
    logits_own, logits_got = logits_own[:vocab], swap(logits_other)[:vocab]
    side = lax.broadcasted_iota(jnp.int32, (1, 2, 1), 1)
    logits_out = jnp.where(side == me, logits_own[:, None, :], logits_got[:, None, :]).transpose(1, 2, 0)

    g_key_enc, dq_e, g_latent, g_value_enc, vectors, g_table, dbytes = bytes_backward(
        vocab + 1, scale_e,
        [
            vd_e, nb, soft_e, q_e, key_enc, query_enc, latent_init, dafter, pn_e, dae16, gain_latent[None, :], wide,
            g_emb_out, gain_sums, p_e, qk_e, rstd_b, codes[None, :], gain_bytes[None, :],
        ],
    )

    def low(g):
        return g.astype(BF16)

    if reducer.n_items == 16:
        first_side = [(n1, [du1]), (a_e, [daft16]), (n3, [du2]), (n2, [dv_s, dk_s])]
        second_side = [
            (h1, [denc16]), (h2, [dlat16]), (a_s, [das16]), (n4, [dv_d, dk_d]), (n2, [dq_s]), (nl, [dq_e]),
        ]
        others = [
            (low(g_dec_query), "xy"), (low(dbytes), "yx"), (low(g_value_enc), "xy"), (low(g_out_dec), "yx"),
            (low(g_table), "yx"), (low(g_key_enc), "xy"), (low(g_query_dec), "yx"), (low(g_latent), "xy"),
            (low(vectors), "yx"),
        ]
        (
            r_up_enc, r_out_enc, r_up_self, r_value_self, r_key_self,
            r_down_enc, r_down_self, r_out_self, r_value_dec, r_key_dec, r_query_self, r_query_enc,
        ), (
            r_dec_query, r_position, r_value_enc, r_out_dec, r_emb, r_key_enc, r_query_dec, r_latent, r_vectors,
        ) = reduce_all((first_side, second_side), others)
    else:
        r_dec_query, r_out_dec, r_value_dec = reducer.reduce([g_dec_query, g_out_dec, tn(n4, dv_d)], order_yx)
        r_down_self, r_up_self, r_out_self = reducer.reduce(
            [tn(h2, dlat16), tn(n3, du2), tn(a_s, das16)], order_xy
        )
        r_value_self, r_down_enc = reducer.reduce([tn(n2, dv_s), tn(h1, denc16)], order_yx)
        r_up_enc, r_out_enc = reducer.reduce([tn(n1, du1), tn(a_e, daft16)], order_xy)
        r_query_dec, r_key_dec, r_query_self, r_key_self = reducer.reduce(
            [g_query_dec, tn(n4, dk_d), tn(n2, dq_s), tn(n2, dk_s)], order_xy
        )
        r_value_enc, r_latent = reducer.reduce([g_value_enc, g_latent], order_xy)
        (r_position,) = reducer.reduce([dbytes], order_yx)
        r_key_enc, r_query_enc = reducer.reduce([g_key_enc, tn(nl, dq_e)], order_yx)
        (r_emb,) = reducer.reduce([g_table], order_yx)
        (r_vectors,) = reducer.reduce([vectors], order_xy)

    plain = [
        r_position, r_key_enc, r_value_enc, r_latent, r_query_enc, r_out_enc, r_up_enc, r_down_enc,
        r_query_self, r_key_self, r_value_self, r_out_self, r_up_self, r_down_self, r_key_dec, r_value_dec,
        r_dec_query, r_query_dec, r_out_dec,
    ]
    plain, r_embedding, (r_mask, r_gain_bytes, r_gain_dec_q, r_gain_final), gains = finish(plain, r_emb, r_vectors, vocab, 1 + len(gains))
    (
        r_position, r_key_enc, r_value_enc, r_latent, r_query_enc, r_out_enc, r_up_enc, r_down_enc,
        r_query_self, r_key_self, r_value_self, r_out_self, r_up_self, r_down_self, r_key_dec, r_value_dec,
        r_dec_query, r_query_dec, r_out_dec,
    ) = plain
    (
        r_gain_latent, r_gain_enc_mlp, r_gain_self, r_gain_self_mlp, r_gain_dec_kv,
    ) = gains
    return (
        logits_out, r_embedding.T, r_position, r_mask, r_gain_bytes, r_key_enc, r_value_enc,
        r_latent, r_gain_latent, r_query_enc, r_out_enc, r_gain_enc_mlp, r_up_enc, r_down_enc, r_gain_self,
        r_query_self, r_key_self, r_value_self, r_out_self, r_gain_self_mlp, r_up_self, r_down_self,
        r_gain_dec_kv, r_key_dec, r_value_dec, r_dec_query, r_gain_dec_q, r_query_dec, r_out_dec, r_gain_final,
    )


def solution(mesh):
    split = P("items", "blk")
    rows = P(("items", "blk"))
    outs = [P("items", "blk", None), P(None, ("items", "blk"))] + [rows] * 28
    return jax.shard_map(
        local,
        mesh=mesh,
        in_specs=(split, P("items", None), P("items", None)) + (P(),) * 29 + (P("items", "blk", None),),
        out_specs=tuple(outs),
        check_vma=False,
    )
```
